32 devices in a mesh: dp: 16 (over z, y, x), mp: 2 (over core).
Axes of the slice: x: 2, y: 2, z: 4, core: 2. Of those that a mesh axis runs over, the one named last changes fastest.
Arguments:
- latents: bfloat16 [8192, 1024], P(('dp', 'mp')), may hold values from -6 to 6
- inputs: bfloat16 [32768, 1024], P(('dp', 'mp')), may hold values from -6 to 6
- valid_counts: int32 [32], P('dp'), may hold values from 1 to 1024, as said below
- cotangent: bfloat16 [8192, 1024], P(('dp', 'mp')), may hold values from -6 to 6
- gain_latent: float32 [1024], replicated, may hold values from 0.1 to 1.9
- shift_latent: float32 [1024], replicated, may hold values from -1.75 to 1.75
- gain_input: float32 [1024], replicated, may hold values from 0.1 to 1.9
- shift_input: float32 [1024], replicated, may hold values from -1.75 to 1.75
- cross_query: bfloat16 [1024, 1024], P(None, 'mp'), may hold values from -0.1875 to 0.1875
- cross_key: bfloat16 [1024, 1024], P(None, 'mp'), may hold values from -0.1875 to 0.1875
- cross_value: bfloat16 [1024, 1024], P(None, 'mp'), may hold values from -0.1875 to 0.1875
- cross_out: bfloat16 [1024, 1024], P('mp'), may hold values from -3 to 3
- gain_self: float32 [1024], replicated, may hold values from 0.1 to 1.9
- shift_self: float32 [1024], replicated, may hold values from -1.75 to 1.75
- self_query: bfloat16 [1024, 1024], P(None, 'mp'), may hold values from -0.1875 to 0.1875
- self_key: bfloat16 [1024, 1024], P(None, 'mp'), may hold values from -0.1875 to 0.1875
- self_value: bfloat16 [1024, 1024], P(None, 'mp'), may hold values from -0.1875 to 0.1875
- self_out: bfloat16 [1024, 1024], P('mp'), may hold values from -3 to 3
- gain_mlp: float32 [1024], replicated, may hold values from 0.1 to 1.9
- shift_mlp: float32 [1024], replicated, may hold values from -1.75 to 1.75
- mlp_in: bfloat16 [1024, 4096], P(None, 'mp'), may hold values from -0.1875 to 0.1875
- mlp_in_bias: float32 [4096], P('mp'), may hold values from -1.75 to 1.75
- mlp_out: bfloat16 [4096, 1024], P('mp'), may hold values from -0.09375 to 0.09375
- mlp_out_bias: float32 [1024], replicated, may hold values from -1.75 to 1.75
Outputs:
- result_latents: bfloat16 [8192, 1024], P(('dp', 'mp'))
- grad_latents: float32 [8192, 1024], P(('dp', 'mp'))
- grad_inputs: float32 [32768, 1024], P(('dp', 'mp'))
- grad_gain_latent: float32 [1024], replicated
- grad_shift_latent: float32 [1024], replicated
- grad_gain_input: float32 [1024], replicated
- grad_shift_input: float32 [1024], replicated
- grad_cross_query: float32 [1024, 1024], P(None, 'mp')
- grad_cross_key: float32 [1024, 1024], P(None, 'mp')
- grad_cross_value: float32 [1024, 1024], P(None, 'mp')
- grad_cross_out: float32 [1024, 1024], P('mp')
- grad_gain_self: float32 [1024], replicated
- grad_shift_self: float32 [1024], replicated
- grad_self_query: float32 [1024, 1024], P(None, 'mp')
- grad_self_key: float32 [1024, 1024], P(None, 'mp')
- grad_self_value: float32 [1024, 1024], P(None, 'mp')
- grad_self_out: float32 [1024, 1024], P('mp')
- grad_gain_mlp: float32 [1024], replicated
- grad_shift_mlp: float32 [1024], replicated
- grad_mlp_in: float32 [1024, 4096], P(None, 'mp')
- grad_mlp_in_bias: float32 [4096], P('mp')
- grad_mlp_out: float32 [4096, 1024], P('mp')
- grad_mlp_out_bias: float32 [1024], replicated
The draws below stay inside these ranges and needn't reach their ends.
Inputs may be any that keep to these rules, and one draw needn't show every extreme that they name: `valid_counts`: valid inputs of each group are its first ones; each aligned block of 2 groups holds one group with all 1024 inputs valid, and some groups hold only a few.
All inputs are finite; a program needn't handle non-finite values.
Results may differ from the reference program's by a relative error of at most 0.04.
Values may be sent and summed in bfloat16 or wider, within the bound.
A program may use at most 256 MiB of HBM per device.

```python
import jax
import jax.numpy as jnp
from jax import lax

D = 1024
HEADS = 32
HD = 32
FF = 4096
GS = 256
IN = 1024
GROUPS_DEV = 2
GROUPS = 32
ROWS = 8192
INPUTS = 32768


def draw_valid_counts(key, part):
    key = jax.random.fold_in(key, 7)
    key_sparse, key_broad, key_flag, key_full = jax.random.split(key, 4)
    sparse_counts = jax.random.randint(key_sparse, (GROUPS,), 1, IN // 16 + 2)
    broad_counts = jax.random.randint(key_broad, (GROUPS,), 1, IN + 1)
    sparse_flag = jax.random.randint(key_flag, (GROUPS,), 0, 3)
    counts = jnp.where(sparse_flag == 0, sparse_counts, broad_counts)
    chosen_slot = jax.random.randint(key_full, (GROUPS // GROUPS_DEV, 1), 0, GROUPS_DEV)
    slot_index = jnp.arange(GROUPS_DEV, dtype=jnp.int32)[None, :]
    full_group = (slot_index == chosen_slot).reshape(GROUPS)
    return jnp.where(full_group, IN, counts).astype(jnp.int32)


def block_levels(stream_key, shape, cuts, low, largest):
    def one(position, shards_of):
        draws = jax.random.uniform(jax.random.fold_in(jax.random.fold_in(stream_key, 6), position), (shards_of,), jnp.float32, low / len(cuts), largest / len(cuts))
        return jnp.repeat(jnp.exp(draws), shape[position] // shards_of).reshape((-1,) + (1,) * (len(shape) - position - 1))

    gain = one(*cuts[0])
    for cut in cuts[1:]:
        gain = gain * one(*cut)
    return gain


def bell_draw(rng, extent, deviation, limit, cuts=(), held_as=jnp.bfloat16):
    gain = block_levels(rng, extent, cuts, -0.22, 0.18) if cuts else 1.0
    entries = jax.random.normal(rng, extent, jnp.float32) * deviation * gain
    return jnp.minimum(jnp.maximum(entries, -limit), limit).astype(held_as)


def setup_inputs(seed: int = 0) -> dict:
    streams_of = jax.random.split(jax.random.key(seed), 25)
    latents = bell_draw(streams_of[0], (ROWS, D), 1.0, 6.0, ((0, 32),))
    inputs = bell_draw(streams_of[1], (INPUTS, D), 1.0, 6.0, ((0, 32),))
    valid_counts = draw_valid_counts(jax.random.fold_in(streams_of[24], 71), 0)
    cotangent = bell_draw(streams_of[3], (ROWS, D), 1.0, 6.0, ((0, 32),))
    gain_latent = jnp.clip(1.0 + 0.18 * jax.random.normal(streams_of[4], (D,), jnp.float32), 0.1, 1.9)
    shift_latent = bell_draw(streams_of[5], (D,), 0.3, 1.75, (), jnp.float32)
    gain_input = jnp.clip(1.0 + 0.18 * jax.random.normal(streams_of[6], (D,), jnp.float32), 0.1, 1.9)
    shift_input = bell_draw(streams_of[7], (D,), 0.3, 1.75, (), jnp.float32)
    cross_query = bell_draw(streams_of[8], (D, HEADS * HD), D ** -0.5, 0.1875, ((1, 2),))
    cross_key = bell_draw(streams_of[9], (D, HEADS * HD), D ** -0.5, 0.1875, ((1, 2),))
    cross_value = bell_draw(streams_of[10], (D, HEADS * HD), D ** -0.5, 0.1875, ((1, 2),))
    cross_out = bell_draw(streams_of[11], (HEADS * HD, D), (D // GS) ** -0.5, 3.0, ((0, 2),))
    gain_self = jnp.clip(1.0 + 0.18 * jax.random.normal(streams_of[12], (D,), jnp.float32), 0.1, 1.9)
    shift_self = bell_draw(streams_of[13], (D,), 0.3, 1.75, (), jnp.float32)
    self_query = bell_draw(streams_of[14], (D, HEADS * HD), D ** -0.5, 0.1875, ((1, 2),))
    self_key = bell_draw(streams_of[15], (D, HEADS * HD), D ** -0.5, 0.1875, ((1, 2),))
    self_value = bell_draw(streams_of[16], (D, HEADS * HD), D ** -0.5, 0.1875, ((1, 2),))
    self_out = bell_draw(streams_of[17], (HEADS * HD, D), (D // GS) ** -0.5, 3.0, ((0, 2),))
    gain_mlp = jnp.clip(1.0 + 0.18 * jax.random.normal(streams_of[18], (D,), jnp.float32), 0.1, 1.9)
    shift_mlp = bell_draw(streams_of[19], (D,), 0.3, 1.75, (), jnp.float32)
    mlp_in = bell_draw(streams_of[20], (D, FF), D ** -0.5, 0.1875, ((1, 2),))
    mlp_in_bias = bell_draw(streams_of[21], (FF,), 0.3, 1.75, ((0, 2),), jnp.float32)
    mlp_out = bell_draw(streams_of[22], (FF, D), FF ** -0.5, 0.09375, ((0, 2),))
    mlp_out_bias = bell_draw(streams_of[23], (D,), 0.3, 1.75, (), jnp.float32)
    return {"latents": latents, "inputs": inputs, "valid_counts": valid_counts, "cotangent": cotangent, "gain_latent": gain_latent, "shift_latent": shift_latent, "gain_input": gain_input, "shift_input": shift_input, "cross_query": cross_query, "cross_key": cross_key, "cross_value": cross_value, "cross_out": cross_out, "gain_self": gain_self, "shift_self": shift_self, "self_query": self_query, "self_key": self_key, "self_value": self_value, "self_out": self_out, "gain_mlp": gain_mlp, "shift_mlp": shift_mlp, "mlp_in": mlp_in, "mlp_in_bias": mlp_in_bias, "mlp_out": mlp_out, "mlp_out_bias": mlp_out_bias}


@jax.custom_vjp
def low(v):
    return lax.optimization_barrier(v.astype(jnp.bfloat16)).astype(jnp.float32)

@jax.custom_vjp
def low_back(v):
    return v

def low_keep(v):
    return (low(v), None)

def low_pass(kept, grad):
    return (grad,)

def back_keep(v):
    return (v, None)

def back_low(kept, grad):
    return (low(grad),)
low.defvjp(low_keep, low_pass)
low_back.defvjp(back_keep, back_low)
epsilon = 1e-05
negative = -1e+30
highest = lax.Precision.HIGHEST

def matmul(left, right):
    return jnp.dot(left, right, precision=highest, preferred_element_type=jnp.float32)

def layer_norm(stream, norm_gain, norm_shift):
    row_mean = lax.optimization_barrier(jnp.mean(stream, axis=-1, keepdims=True))
    centered = stream - row_mean
    row_var = lax.optimization_barrier(jnp.mean(centered * centered, axis=-1, keepdims=True))
    return centered * lax.rsqrt(row_var + epsilon) * norm_gain + norm_shift

def attend(queries, key_rows, value_rows, valid_mask):
    raw = jnp.einsum('gshe,gkhe->ghsk', queries, key_rows, precision=highest, preferred_element_type=jnp.float32)
    scores = low_back(raw) * HD ** (-0.5)
    scores = jnp.where(valid_mask[:, None, None, :], scores, negative)
    attn_prob = jax.nn.softmax(scores, axis=-1)
    mixed = jnp.einsum('ghsk,gkhe->gshe', low(attn_prob), value_rows, precision=highest, preferred_element_type=jnp.float32)
    return low(low_back(mixed))

def block_forward(params, latent_rows, input_rows, valid_mask):
    gain_latent, shift_latent, gain_input, shift_input, cross_query, cross_key, cross_value, cross_out, gain_self, shift_self, self_query, self_key, self_value, self_out, gain_mlp, shift_mlp, mlp_in, mlp_in_bias, mlp_out, mlp_out_bias = params
    group_count = valid_mask.shape[0]
    latent_normed = low(layer_norm(latent_rows, gain_latent, shift_latent))
    input_normed = low(layer_norm(input_rows, gain_input, shift_input))
    queries = low(low_back(matmul(latent_normed, cross_query))).reshape(group_count, GS, HEADS, HD)
    key_rows = low(low_back(matmul(input_normed, cross_key))).reshape(group_count, IN, HEADS, HD)
    value_rows = low(low_back(matmul(input_normed, cross_value))).reshape(group_count, IN, HEADS, HD)
    mixed = attend(queries, key_rows, value_rows, valid_mask).reshape(group_count * GS, HEADS * HD)
    stream = latent_rows + low_back(matmul(mixed, cross_out))
    self_normed = low(layer_norm(stream, gain_self, shift_self))
    queries = low(low_back(matmul(self_normed, self_query))).reshape(group_count, GS, HEADS, HD)
    key_rows = low(low_back(matmul(self_normed, self_key))).reshape(group_count, GS, HEADS, HD)
    value_rows = low(low_back(matmul(self_normed, self_value))).reshape(group_count, GS, HEADS, HD)
    all_valid = jnp.ones((group_count, GS), dtype=jnp.bool_)
    mixed = attend(queries, key_rows, value_rows, all_valid).reshape(group_count * GS, HEADS * HD)
    stream = stream + low_back(matmul(mixed, self_out))
    mlp_normed = low(layer_norm(stream, gain_mlp, shift_mlp))
    hidden = low_back(matmul(mlp_normed, mlp_in) + mlp_in_bias)
    activation = low(jax.nn.gelu(hidden, approximate=False))
    return stream + low_back(matmul(activation, mlp_out) + mlp_out_bias)

def reference(latents, inputs, valid_counts, cotangent, gain_latent, shift_latent, gain_input, shift_input, cross_query, cross_key, cross_value, cross_out, gain_self, shift_self, self_query, self_key, self_value, self_out, gain_mlp, shift_mlp, mlp_in, mlp_in_bias, mlp_out, mlp_out_bias):
    params = tuple((weight.astype(jnp.float32) for weight in (gain_latent, shift_latent, gain_input, shift_input, cross_query, cross_key, cross_value, cross_out, gain_self, shift_self, self_query, self_key, self_value, self_out, gain_mlp, shift_mlp, mlp_in, mlp_in_bias, mlp_out, mlp_out_bias)))
    group_block = 4
    block_count = GROUPS // group_block
    latent_blocks = latents.reshape(block_count, group_block * GS, D)
    input_blocks = inputs.reshape(block_count, group_block * IN, D)
    cotangent_blocks = cotangent.reshape(block_count, group_block * GS, D)
    count_blocks = valid_counts.reshape(block_count, group_block)

    def one_block(summed, pieces):
        latent_piece, input_piece, cotangent_piece, count_piece = pieces
        valid_mask = jnp.arange(IN, dtype=jnp.int32)[None, :] < count_piece[:, None]

        def forward(weights, latent_rows, input_rows):
            return block_forward(weights, latent_rows, input_rows, valid_mask)
        result, pullback = jax.vjp(forward, params, latent_piece.astype(jnp.float32), input_piece.astype(jnp.float32))
        grad_params, grad_latent, grad_input = pullback(cotangent_piece.astype(jnp.float32))
        summed = jax.tree.map(lambda before, addend: before + addend, summed, grad_params)
        return (summed, (result.astype(jnp.bfloat16), grad_latent, grad_input))
    initial = jax.tree.map(jnp.zeros_like, params)
    totals, outputs = lax.scan(one_block, initial, (latent_blocks, input_blocks, cotangent_blocks, count_blocks))
    result_blocks, grad_latent_blocks, grad_input_blocks = outputs
    return (result_blocks.reshape(ROWS, D), grad_latent_blocks.reshape(ROWS, D), grad_input_blocks.reshape(INPUTS, D), totals[0], totals[1], totals[2], totals[3], totals[4], totals[5], totals[6], totals[7], totals[8], totals[9], totals[10], totals[11], totals[12], totals[13], totals[14], totals[15], totals[16], totals[17], totals[18], totals[19])
```

```python
import functools
from functools import partial

import jax
import jax.numpy as jnp
from jax import lax
from jax.experimental import pallas as pl
from jax.experimental.pallas import tpu as pltpu
from jax.sharding import PartitionSpec as P

HD = 32
GS = 256
IN = 1024


MESH = pl.DeviceIdType.MESH
NS = 16
AHEAD = 2
ORDER = (("a", -2), ("b", 0), ("f", 2), ("j", 4), ("d", 1), ("h", 3), ("c", 0), ("g", 2), ("e", 1), ("i", 3), ("k", 6))
CH = 256
HALF = CH // 2
PIECE = HALF // 4
SUB = PIECE // 2
SMALL = 16


def reduce_kernel(pairs, g_ref, small_ref, out_ref, small_out, own, xr, ur, dr, fb, yr, sacc, sbuf, send, recv, loc, ssend, srecv):
    dp = lax.axis_index("dp")
    core = lax.axis_index("mp")
    z = dp // 4
    px = lax.rem(dp, 2)
    py = lax.rem(dp // 2, 2)
    x_dev = (dp + 1 - 2 * px, core)
    y_dev = (dp + 2 - 4 * py, core)
    c_dev = (dp, 1 - core)
    up_dev = (dp + 4, core)
    down_dev = (dp - 4, core)
    z1_dev = (dp + 4 - 8 * lax.rem(z, 2), core)
    z2_dev = (dp + 8 - 16 * (z // 2), core)
    has_up = z < 3
    has_down = z > 0

    barrier = pltpu.get_barrier_semaphore()
    for dev in (x_dev, y_dev, c_dev, z2_dev):
        pl.semaphore_signal(barrier, inc=1, device_id=dev, device_id_type=MESH)

    @pl.when(has_up)
    def _():
        pl.semaphore_signal(barrier, inc=1, device_id=up_dev, device_id_type=MESH)

    @pl.when(has_down)
    def _():
        pl.semaphore_signal(barrier, inc=1, device_id=down_dev, device_id_type=MESH)

    pl.semaphore_wait(barrier, 4 + has_up.astype(jnp.int32) + has_down.astype(jnp.int32))

    def remote(src, dst, kind, p, s, dev):
        slot = lax.rem(p, NS)
        return pltpu.make_async_remote_copy(
            src_ref=src, dst_ref=dst, send_sem=send.at[kind, s, slot], recv_sem=recv.at[kind, s, slot],
            device_id=dev, device_id_type=MESH)

    a_pos = (px, py)
    b_pos = (py, px)
    a_dev = (x_dev, y_dev)
    b_dev = (y_dev, x_dev)

    def base(p, s):
        return (2 * p + s) * CH

    def first(p, s):
        c = 2 * p + s
        return remote(g_ref.at[pl.ds(base(p, s) + (1 - a_pos[s]) * HALF, HALF)], xr.at[c], 0, p, s, a_dev[s])

    def mine(p, s):
        c = 2 * p + s
        return pltpu.make_async_copy(g_ref.at[pl.ds(base(p, s) + a_pos[s] * HALF, HALF)], own.at[c], loc.at[0, s, lax.rem(p, NS)])

    def up(p, s, lo):
        c = 2 * p + s
        src = xr if lo == 1 else ur
        return remote(src.at[c, pl.ds(lo * PIECE, (4 - lo) * PIECE)], ur.at[c, pl.ds(lo * PIECE, (4 - lo) * PIECE)], 1, p, s, up_dev)

    def down(p, s, hi):
        c = 2 * p + s
        src = xr if hi == 3 else dr
        return remote(src.at[c, pl.ds(0, hi * PIECE)], dr.at[c, pl.ds(0, hi * PIECE)], 2, p, s, down_dev)

    def last(p, s):
        c = 2 * p + s
        return remote(fb.at[c, pl.ds((1 - b_pos[s]) * SUB, SUB)], yr.at[c], 3, p, s, b_dev[s])

    def sub_rows(p, s):
        return pl.ds(base(p, s) + a_pos[s] * HALF + z * PIECE + b_pos[s] * SUB, SUB)

    def last_back(p, s):
        c = 2 * p + s
        return remote(fb.at[c, pl.ds(b_pos[s] * SUB, SUB)], out_ref.at[sub_rows(p, s)], 4, p, s, b_dev[s])

    def keep(p, s):
        c = 2 * p + s
        return pltpu.make_async_copy(fb.at[c, pl.ds(b_pos[s] * SUB, SUB)], out_ref.at[sub_rows(p, s)], loc.at[1, s, lax.rem(p, NS)])

    def piece_of(p, s, k):
        return out_ref.at[pl.ds(base(p, s) + a_pos[s] * HALF + k * PIECE, PIECE)]

    def up_back(p, s, hop):
        k = jnp.maximum(z - hop, 0)
        return remote(piece_of(p, s, k), piece_of(p, s, k), 5 + hop, p, s, up_dev)

    def down_back(p, s, hop):
        k = jnp.minimum(z + hop, 3)
        return remote(piece_of(p, s, k), piece_of(p, s, k), 8 + hop, p, s, down_dev)

    def first_back(p, s):
        rows = out_ref.at[pl.ds(base(p, s) + a_pos[s] * HALF, HALF)]
        return remote(rows, rows, 11, p, s, a_dev[s])

    def add(*terms):
        total = terms[0].astype(jnp.float32)
        for term in terms[1:]:
            total = total + term.astype(jnp.float32)
        return total.astype(jnp.bfloat16)

    def step_a(p):
        for s in range(2):
            first(p, s).start()
            mine(p, s).start()

    def step_b(p):
        for s in range(2):
            c = 2 * p + s
            first(p, s).wait_recv()
            mine(p, s).wait()
            xr[c] = add(own[c], xr[c])

            @pl.when(z == 0)
            def _():
                up(p, s, 1).start()

            @pl.when(z == 3)
            def _():
                down(p, s, 3).start()

    def step_c(p):
        for s in range(2):
            c = 2 * p + s

            @pl.when(z == 1)
            def _():
                up(p, s, 1).wait_recv()
                ur[c, 2 * PIECE:] = add(ur[c, 2 * PIECE:], xr[c, 2 * PIECE:])
                up(p, s, 2).start()

            @pl.when(z == 2)
            def _():
                down(p, s, 3).wait_recv()
                dr[c, : 2 * PIECE] = add(dr[c, : 2 * PIECE], xr[c, : 2 * PIECE])
                down(p, s, 2).start()

    def step_d(p):
        for s in range(2):
            c = 2 * p + s

            @pl.when(z == 2)
            def _():
                up(p, s, 2).wait_recv()
                ur[c, 3 * PIECE:] = add(ur[c, 3 * PIECE:], xr[c, 3 * PIECE:])
                up(p, s, 3).start()

            @pl.when(z == 1)
            def _():
                down(p, s, 2).wait_recv()
                dr[c, :PIECE] = add(dr[c, :PIECE], xr[c, :PIECE])
                down(p, s, 1).start()

    def step_e(p):
        for s in range(2):
            c = 2 * p + s

            @pl.when(z == 0)
            def _():
                down(p, s, 1).wait_recv()
                fb[c] = add(xr[c, :PIECE], dr[c, :PIECE])

            @pl.when(z == 1)
            def _():
                fb[c] = add(xr[c, PIECE: 2 * PIECE], ur[c, PIECE: 2 * PIECE], dr[c, PIECE: 2 * PIECE])

            @pl.when(z == 2)
            def _():
                fb[c] = add(xr[c, 2 * PIECE: 3 * PIECE], ur[c, 2 * PIECE: 3 * PIECE], dr[c, 2 * PIECE: 3 * PIECE])

            @pl.when(z == 3)
            def _():
                up(p, s, 3).wait_recv()
                fb[c] = add(xr[c, 3 * PIECE:], ur[c, 3 * PIECE:])

            last(p, s).start()

    def step_f(p):
        for s in range(2):
            c = 2 * p + s
            last(p, s).wait_recv()
            rows = pl.ds(pl.multiple_of(b_pos[s] * SUB, SUB), SUB)
            fb[c, rows] = add(fb[c, rows], yr[c])
            last_back(p, s).start()
            keep(p, s).start()

    def step_g(p):
        for s in range(2):
            last_back(p, s).wait_recv()
            keep(p, s).wait()

            @pl.when(has_up)
            def _():
                up_back(p, s, 0).start()

            @pl.when(has_down)
            def _():
                down_back(p, s, 0).start()

    def step_h(p):
        for s in range(2):
            @pl.when(has_down)
            def _():
                up_back(p, s, 0).wait_recv()

            @pl.when(has_down & has_up)
            def _():
                up_back(p, s, 1).start()

            @pl.when(has_up)
            def _():
                down_back(p, s, 0).wait_recv()

            @pl.when(has_down & has_up)
            def _():
                down_back(p, s, 1).start()

    def step_i(p):
        for s in range(2):
            @pl.when(z >= 2)
            def _():
                up_back(p, s, 1).wait_recv()

            @pl.when(z == 2)
            def _():
                up_back(p, s, 2).start()

            @pl.when(z <= 1)
            def _():
                down_back(p, s, 1).wait_recv()

            @pl.when(z == 1)
            def _():
                down_back(p, s, 2).start()

    def step_j(p):
        for s in range(2):
            @pl.when(z == 3)
            def _():
                up_back(p, s, 2).wait_recv()

            @pl.when(z == 0)
            def _():
                down_back(p, s, 2).wait_recv()

            first_back(p, s).start()

    def step_k(p):
        for s in range(2):
            first_back(p, s).wait()
            first(p, s).wait_send()
            last(p, s).wait_send()
            last_back(p, s).wait_send()
            for k in range(3):
                @pl.when(z == k)
                def _():
                    up(p, s, k + 1).wait_send()

                @pl.when(z == k + 1)
                def _():
                    down(p, s, k + 1).wait_send()

            @pl.when(has_up)
            def _():
                up_back(p, s, 0).wait_send()

            @pl.when(has_down)
            def _():
                down_back(p, s, 0).wait_send()

            @pl.when(has_up & has_down)
            def _():
                up_back(p, s, 1).wait_send()
                down_back(p, s, 1).wait_send()

            @pl.when(z == 2)
            def _():
                up_back(p, s, 2).wait_send()

            @pl.when(z == 1)
            def _():
                down_back(p, s, 2).wait_send()

    small_devs = (c_dev, x_dev, y_dev, z1_dev, z2_dev)

    def small_copy(i):
        return pltpu.make_async_remote_copy(
            src_ref=sacc, dst_ref=sbuf.at[i], send_sem=ssend.at[i], recv_sem=srecv.at[i],
            device_id=small_devs[i], device_id_type=MESH)

    sacc[...] = small_ref[...]
    small_copy(0).start()
    for q in range(AHEAD):
        step_a(q)

    def iteration(t, _):
        def run(step, offset):
            p = t - offset

            @pl.when((p >= 0) & (p < pairs))
            def _():
                step(p)

        steps = dict(a=step_a, b=step_b, c=step_c, d=step_d, e=step_e, f=step_f, g=step_g, h=step_h, i=step_i, j=step_j, k=step_k)
        for name, off in ORDER:
            run(steps[name], off)
        for i in range(5):
            @pl.when(t == i + 1)
            def _():
                small_copy(i).wait()
                sacc[...] += sbuf[i]
                if i < 4:
                    small_copy(i + 1).start()
        return 0


    lax.fori_loop(0, pairs + max(o for _, o in ORDER), iteration, 0)
    small_out[...] = sacc[...]


def reduce_all(grads, small):
    rows = grads.shape[0]
    chunks = rows // CH
    return pl.pallas_call(
        functools.partial(reduce_kernel, chunks // 2),
        out_shape=(jax.ShapeDtypeStruct(grads.shape, jnp.bfloat16), jax.ShapeDtypeStruct(small.shape, jnp.float32)),
        in_specs=[pl.BlockSpec(memory_space=pl.ANY), pl.BlockSpec(memory_space=pltpu.VMEM)],
        out_specs=(pl.BlockSpec(memory_space=pl.ANY), pl.BlockSpec(memory_space=pltpu.VMEM)),
        scratch_shapes=[
            pltpu.VMEM((chunks, HALF, 1024), jnp.bfloat16),
            pltpu.VMEM((chunks, HALF, 1024), jnp.bfloat16),
            pltpu.VMEM((chunks, HALF, 1024), jnp.bfloat16),
            pltpu.VMEM((chunks, HALF, 1024), jnp.bfloat16),
            pltpu.VMEM((chunks, PIECE, 1024), jnp.bfloat16),
            pltpu.VMEM((chunks, SUB, 1024), jnp.bfloat16),
            pltpu.VMEM((SMALL, 1024), jnp.float32),
            pltpu.VMEM((5, SMALL, 1024), jnp.float32),
            pltpu.SemaphoreType.DMA((12, 2, NS)),
            pltpu.SemaphoreType.DMA((12, 2, NS)),
            pltpu.SemaphoreType.DMA((2, 2, NS)),
            pltpu.SemaphoreType.DMA((5,)),
            pltpu.SemaphoreType.DMA((5,)),
        ],
        compiler_params=pltpu.CompilerParams(collective_id=0, has_side_effects=True, vmem_limit_bytes=56 << 20),
    )(grads, small)


epsilon = 1e-05
negative = -1e30


def layer_norm(stream, norm_gain, norm_shift):
    row_mean = jnp.mean(stream, axis=-1, keepdims=True)
    centered = stream - row_mean
    row_var = jnp.mean(centered * centered, axis=-1, keepdims=True)
    return centered * lax.rsqrt(row_var + epsilon) * norm_gain + norm_shift


def norm_back(stream, norm_gain, norm_shift, upstream):
    outcome, pullback = jax.vjp(layer_norm, stream, norm_gain, norm_shift)
    return pullback(upstream)


def product(left, right):
    return jnp.dot(left, right, preferred_element_type=jnp.float32)


def contract_rows(left, right):
    return lax.dot_general(
        left, right, (((0,), (0,)), ((), ())), preferred_element_type=jnp.float32
    )


def contract_cols(left, right):
    return lax.dot_general(
        left, right, (((1,), (1,)), ((), ())), preferred_element_type=jnp.float32
    )


def score_block(query_blk, key_blk, count_blk, key_limit):
    raw = jnp.einsum("gshe,gkhe->ghsk", query_blk, key_blk, preferred_element_type=jnp.float32)
    scores = raw * HD ** (-0.5)
    positions = jnp.arange(key_limit, dtype=jnp.int32)
    valid_mask = positions[None, :] < count_blk[:, None]
    return jnp.where(valid_mask[:, None, None, :], scores, negative)


def attend_block(operands, key_limit):
    query_blk, key_blk, value_blk, count_blk = operands
    scores = score_block(query_blk, key_blk, count_blk, key_limit)
    top_score = jnp.max(scores, axis=-1, keepdims=True)
    row_total = jnp.sum(jnp.exp(scores - top_score), axis=-1, keepdims=True)
    log_total = top_score + jnp.log(row_total)
    attn_prob = jnp.exp(scores - log_total).astype(jnp.bfloat16)
    mixed = jnp.einsum("ghsk,gkhe->gshe", attn_prob, value_blk, preferred_element_type=jnp.float32)
    return (mixed, log_total[..., 0])


def attend_back(operands, key_limit):
    query_blk, key_blk, value_blk, count_blk, total_blk, grad_blk = operands
    scores = score_block(query_blk, key_blk, count_blk, key_limit)
    attn_full = jnp.exp(scores - total_blk[..., None])
    attn_prob = attn_full.astype(jnp.bfloat16)
    grad_value = jnp.einsum(
        "ghsk,gshe->gkhe", attn_prob, grad_blk, preferred_element_type=jnp.float32
    )
    grad_prob = jnp.einsum(
        "gshe,gkhe->ghsk", grad_blk, value_blk, preferred_element_type=jnp.float32
    )
    inner = jnp.sum(grad_prob * attn_full, axis=-1, keepdims=True)
    grad_score = (attn_full * (grad_prob - inner) * HD ** (-0.5)).astype(jnp.bfloat16)
    grad_query = jnp.einsum(
        "ghsk,gkhe->gshe", grad_score, key_blk, preferred_element_type=jnp.float32
    )
    grad_key = jnp.einsum(
        "ghsk,gshe->gkhe", grad_score, query_blk, preferred_element_type=jnp.float32
    )
    return (grad_query, grad_key, grad_value)


def fold(matrix):
    rows, width = matrix.shape
    if width < 1024:
        return jnp.concatenate(jnp.split(matrix, 1024 // width, axis=0), axis=1)
    return jnp.concatenate(jnp.split(matrix, width // 1024, axis=1), axis=0)


def unfold(block, rows):
    height = block.shape[0]
    if height < rows:
        pieces = jnp.split(block, rows // height, axis=1)
        return jnp.concatenate(pieces, axis=0).astype(jnp.float32)
    pieces = jnp.split(block, height // rows, axis=0)
    return jnp.concatenate(pieces, axis=1).astype(jnp.float32)


def pair_apply(block_fn, span, operands):
    return block_fn(operands, key_limit=span)


def group_size_of():
    return 2


def attention_forward(queries, key_rows, value_rows, counts, span):
    group_count = counts.shape[0]
    pair_size = group_size_of()
    pair_count = group_count // pair_size
    head_local = queries.shape[1] // HD
    query_pairs = queries.reshape(pair_count, pair_size, GS, head_local, HD)
    key_pairs = key_rows.reshape(pair_count, pair_size, span, head_local, HD)
    value_pairs = value_rows.reshape(pair_count, pair_size, span, head_local, HD)
    count_pairs = counts.reshape(pair_count, pair_size)

    def one_pair(pieces):
        return pair_apply(attend_block, span, pieces)

    mixed, log_total = lax.map(one_pair, (query_pairs, key_pairs, value_pairs, count_pairs))
    return (mixed.reshape(group_count * GS, head_local * HD).astype(jnp.bfloat16), log_total)


def attention_backward(queries, key_rows, value_rows, counts, log_total, grad_mixed, span):
    group_count = counts.shape[0]
    pair_size = group_size_of()
    pair_count = group_count // pair_size
    head_local = queries.shape[1] // HD
    query_pairs = queries.reshape(pair_count, pair_size, GS, head_local, HD)
    key_pairs = key_rows.reshape(pair_count, pair_size, span, head_local, HD)
    value_pairs = value_rows.reshape(pair_count, pair_size, span, head_local, HD)
    count_pairs = counts.reshape(pair_count, pair_size)
    grad_pairs = grad_mixed.reshape(pair_count, pair_size, GS, head_local, HD)

    def one_pair(pieces):
        return pair_apply(attend_back, span, pieces)

    grad_query, grad_key, grad_value = lax.map(
        one_pair, (query_pairs, key_pairs, value_pairs, count_pairs, log_total, grad_pairs)
    )
    width_local = head_local * HD
    return (
        grad_query.reshape(group_count * GS, width_local).astype(jnp.bfloat16),
        grad_key.reshape(group_count * span, width_local).astype(jnp.bfloat16),
        grad_value.reshape(group_count * span, width_local).astype(jnp.bfloat16),
    )


def local(
    latents,
    inputs,
    valid_counts,
    cotangent,
    gain_latent,
    shift_latent,
    gain_input,
    shift_input,
    cross_query,
    cross_key,
    cross_value,
    cross_out,
    gain_self,
    shift_self,
    self_query,
    self_key,
    self_value,
    self_out,
    gain_mlp,
    shift_mlp,
    mlp_in,
    mlp_in_bias,
    mlp_out,
    mlp_out_bias,
):
    stream_zero = latents.astype(jnp.float32)
    input_rows = inputs.astype(jnp.float32)
    latent_normed = layer_norm(stream_zero, gain_latent, shift_latent).astype(jnp.bfloat16)
    input_normed = layer_norm(input_rows, gain_input, shift_input).astype(jnp.bfloat16)
    cross_rows, cross_inputs, all_cotangent = (
        lax.all_gather(latent_normed, "mp", axis=0, tiled=True),
        lax.all_gather(input_normed, "mp", axis=0, tiled=True),
        lax.all_gather(cotangent, "mp", axis=0, tiled=True),
    )
    cross_queries = product(cross_rows, cross_query).astype(jnp.bfloat16)
    cross_keys = product(cross_inputs, cross_key).astype(jnp.bfloat16)
    cross_values = product(cross_inputs, cross_value).astype(jnp.bfloat16)
    cross_mixed, cross_total = attention_forward(
        cross_queries, cross_keys, cross_values, valid_counts, IN
    )
    stream_one = stream_zero + lax.psum_scatter(
        product(cross_mixed, cross_out).astype(jnp.bfloat16), "mp", scatter_dimension=0, tiled=True
    ).astype(jnp.float32)
    self_normed = layer_norm(stream_one, gain_self, shift_self).astype(jnp.bfloat16)
    self_rows = lax.all_gather(self_normed, "mp", axis=0, tiled=True)
    self_queries = product(self_rows, self_query).astype(jnp.bfloat16)
    self_keys = product(self_rows, self_key).astype(jnp.bfloat16)
    self_values = product(self_rows, self_value).astype(jnp.bfloat16)
    full_counts = jnp.full(valid_counts.shape, GS, jnp.int32)
    self_mixed, self_total = attention_forward(
        self_queries, self_keys, self_values, full_counts, GS
    )
    stream_two = stream_one + lax.psum_scatter(
        product(self_mixed, self_out).astype(jnp.bfloat16), "mp", scatter_dimension=0, tiled=True
    ).astype(jnp.float32)
    mlp_normed = layer_norm(stream_two, gain_mlp, shift_mlp).astype(jnp.bfloat16)
    mlp_rows = lax.all_gather(mlp_normed, "mp", axis=0, tiled=True)
    hidden = product(mlp_rows, mlp_in) + mlp_in_bias
    activation = jax.nn.gelu(hidden, approximate=False).astype(jnp.bfloat16)
    stream_three = stream_two + (
        lax.psum_scatter(
            product(activation, mlp_out).astype(jnp.bfloat16), "mp", scatter_dimension=0, tiled=True
        ).astype(jnp.float32)
        + mlp_out_bias
    )
    result_latents = stream_three.astype(jnp.bfloat16)
    grad_mlp_out = contract_rows(activation, all_cotangent)
    grad_mlp_out_bias = jnp.sum(all_cotangent, axis=0, dtype=jnp.float32)
    grad_activation = contract_cols(all_cotangent, mlp_out)
    outcome, gelu_pull = jax.vjp(partial(jax.nn.gelu, approximate=False), hidden)
    grad_hidden = gelu_pull(grad_activation)[0].astype(jnp.bfloat16)
    grad_mlp_in = contract_rows(mlp_rows, grad_hidden)
    grad_mlp_in_bias = jnp.sum(grad_hidden, axis=0, dtype=jnp.float32)
    grad_mlp_normed = lax.psum_scatter(
        contract_cols(grad_hidden, mlp_in).astype(jnp.bfloat16),
        "mp",
        scatter_dimension=0,
        tiled=True,
    ).astype(jnp.float32)
    grad_added, grad_gain_mlp, grad_shift_mlp = norm_back(
        stream_two, gain_mlp, shift_mlp, grad_mlp_normed
    )
    grad_two = cotangent.astype(jnp.float32) + grad_added
    self_cotangent = lax.all_gather(grad_two.astype(jnp.bfloat16), "mp", axis=0, tiled=True)
    grad_self_out = contract_rows(self_mixed, self_cotangent)
    grad_self_mixed = contract_cols(self_cotangent, self_out).astype(jnp.bfloat16)
    grad_self_queries, grad_self_keys, grad_self_values = attention_backward(
        self_queries, self_keys, self_values, full_counts, self_total, grad_self_mixed, GS
    )
    grad_self_query = contract_rows(self_rows, grad_self_queries)
    grad_self_key = contract_rows(self_rows, grad_self_keys)
    grad_self_value = contract_rows(self_rows, grad_self_values)
    grad_self_normed = lax.psum_scatter(
        (
            contract_cols(grad_self_queries, self_query)
            + contract_cols(grad_self_keys, self_key)
            + contract_cols(grad_self_values, self_value)
        ).astype(jnp.bfloat16),
        "mp",
        scatter_dimension=0,
        tiled=True,
    ).astype(jnp.float32)
    grad_added, grad_gain_self, grad_shift_self = norm_back(
        stream_one, gain_self, shift_self, grad_self_normed
    )
    grad_one = grad_two + grad_added
    cross_cotangent = lax.all_gather(grad_one.astype(jnp.bfloat16), "mp", axis=0, tiled=True)
    grad_cross_out = contract_rows(cross_mixed, cross_cotangent)
    grad_cross_mixed = contract_cols(cross_cotangent, cross_out).astype(jnp.bfloat16)
    grad_cross_queries, grad_cross_keys, grad_cross_values = attention_backward(
        cross_queries, cross_keys, cross_values, valid_counts, cross_total, grad_cross_mixed, IN
    )
    grad_cross_query = contract_rows(cross_rows, grad_cross_queries)
    grad_cross_key = contract_rows(cross_inputs, grad_cross_keys)
    grad_cross_value = contract_rows(cross_inputs, grad_cross_values)
    latent_part = contract_cols(grad_cross_queries, cross_query)
    input_part = contract_cols(grad_cross_keys, cross_key) + contract_cols(
        grad_cross_values, cross_value
    )
    grad_latent_normed, grad_input_normed = (
        lax.psum_scatter(
            latent_part.astype(jnp.bfloat16), "mp", scatter_dimension=0, tiled=True
        ).astype(jnp.float32),
        lax.psum_scatter(
            input_part.astype(jnp.bfloat16), "mp", scatter_dimension=0, tiled=True
        ).astype(jnp.float32),
    )
    grad_added, grad_gain_latent, grad_shift_latent = norm_back(
        stream_zero, gain_latent, shift_latent, grad_latent_normed
    )
    grad_latents = grad_one + grad_added
    grad_inputs, grad_gain_input, grad_shift_input = norm_back(
        input_rows, gain_input, shift_input, grad_input_normed
    )
    core = lax.axis_index("mp")
    half = mlp_in_bias.shape[0]
    bias_row = jnp.zeros((2, half), jnp.float32).at[core].set(grad_mlp_in_bias)
    out_bias = jnp.sum(cotangent, axis=0, dtype=jnp.float32)
    small = jnp.concatenate(
        [
            jnp.stack(
                [
                    grad_gain_latent,
                    grad_shift_latent,
                    grad_gain_input,
                    grad_shift_input,
                    grad_gain_self,
                    grad_shift_self,
                    grad_gain_mlp,
                    grad_shift_mlp,
                    out_bias,
                ]
            ),
            bias_row.reshape(4, 1024),
            jnp.zeros((3, 1024), jnp.float32),
        ]
    )
    tall = (grad_cross_query, grad_cross_key, grad_cross_value, grad_self_query, grad_self_key, grad_self_value)
    blocks = [grad_mlp_out, fold(grad_mlp_in), grad_self_out, grad_cross_out] + [fold(v) for v in tall]
    packed = jnp.concatenate([v.astype(jnp.bfloat16) for v in blocks])
    if lax.axis_size("dp") == 16:
        packed, small = reduce_all(packed, small)
    else:
        packed, small = lax.psum(packed, "dp"), lax.psum(small, ("dp", "mp"))
    parts, place = [], 0
    for block in blocks:
        parts.append(lax.slice_in_dim(packed, place, place + block.shape[0]))
        place += block.shape[0]
    grad_mlp_out = parts[0].astype(jnp.float32)
    grad_mlp_in = unfold(parts[1], 1024)
    grad_self_out = parts[2].astype(jnp.float32)
    grad_cross_out = parts[3].astype(jnp.float32)
    grad_cross_query, grad_cross_key, grad_cross_value, grad_self_query, grad_self_key, grad_self_value = [
        unfold(v, 1024) for v in parts[4:]
    ]
    (
        grad_gain_latent,
        grad_shift_latent,
        grad_gain_input,
        grad_shift_input,
        grad_gain_self,
        grad_shift_self,
        grad_gain_mlp,
        grad_shift_mlp,
        grad_mlp_out_bias,
    ) = [small[i] for i in range(9)]
    grad_mlp_in_bias = lax.dynamic_slice_in_dim(small[9:13].reshape(-1), core * half, half)
    return (
        result_latents,
        grad_latents,
        grad_inputs,
        grad_gain_latent,
        grad_shift_latent,
        grad_gain_input,
        grad_shift_input,
        grad_cross_query,
        grad_cross_key,
        grad_cross_value,
        grad_cross_out,
        grad_gain_self,
        grad_shift_self,
        grad_self_query,
        grad_self_key,
        grad_self_value,
        grad_self_out,
        grad_gain_mlp,
        grad_shift_mlp,
        grad_mlp_in,
        grad_mlp_in_bias,
        grad_mlp_out,
        grad_mlp_out_bias,
    )


def solution(mesh):
    return jax.shard_map(
        local,
        mesh=mesh,
        in_specs=(
            P(("dp", "mp"), None),
            P(("dp", "mp"), None),
            P("dp"),
            P(("dp", "mp"), None),
            P(),
            P(),
            P(),
            P(),
            P(None, "mp"),
            P(None, "mp"),
            P(None, "mp"),
            P("mp", None),
            P(),
            P(),
            P(None, "mp"),
            P(None, "mp"),
            P(None, "mp"),
            P("mp", None),
            P(),
            P(),
            P(None, "mp"),
            P("mp"),
            P("mp", None),
            P(),
        ),
        out_specs=(
            P(("dp", "mp"), None),
            P(("dp", "mp"), None),
            P(("dp", "mp"), None),
            P(),
            P(),
            P(),
            P(),
            P(None, "mp"),
            P(None, "mp"),
            P(None, "mp"),
            P("mp", None),
            P(),
            P(),
            P(None, "mp"),
            P(None, "mp"),
            P(None, "mp"),
            P("mp", None),
            P(),
            P(),
            P(None, "mp"),
            P("mp"),
            P("mp", None),
            P(),
        ),
        check_vma=False,
    )
```

```python
import functools
import math

import jax
import jax.numpy as jnp
from jax import lax
from jax.experimental import pallas as pl
from jax.experimental.pallas import tpu as pltpu
from jax.sharding import PartitionSpec as P

MESH = pl.DeviceIdType.MESH
NS = 16
AHEAD = 2
ORDER = (("a", -2), ("b", 0), ("f", 2), ("j", 4), ("d", 1), ("h", 3), ("c", 0), ("g", 2), ("e", 1), ("i", 3), ("k", 6))
CH = 256
HALF = CH // 2
PIECE = HALF // 4
SUB = PIECE // 2
SMALL = 16


def reduce_kernel(pairs, g_ref, small_ref, out_ref, small_out, own, xr, ur, dr, fb, yr, sacc, sbuf, send, recv, loc, ssend, srecv):
    dp = lax.axis_index("dp")
    core = lax.axis_index("mp")
    z = dp // 4
    px = lax.rem(dp, 2)
    py = lax.rem(dp // 2, 2)
    x_dev = (dp + 1 - 2 * px, core)
    y_dev = (dp + 2 - 4 * py, core)
    c_dev = (dp, 1 - core)
    up_dev = (dp + 4, core)
    down_dev = (dp - 4, core)
    z1_dev = (dp + 4 - 8 * lax.rem(z, 2), core)
    z2_dev = (dp + 8 - 16 * (z // 2), core)
    has_up = z < 3
    has_down = z > 0

    barrier = pltpu.get_barrier_semaphore()
    for dev in (x_dev, y_dev, c_dev, z2_dev):
        pl.semaphore_signal(barrier, inc=1, device_id=dev, device_id_type=MESH)

    @pl.when(has_up)
    def _():
        pl.semaphore_signal(barrier, inc=1, device_id=up_dev, device_id_type=MESH)

    @pl.when(has_down)
    def _():
        pl.semaphore_signal(barrier, inc=1, device_id=down_dev, device_id_type=MESH)

    pl.semaphore_wait(barrier, 4 + has_up.astype(jnp.int32) + has_down.astype(jnp.int32))

    def remote(src, dst, kind, p, s, dev):
        slot = lax.rem(p, NS)
        return pltpu.make_async_remote_copy(
            src_ref=src, dst_ref=dst, send_sem=send.at[kind, s, slot], recv_sem=recv.at[kind, s, slot],
            device_id=dev, device_id_type=MESH)

    a_pos = (px, py)
    b_pos = (py, px)
    a_dev = (x_dev, y_dev)
    b_dev = (y_dev, x_dev)

    def base(p, s):
        return (2 * p + s) * CH

    def first(p, s):
        c = 2 * p + s
        return remote(g_ref.at[pl.ds(base(p, s) + (1 - a_pos[s]) * HALF, HALF)], xr.at[c], 0, p, s, a_dev[s])

    def mine(p, s):
        c = 2 * p + s
        return pltpu.make_async_copy(g_ref.at[pl.ds(base(p, s) + a_pos[s] * HALF, HALF)], own.at[c], loc.at[0, s, lax.rem(p, NS)])

    def up(p, s, lo):
        c = 2 * p + s
        src = xr if lo == 1 else ur
        return remote(src.at[c, pl.ds(lo * PIECE, (4 - lo) * PIECE)], ur.at[c, pl.ds(lo * PIECE, (4 - lo) * PIECE)], 1, p, s, up_dev)

    def down(p, s, hi):
        c = 2 * p + s
        src = xr if hi == 3 else dr
        return remote(src.at[c, pl.ds(0, hi * PIECE)], dr.at[c, pl.ds(0, hi * PIECE)], 2, p, s, down_dev)

    def last(p, s):
        c = 2 * p + s
        return remote(fb.at[c, pl.ds((1 - b_pos[s]) * SUB, SUB)], yr.at[c], 3, p, s, b_dev[s])

    def sub_rows(p, s):
        return pl.ds(base(p, s) + a_pos[s] * HALF + z * PIECE + b_pos[s] * SUB, SUB)

    def last_back(p, s):
        c = 2 * p + s
        return remote(fb.at[c, pl.ds(b_pos[s] * SUB, SUB)], out_ref.at[sub_rows(p, s)], 4, p, s, b_dev[s])

    def keep(p, s):
        c = 2 * p + s
        return pltpu.make_async_copy(fb.at[c, pl.ds(b_pos[s] * SUB, SUB)], out_ref.at[sub_rows(p, s)], loc.at[1, s, lax.rem(p, NS)])

    def piece_of(p, s, k):
        return out_ref.at[pl.ds(base(p, s) + a_pos[s] * HALF + k * PIECE, PIECE)]

    def up_back(p, s, hop):
        k = jnp.maximum(z - hop, 0)
        return remote(piece_of(p, s, k), piece_of(p, s, k), 5 + hop, p, s, up_dev)

    def down_back(p, s, hop):
        k = jnp.minimum(z + hop, 3)
        return remote(piece_of(p, s, k), piece_of(p, s, k), 8 + hop, p, s, down_dev)

    def first_back(p, s):
        rows = out_ref.at[pl.ds(base(p, s) + a_pos[s] * HALF, HALF)]
        return remote(rows, rows, 11, p, s, a_dev[s])

    def add(*terms):
        total = terms[0].astype(jnp.float32)
        for term in terms[1:]:
            total = total + term.astype(jnp.float32)
        return total.astype(jnp.bfloat16)

    def step_a(p):
        for s in range(2):
            first(p, s).start()
            mine(p, s).start()

    def step_b(p):
        for s in range(2):
            c = 2 * p + s
            first(p, s).wait_recv()
            mine(p, s).wait()
            xr[c] = add(own[c], xr[c])

            @pl.when(z == 0)
            def _():
                up(p, s, 1).start()

            @pl.when(z == 3)
            def _():
                down(p, s, 3).start()

    def step_c(p):
        for s in range(2):
            c = 2 * p + s

            @pl.when(z == 1)
            def _():
                up(p, s, 1).wait_recv()
                ur[c, 2 * PIECE:] = add(ur[c, 2 * PIECE:], xr[c, 2 * PIECE:])
                up(p, s, 2).start()

            @pl.when(z == 2)
            def _():
                down(p, s, 3).wait_recv()
                dr[c, : 2 * PIECE] = add(dr[c, : 2 * PIECE], xr[c, : 2 * PIECE])
                down(p, s, 2).start()

    def step_d(p):
        for s in range(2):
            c = 2 * p + s

            @pl.when(z == 2)
            def _():
                up(p, s, 2).wait_recv()
                ur[c, 3 * PIECE:] = add(ur[c, 3 * PIECE:], xr[c, 3 * PIECE:])
                up(p, s, 3).start()

            @pl.when(z == 1)
            def _():
                down(p, s, 2).wait_recv()
                dr[c, :PIECE] = add(dr[c, :PIECE], xr[c, :PIECE])
                down(p, s, 1).start()

    def step_e(p):
        for s in range(2):
            c = 2 * p + s

            @pl.when(z == 0)
            def _():
                down(p, s, 1).wait_recv()
                fb[c] = add(xr[c, :PIECE], dr[c, :PIECE])

            @pl.when(z == 1)
            def _():
                fb[c] = add(xr[c, PIECE: 2 * PIECE], ur[c, PIECE: 2 * PIECE], dr[c, PIECE: 2 * PIECE])

            @pl.when(z == 2)
            def _():
                fb[c] = add(xr[c, 2 * PIECE: 3 * PIECE], ur[c, 2 * PIECE: 3 * PIECE], dr[c, 2 * PIECE: 3 * PIECE])

            @pl.when(z == 3)
            def _():
                up(p, s, 3).wait_recv()
                fb[c] = add(xr[c, 3 * PIECE:], ur[c, 3 * PIECE:])

            last(p, s).start()

    def step_f(p):
        for s in range(2):
            c = 2 * p + s
            last(p, s).wait_recv()
            rows = pl.ds(pl.multiple_of(b_pos[s] * SUB, SUB), SUB)
            fb[c, rows] = add(fb[c, rows], yr[c])
            last_back(p, s).start()
            keep(p, s).start()

    def step_g(p):
        for s in range(2):
            last_back(p, s).wait_recv()
            keep(p, s).wait()

            @pl.when(has_up)
            def _():
                up_back(p, s, 0).start()

            @pl.when(has_down)
            def _():
                down_back(p, s, 0).start()

    def step_h(p):
        for s in range(2):
            @pl.when(has_down)
            def _():
                up_back(p, s, 0).wait_recv()

            @pl.when(has_down & has_up)
            def _():
                up_back(p, s, 1).start()

            @pl.when(has_up)
            def _():
                down_back(p, s, 0).wait_recv()

            @pl.when(has_down & has_up)
            def _():
                down_back(p, s, 1).start()

    def step_i(p):
        for s in range(2):
            @pl.when(z >= 2)
            def _():
                up_back(p, s, 1).wait_recv()

            @pl.when(z == 2)
            def _():
                up_back(p, s, 2).start()

            @pl.when(z <= 1)
            def _():
                down_back(p, s, 1).wait_recv()

            @pl.when(z == 1)
            def _():
                down_back(p, s, 2).start()

    def step_j(p):
        for s in range(2):
            @pl.when(z == 3)
            def _():
                up_back(p, s, 2).wait_recv()

            @pl.when(z == 0)
            def _():
                down_back(p, s, 2).wait_recv()

            first_back(p, s).start()

    def step_k(p):
        for s in range(2):
            first_back(p, s).wait()
            first(p, s).wait_send()
            last(p, s).wait_send()
            last_back(p, s).wait_send()
            for k in range(3):
                @pl.when(z == k)
                def _():
                    up(p, s, k + 1).wait_send()

                @pl.when(z == k + 1)
                def _():
                    down(p, s, k + 1).wait_send()

            @pl.when(has_up)
            def _():
                up_back(p, s, 0).wait_send()

            @pl.when(has_down)
            def _():
                down_back(p, s, 0).wait_send()

            @pl.when(has_up & has_down)
            def _():
                up_back(p, s, 1).wait_send()
                down_back(p, s, 1).wait_send()

            @pl.when(z == 2)
            def _():
                up_back(p, s, 2).wait_send()

            @pl.when(z == 1)
            def _():
                down_back(p, s, 2).wait_send()

    small_devs = (c_dev, x_dev, y_dev, z1_dev, z2_dev)

    def small_copy(i):
        return pltpu.make_async_remote_copy(
            src_ref=sacc, dst_ref=sbuf.at[i], send_sem=ssend.at[i], recv_sem=srecv.at[i],
            device_id=small_devs[i], device_id_type=MESH)

    sacc[...] = small_ref[...]
    small_copy(0).start()
    for q in range(AHEAD):
        step_a(q)

    def iteration(t, _):
        def run(step, offset):
            p = t - offset

            @pl.when((p >= 0) & (p < pairs))
            def _():
                step(p)

        steps = dict(a=step_a, b=step_b, c=step_c, d=step_d, e=step_e, f=step_f, g=step_g, h=step_h, i=step_i, j=step_j, k=step_k)
        for name, off in ORDER:
            run(steps[name], off)
        for i in range(5):
            @pl.when(t == i + 1)
            def _():
                small_copy(i).wait()
                sacc[...] += sbuf[i]
                if i < 4:
                    small_copy(i + 1).start()
        return 0


    lax.fori_loop(0, pairs + max(o for _, o in ORDER), iteration, 0)
    small_out[...] = sacc[...]


def reduce_all(grads, small):
    rows = grads.shape[0]
    chunks = rows // CH
    return pl.pallas_call(
        functools.partial(reduce_kernel, chunks // 2),
        out_shape=(jax.ShapeDtypeStruct(grads.shape, jnp.bfloat16), jax.ShapeDtypeStruct(small.shape, jnp.float32)),
        in_specs=[pl.BlockSpec(memory_space=pl.ANY), pl.BlockSpec(memory_space=pltpu.VMEM)],
        out_specs=(pl.BlockSpec(memory_space=pl.ANY), pl.BlockSpec(memory_space=pltpu.VMEM)),
        scratch_shapes=[
            pltpu.VMEM((chunks, HALF, 1024), jnp.bfloat16),
            pltpu.VMEM((chunks, HALF, 1024), jnp.bfloat16),
            pltpu.VMEM((chunks, HALF, 1024), jnp.bfloat16),
            pltpu.VMEM((chunks, HALF, 1024), jnp.bfloat16),
            pltpu.VMEM((chunks, PIECE, 1024), jnp.bfloat16),
            pltpu.VMEM((chunks, SUB, 1024), jnp.bfloat16),
            pltpu.VMEM((SMALL, 1024), jnp.float32),
            pltpu.VMEM((5, SMALL, 1024), jnp.float32),
            pltpu.SemaphoreType.DMA((12, 2, NS)),
            pltpu.SemaphoreType.DMA((12, 2, NS)),
            pltpu.SemaphoreType.DMA((2, 2, NS)),
            pltpu.SemaphoreType.DMA((5,)),
            pltpu.SemaphoreType.DMA((5,)),
        ],
        compiler_params=pltpu.CompilerParams(collective_id=0, has_side_effects=True, vmem_limit_bytes=56 << 20),
    )(grads, small)


HD = 32
GS = 256
IN = 1024
WIDE = 1024
HALFW = 512
NEG = -1e30
EPS = 1e-05
LOG2E = math.log2(math.e)
SCALE = HD ** -0.5
bf16 = jnp.bfloat16
f32 = jnp.float32
ANY = pl.BlockSpec(memory_space=pl.ANY)
VM = pl.BlockSpec(memory_space=pltpu.VMEM)
SM = pl.BlockSpec(memory_space=pltpu.SMEM)


def nn(left, right):
    return jnp.dot(left, right, preferred_element_type=f32)


def nt(left, right):
    return lax.dot_general(left, right, (((1,), (1,)), ((), ())), preferred_element_type=f32)


def lanes(start, size):
    return pl.ds(pl.multiple_of(start, 128), size)


def rows_at(start, size):
    return pl.ds(pl.multiple_of(start, size), size)


def head_block(tile):
    lane = lax.broadcasted_iota(jnp.int32, tile.shape, 1) // HD
    zero = jnp.zeros_like(tile)
    return jnp.concatenate([jnp.where(lane == j, tile, zero) for j in range(4)], axis=0)


def scores_of(keys, query_block, count):
    scores = nt(keys, query_block)
    if count is None:
        return scores
    place = lax.broadcasted_iota(jnp.int32, scores.shape, 0)
    return jnp.where(place < count, scores, NEG)


def attend(queries, keys, values, count):
    values_t = values.T
    scores = scores_of(keys, head_block(queries), count)
    top = jnp.max(scores, axis=0, keepdims=True)
    weights = jnp.exp2((scores - top) * (LOG2E * SCALE))
    total = jnp.sum(weights, axis=0, keepdims=True)
    low = weights.astype(bf16)
    log_total = top * (LOG2E * SCALE) + jnp.log2(total)
    inverse = 1.0 / total
    mixed, logs = [], []
    for j in range(4):
        span = slice(j * GS, (j + 1) * GS)
        mixed.append(nn(values_t[j * HD:(j + 1) * HD], low[:, span]) * inverse[:, span])
        logs.append(log_total[:, span])
    return jnp.concatenate(mixed, axis=0), jnp.concatenate(logs, axis=0)


def attend_back(queries, keys, values, grads, logs, count):
    keys_t = keys.T
    query_block = head_block(queries)
    grad_block = head_block(grads)
    grad_keys = grad_values = None
    grad_queries = []
    for j in range(4):
        own_query = query_block[j * GS:(j + 1) * GS]
        own_grad = grad_block[j * GS:(j + 1) * GS]
        weights = jnp.exp2(scores_of(keys, own_query, count) * (LOG2E * SCALE) - logs[j:j + 1])
        weighted = weights * nt(values, own_grad)
        inner = jnp.sum(weighted, axis=0, keepdims=True)
        grad_scores = (weighted - weights * inner).astype(bf16)
        value_part = nn(weights.astype(bf16), own_grad)
        key_part = nn(grad_scores, own_query)
        grad_values = value_part if j == 0 else grad_values + value_part
        grad_keys = key_part if j == 0 else grad_keys + key_part
        grad_queries.append(nn(keys_t[j * HD:(j + 1) * HD], grad_scores))
    return jnp.concatenate(grad_queries, axis=0) * SCALE, grad_keys * SCALE, grad_values


def centre(stream):
    centered = stream - jnp.mean(stream, axis=1, keepdims=True)
    inverse = lax.rsqrt(jnp.mean(centered * centered, axis=1, keepdims=True) + EPS)
    return centered * inverse, inverse


def normed(stream, gain, shift):
    return (centre(stream)[0] * gain + shift).astype(bf16)


def norm_back(stream, gain, upstream):
    xhat, inverse = centre(stream)
    scaled = upstream * gain
    along = upstream * xhat
    mean_scaled = jnp.mean(scaled, axis=1, keepdims=True)
    mean_along = jnp.mean(scaled * xhat, axis=1, keepdims=True)
    grad = inverse * (scaled - mean_scaled - xhat * mean_along)
    return grad, jnp.sum(along, axis=0, keepdims=True), jnp.sum(upstream, axis=0, keepdims=True)


def meet(partner):
    barrier = pltpu.get_barrier_semaphore()
    pl.semaphore_signal(barrier, inc=1, device_id=partner, device_id_type=MESH)
    pl.semaphore_wait(barrier, 1)


FWD_IN = (
    ("latents", VM), ("inputs", VM), ("counts", SM), ("cot", ANY),
    ("gain_latent", VM), ("shift_latent", VM), ("gain_input", VM), ("shift_input", VM),
    ("gain_self", VM), ("shift_self", VM), ("gain_mlp", VM), ("shift_mlp", VM),
    ("cq", ANY), ("ck", ANY), ("cv", ANY), ("co", ANY), ("sq", ANY), ("sk", ANY), ("sv", ANY), ("so", ANY),
    ("mi", ANY), ("mib", VM), ("mo", ANY), ("mob", VM),
)
FWD_OUT = (
    ("result", (GS, WIDE), bf16, VM),
    ("s1", (GS, WIDE), f32, VM), ("s2", (GS, WIDE), f32, VM),
    ("lnlT", (WIDE, 2 * GS), bf16, ANY), ("lniT", (WIDE, 2 * IN), bf16, ANY),
    ("snT", (WIDE, 2 * GS), bf16, ANY), ("mnT", (WIDE, 2 * GS), bf16, ANY),
    ("actT", (2048, 2 * GS), bf16, ANY), ("dg", (GS, 4096), bf16, ANY),
    ("xq", (GS, WIDE), bf16, ANY), ("xk", (IN, WIDE), bf16, ANY), ("xv", (IN, WIDE), bf16, ANY),
    ("xoT", (HALFW, 2 * GS), bf16, ANY), ("xl", (8, 4, GS), f32, VM),
    ("yq", (GS, WIDE), bf16, ANY), ("yk", (GS, WIDE), bf16, ANY), ("yv", (GS, WIDE), bf16, ANY),
    ("yoT", (HALFW, 2 * GS), bf16, ANY), ("yl", (8, 4, GS), f32, VM),
    ("cotp", (GS, WIDE), bf16, ANY),
    ("rin", (6, WIDE, HALFW), bf16, ANY), ("rout", (2, HALFW, WIDE), bf16, ANY),
    ("rmi", (WIDE, 2048), bf16, ANY), ("rmo", (2048, WIDE), bf16, ANY),
)
FWD_SCRATCH = (
    ("wx", (2, 3, WIDE, HALFW), bf16), ("wxo", (2, HALFW, WIDE), bf16),
    ("wy", (2, 3, WIDE, HALFW), bf16), ("wyo", (2, HALFW, WIDE), bf16),
    ("wmi", (2, WIDE, HALFW), bf16), ("wmo", (2, HALFW, WIDE), bf16),
    ("rbias", (4, HALFW), f32),
    ("n", (GS, WIDE), bf16), ("ln", (IN, WIDE), bf16),
    ("t_l", (WIDE, GS), bf16), ("t_i", (WIDE, IN), bf16), ("t_s", (WIDE, GS), bf16), ("t_m", (WIDE, GS), bf16),
    ("q", (GS, WIDE), bf16), ("k", (IN, WIDE), bf16), ("v", (IN, WIDE), bf16), ("o", (GS, WIDE), bf16), ("oT", (WIDE, GS), bf16),
    ("q2", (GS, WIDE), bf16), ("k2", (GS, WIDE), bf16), ("v2", (GS, WIDE), bf16), ("o2", (GS, WIDE), bf16), ("oT2", (WIDE, GS), bf16),
    ("aT", (8, HALFW, GS), bf16), ("dgs", (8, GS, HALFW), bf16), ("acc", (GS, WIDE), f32),
)


class Names:
    pass


def named(refs, *tables):
    out = Names()
    place = 0
    for table in tables:
        for entry in table:
            setattr(out, entry[0], refs[place])
            place += 1
    out.rest = refs[place:]
    return out


def forward_kernel(*refs):
    r = named(refs, FWD_IN, FWD_OUT, FWD_SCRATCH)
    send, recv, local = r.rest
    core = lax.axis_index("mp")
    partner = (lax.axis_index("dp"), 1 - core)
    meet(partner)
    sent, kept = [], []

    def push(src, dst):
        i = len(sent)
        copy = pltpu.make_async_remote_copy(
            src_ref=src, dst_ref=dst, send_sem=send.at[i], recv_sem=recv.at[i], device_id=partner, device_id_type=MESH)
        copy.start()
        sent.append(copy)
        return copy

    def fetch(src, dst):
        i = len(kept)
        copy = pltpu.make_async_copy(src, dst, local.at[i])
        copy.start()
        kept.append([copy, False])
        return i

    def ready(i):
        kept[i][0].wait()
        kept[i][1] = True

    got = [push(r.ck, r.rin.at[1]), push(r.cv, r.rin.at[2]), push(r.cq, r.rin.at[0]), push(r.co, r.rout.at[0])]
    got.append(push(r.mib, r.rbias))
    near = [fetch(w, r.wx.at[0, i]) for i, w in ((1, r.ck), (2, r.cv), (0, r.cq))] + [fetch(r.co, r.wxo.at[0])]

    r.n[...] = normed(r.latents[...].astype(f32), r.gain_latent[...], r.shift_latent[...])
    r.t_l[...] = r.n[...].T
    fetch(r.t_l, r.lnlT.at[:, pl.ds(0, GS)])
    gain, shift = r.gain_input[...], r.shift_input[...]

    def input_norm(b, _):
        span = rows_at(b * GS, GS)
        block = normed(r.inputs[span].astype(f32), gain, shift)
        r.ln[span] = block
        r.t_i[:, lanes(b * GS, GS)] = block.T
        return 0

    lax.fori_loop(0, IN // GS, input_norm, 0)
    fetch(r.t_i, r.lniT.at[:, pl.ds(0, IN)])
    for i in near[:3]:
        ready(i)

    def project_inputs(half):
        def block(b, _):
            span = rows_at(b * GS, GS)
            rows = r.ln[span]
            r.k[span, half * HALFW:(half + 1) * HALFW] = nn(rows, r.wx[half, 1]).astype(bf16)
            r.v[span, half * HALFW:(half + 1) * HALFW] = nn(rows, r.wx[half, 2]).astype(bf16)
            return 0

        lax.fori_loop(0, IN // GS, block, 0)
        r.q[:, half * HALFW:(half + 1) * HALFW] = nn(r.n[...], r.wx[half, 0]).astype(bf16)

    project_inputs(0)
    got += [push(w, r.rin.at[i]) for i, w in ((3, r.sq), (4, r.sk), (5, r.sv))] + [push(r.so, r.rout.at[1])]
    far = []
    for copy, src, dst in (
        (got[0], r.rin.at[1], r.wx.at[1, 1]), (got[1], r.rin.at[2], r.wx.at[1, 2]),
        (got[2], r.rin.at[0], r.wx.at[1, 0]), (got[3], r.rout.at[0], r.wxo.at[1])):
        copy.wait_recv()
        far.append(fetch(src, dst))
    near2 = [fetch(w, r.wy.at[0, i]) for i, w in enumerate((r.sq, r.sk, r.sv))] + [fetch(r.so, r.wyo.at[0])]
    count = r.counts[core]

    def attention(queries, keys, values, mixed, mixed_t, logs, limit, first):
        def group(g, _):
            at = lanes(g * 128, 128)
            out_t, log_total = attend(queries[:, at], keys[:, at], values[:, at], limit)
            out_t = out_t.astype(bf16)
            mixed_t[rows_at(g * 128, 128)] = out_t
            mixed[:, at] = out_t.T
            logs[g] = log_total
            return 0

        lax.fori_loop(first, first + 4, group, 0)

    attention(r.q, r.k, r.v, r.o, r.oT, r.xl, count, 0)
    got.append(push(r.mi, r.rmi))
    got.append(push(r.mo, r.rmo))
    for i in far[:3]:
        ready(i)
    project_inputs(1)
    fetch(r.q, r.xq)
    fetch(r.k, r.xk)
    fetch(r.v, r.xv)
    attention(r.q, r.k, r.v, r.o, r.oT, r.xl, count, 4)
    fetch(r.oT.at[pl.ds(0, HALFW)], r.xoT.at[:, pl.ds(0, GS)])
    push(r.oT.at[pl.ds(HALFW, HALFW)], r.xoT.at[:, pl.ds(GS, GS)])
    push(r.t_l, r.lnlT.at[:, pl.ds(GS, GS)])
    push(r.t_i, r.lniT.at[:, pl.ds(IN, IN)])
    push(r.cot, r.cotp)
    ready(near[3])
    ready(far[3])

    def out_project(mixed, weight):
        return nn(mixed[:, :HALFW], weight[0]) + nn(mixed[:, HALFW:], weight[1])

    r.s1[...] = r.latents[...].astype(f32) + out_project(r.o, r.wxo)
    r.n[...] = normed(r.s1[...], r.gain_self[...], r.shift_self[...])
    far2 = []
    for copy, src, dst in (
        (got[5], r.rin.at[3], r.wy.at[1, 0]), (got[6], r.rin.at[4], r.wy.at[1, 1]),
        (got[7], r.rin.at[5], r.wy.at[1, 2]), (got[8], r.rout.at[1], r.wyo.at[1])):
        copy.wait_recv()
        far2.append(fetch(src, dst))
    r.t_s[...] = r.n[...].T
    fetch(r.t_s, r.snT.at[:, pl.ds(0, GS)])
    push(r.t_s, r.snT.at[:, pl.ds(GS, GS)])
    for i in near2 + far2:
        ready(i)
    for half in range(2):
        at = slice(half * HALFW, (half + 1) * HALFW)
        for i, dst in enumerate((r.q2, r.k2, r.v2)):
            dst[:, at] = nn(r.n[...], r.wy[half, i]).astype(bf16)
    fetch(r.q2, r.yq)
    fetch(r.k2, r.yk)
    fetch(r.v2, r.yv)
    attention(r.q2, r.k2, r.v2, r.o2, r.oT2, r.yl, None, 0)
    attention(r.q2, r.k2, r.v2, r.o2, r.oT2, r.yl, None, 4)
    fetch(r.oT2.at[pl.ds(0, HALFW)], r.yoT.at[:, pl.ds(0, GS)])
    push(r.oT2.at[pl.ds(HALFW, HALFW)], r.yoT.at[:, pl.ds(GS, GS)])

    chunk_sem = len(kept)

    def chunk_copies(src_in, src_out, c, slot):
        at = lanes(c * HALFW, HALFW)
        return (
            pltpu.make_async_copy(src_in.at[:, at], r.wmi.at[slot], local.at[chunk_sem + slot]),
            pltpu.make_async_copy(src_out.at[rows_at(c * HALFW, HALFW)], r.wmo.at[slot], local.at[chunk_sem + 2 + slot]),
        )

    def start_chunk(n):
        slot = lax.rem(n, 2)

        @pl.when(n < 4)
        def _():
            for copy in chunk_copies(r.mi, r.mo, n, slot):
                copy.start()

        @pl.when(n >= 4)
        def _():
            for copy in chunk_copies(r.rmi, r.rmo, n - 4, slot):
                copy.start()

    start_chunk(jnp.int32(0))
    r.s2[...] = r.s1[...] + out_project(r.o2, r.wyo)
    r.n[...] = normed(r.s2[...], r.gain_mlp[...], r.shift_mlp[...])
    r.t_m[...] = r.n[...].T
    kept += [None] * 4
    fetch(r.t_m, r.mnT.at[:, pl.ds(0, GS)])
    push(r.t_m, r.mnT.at[:, pl.ds(GS, GS)])
    r.acc[...] = jnp.zeros((GS, WIDE), f32)
    for copy in (got[4], got[9], got[10]):
        copy.wait_recv()

    def feed(n, _):
        slot = lax.rem(n, 2)

        @pl.when(n + 1 < 8)
        def _():
            start_chunk(n + 1)

        for copy in chunk_copies(r.mi, r.mo, 0, slot):
            copy.wait()
        bias = jnp.where(n < 4, r.mib[pl.ds(lax.rem(n, 4), 1)], r.rbias[pl.ds(lax.rem(n, 4), 1)])
        hidden = nn(r.n[...], r.wmi[slot]) + bias
        area = 0.5 + 0.5 * lax.erf(hidden * (0.5 ** 0.5))
        density = jnp.exp(-0.5 * hidden * hidden) * ((2 * math.pi) ** -0.5)
        act = (hidden * area).astype(bf16)
        r.dgs[n] = (area + hidden * density).astype(bf16)
        r.aT[n] = act.T
        r.acc[...] += nn(act, r.wmo[slot])
        return 0

    lax.fori_loop(0, 8, feed, 0)
    for c in range(4):
        fetch(r.aT.at[c], r.actT.at[pl.ds(c * HALFW, HALFW), pl.ds(0, GS)])
        push(r.aT.at[4 + c], r.actT.at[pl.ds(c * HALFW, HALFW), pl.ds(GS, GS)])
    for c in range(8):
        fetch(r.dgs.at[c], r.dg.at[:, pl.ds(c * HALFW, HALFW)])
    r.result[...] = (r.s2[...] + (r.acc[...] + r.mob[...])).astype(bf16)
    for i, entry in enumerate(kept):
        if entry is not None and not entry[1]:
            ready(i)
    seen = [id(c) for c in got]
    for copy in sent:
        copy.wait_send()
        if id(copy) not in seen:
            copy.wait_recv()


def forward(*args):
    return pl.pallas_call(
        forward_kernel,
        out_shape=[jax.ShapeDtypeStruct(shape, dtype) for _, shape, dtype, _ in FWD_OUT],
        in_specs=[spec for _, spec in FWD_IN],
        out_specs=[spec for _, _, _, spec in FWD_OUT],
        scratch_shapes=[pltpu.VMEM(shape, dtype) for _, shape, dtype in FWD_SCRATCH]
        + [pltpu.SemaphoreType.DMA((24,)), pltpu.SemaphoreType.DMA((24,)), pltpu.SemaphoreType.DMA((64,))],
        compiler_params=pltpu.CompilerParams(collective_id=1, has_side_effects=True, vmem_limit_bytes=60 << 20),
    )(*args)


BWD_IN = (
    ("latents", VM), ("inputs", ANY), ("counts", SM), ("cot", VM),
    ("gain_latent", VM), ("gain_input", VM), ("gain_self", VM), ("gain_mlp", VM),
    ("cq", ANY), ("ck", ANY), ("cv", ANY), ("co", ANY), ("sq", ANY), ("sk", ANY), ("sv", ANY), ("so", ANY),
    ("mi", ANY), ("mo", ANY),
) + tuple((name, VM if name in ("s1", "s2", "xl", "yl") else ANY) for name, _, _, _ in FWD_OUT[1:])
ROWS_OUT = 8192
BWD_OUT = (
    ("grads", (ROWS_OUT, WIDE), bf16, ANY), ("small", (16, WIDE), f32, VM),
    ("grad_latents", (GS, WIDE), f32, VM), ("grad_inputs", (IN, WIDE), f32, ANY),
)
BWD_SCRATCH = (
    ("wy", (2, 3, WIDE, HALFW), bf16), ("wyo", (2, HALFW, WIDE), bf16), ("wxo", (2, HALFW, WIDE), bf16),
    ("wmi", (2, WIDE, HALFW), bf16), ("wmo", (2, HALFW, WIDE), bf16),
    ("mc", (2 * GS, WIDE), bf16), ("sc", (2 * GS, WIDE), bf16), ("xc", (2 * GS, WIDE), bf16),
    ("dk", (2 * IN, HALFW), bf16), ("dgs", (2, GS, HALFW), bf16),
    ("mT", (WIDE, 2 * GS), bf16), ("dh", (2 * GS, 2048), bf16), ("dhr", (GS, 2048), bf16),
    ("sT", (WIDE, 2 * GS), bf16), ("kv", (2, IN, WIDE), bf16),
    ("q", (GS, WIDE), bf16), ("oT", (HALFW, 2 * GS), bf16),
    ("q2", (GS, WIDE), bf16), ("k2", (GS, WIDE), bf16), ("v2", (GS, WIDE), bf16), ("oT2", (HALFW, 2 * GS), bf16),
    ("g", (GS, WIDE), bf16),
    ("dq", (2 * GS, HALFW), bf16), ("dv", (2 * IN, HALFW), bf16),
    ("dqr", (GS, HALFW), bf16), ("dkr", (IN, HALFW), bf16), ("dvr", (IN, HALFW), bf16),
    ("dq2", (3, 2 * GS, HALFW), bf16), ("dqr2", (3, GS, HALFW), bf16),
    ("acc", (GS, WIDE), f32), ("xin", (2, GS, WIDE), bf16), ("xout", (2, GS, WIDE), f32),
    ("stage", (2, HALFW, WIDE), bf16), ("bsum", (8, HALFW), f32),
)
ROW_MO, ROW_MI, ROW_SO, ROW_SQ, ROW_CO, ROW_CQ = 0, 2048, 4096, 4608, 6144, 6656


def backward_kernel(*refs):
    r = named(refs, BWD_IN, BWD_OUT, BWD_SCRATCH)
    send, recv, local, stage_sem, chunk_sem, x_sem = r.rest
    core = lax.axis_index("mp")
    partner = (lax.axis_index("dp"), 1 - core)
    meet(partner)
    sent, kept = [], []

    def push(src, dst):
        i = len(sent)
        copy = pltpu.make_async_remote_copy(
            src_ref=src, dst_ref=dst, send_sem=send.at[i], recv_sem=recv.at[i], device_id=partner, device_id_type=MESH)
        copy.start()
        sent.append(copy)
        return copy

    def fetch(src, dst):
        copy = pltpu.make_async_copy(src, dst, local.at[len(kept)])
        copy.start()
        kept.append(copy)
        return copy

    staged = []

    def stage(write, row):
        i = len(staged)
        slot = i % 2
        if i >= 2:
            staged[i - 2].wait()
        write(r.stage.at[slot])
        copy = pltpu.make_async_copy(r.stage.at[slot], r.grads.at[pl.ds(row, HALFW)], stage_sem.at[slot])
        copy.start()
        staged.append(copy)

    early = [fetch(r.actT, r.dk), fetch(r.cotp, r.mc.at[pl.ds(GS, GS)])]

    def chunk_copies(src_in, src_out, c, n, slot):
        at = lanes(c * HALFW, HALFW)
        return (
            pltpu.make_async_copy(src_in.at[:, at], r.wmi.at[slot], chunk_sem.at[0, slot]),
            pltpu.make_async_copy(src_out.at[rows_at(c * HALFW, HALFW)], r.wmo.at[slot], chunk_sem.at[1, slot]),
            pltpu.make_async_copy(r.dg.at[:, lanes(n * HALFW, HALFW)], r.dgs.at[slot], chunk_sem.at[2, slot]),
        )

    def start_chunk(i):
        slot = lax.rem(i, 2)

        @pl.when(i < 4)
        def _():
            for copy in chunk_copies(r.rmi, r.rmo, i, 4 + i, slot):
                copy.start()

        @pl.when(i >= 4)
        def _():
            for copy in chunk_copies(r.mi, r.mo, i - 4, i - 4, slot):
                copy.start()

    start_chunk(jnp.int32(0))
    load_m = fetch(r.mnT, r.mT)
    load_y = [fetch(w, r.wy.at[0, i]) for i, w in enumerate((r.sq, r.sk, r.sv))]
    load_y += [fetch(r.rin.at[pl.ds(3, 3)], r.wy.at[1]), fetch(r.so, r.wyo.at[0]), fetch(r.rout.at[1], r.wyo.at[1])]
    load_y += [fetch(a, b) for a, b in ((r.yq, r.q2), (r.yk, r.k2), (r.yv, r.v2), (r.yoT, r.oT2), (r.snT, r.sT))]
    r.mc[pl.ds(0, GS)] = r.cot[...]
    for copy in early:
        copy.wait()
    for m in range(4):
        def write(dst, m=m):
            dst[...] = nn(r.dk[m * HALFW:(m + 1) * HALFW], r.mc[...]).astype(bf16)

        stage(write, ROW_MO + m * HALFW)
    r.acc[...] = jnp.zeros((GS, WIDE), f32)

    def feed(i, _):
        slot = lax.rem(i, 2)

        @pl.when(i + 1 < 8)
        def _():
            start_chunk(i + 1)

        for copy in chunk_copies(r.mi, r.mo, 0, 0, slot):
            copy.wait()
        grad = (nt(r.cot[...], r.wmo[slot]) * r.dgs[slot].astype(f32)).astype(bf16)
        r.bsum[pl.ds(lax.rem(i + 4, 8), 1)] = jnp.sum(grad.astype(f32), axis=0, keepdims=True)
        at = lanes(lax.rem(i, 4) * HALFW, HALFW)

        @pl.when(i < 4)
        def _():
            r.dhr[:, at] = grad

        @pl.when(i >= 4)
        def _():
            r.dh[pl.ds(0, GS), at] = grad

        r.acc[...] += nt(grad, r.wmi[slot])
        return 0

    lax.fori_loop(0, 4, feed, 0)
    push_dh = push(r.dhr, r.dh.at[pl.ds(GS, GS)])
    lax.fori_loop(4, 8, feed, 0)
    load_x = [fetch(r.co, r.wxo.at[0]), fetch(r.rout.at[0], r.wxo.at[1])]
    load_x += [fetch(a, b) for a, b in ((r.xq, r.q), (r.xk, r.kv.at[0]), (r.xv, r.kv.at[1]), (r.xoT, r.oT))]

    grad, along, plain = norm_back(r.s2[...], r.gain_mlp[...], r.acc[...])
    r.small[6:7] = along
    r.small[7:8] = plain
    r.acc[...] = r.cot[...].astype(f32) + grad
    r.sc[pl.ds(0, GS)] = r.acc[...].astype(bf16)
    push_c = push(r.sc.at[pl.ds(0, GS)], r.sc.at[pl.ds(GS, GS)])
    load_m.wait()
    push_dh.wait_recv()
    for c in range(4):
        def write(dst, c=c):
            dst[...] = jnp.concatenate(
                [nn(r.mT[c % 2 * HALFW:(c % 2 + 1) * HALFW], r.dh[:, (c // 2 * 2 + e) * HALFW:(c // 2 * 2 + e + 1) * HALFW]).astype(bf16)
                 for e in range(2)], axis=1)

        stage(write, ROW_MI + c * HALFW)
    load_l = fetch(r.lnlT, r.mT)

    def attention_back(queries, keys, values, logs, limit, first, dst_q, dst_k, dst_v):
        def group(g, _):
            at = lanes(g * 128, 128)
            to = lanes((g - first) * 128, 128)
            grad_q, grad_k, grad_v = attend_back(queries[:, at], keys[:, at], values[:, at], r.g[:, at], logs[g], limit)
            dst_q[pl.ds(0, GS), to] = grad_q.astype(bf16).T
            rows = grad_k.shape[0]
            dst_k[pl.ds(0, rows), to] = grad_k.astype(bf16)
            dst_v[pl.ds(0, rows), to] = grad_v.astype(bf16)
            return 0

        lax.fori_loop(first, first + 4, group, 0)

    def out_back(cots, weight):
        cot = cots[pl.ds(0, GS)]
        for half in range(2):
            r.g[:, half * HALFW:(half + 1) * HALFW] = nt(cot, weight[half]).astype(bf16)

    def grad_fold(left, right, row):
        def write(dst):
            for e in range(2):
                dst[:, e * HALFW:(e + 1) * HALFW] = nn(left[e * HALFW:(e + 1) * HALFW], right[...]).astype(bf16)

        stage(write, row)

    for copy in load_y:
        copy.wait()
    out_back(r.sc, r.wyo)
    attention_back(r.q2, r.k2, r.v2, r.yl, None, 4, r.dqr2.at[0], r.dqr2.at[1], r.dqr2.at[2])
    push_y = push(r.dqr2, r.dq2.at[:, pl.ds(GS, GS)])
    attention_back(r.q2, r.k2, r.v2, r.yl, None, 0, r.dq2.at[0], r.dq2.at[1], r.dq2.at[2])
    push_c.wait_recv()

    def write_so(dst):
        dst[...] = nn(r.oT2[...], r.sc[...]).astype(bf16)

    stage(write_so, ROW_SO)
    upstream = None
    for i in range(3):
        term = nt(r.dq2[i, :GS], r.wy[0, i]) + nt(r.dqr2[i], r.wy[1, i])
        upstream = term if upstream is None else upstream + term
    grad, along, plain = norm_back(r.s1[...], r.gain_self[...], upstream)
    r.small[4:5] = along
    r.small[5:6] = plain
    r.acc[...] += grad
    load_w = [fetch(w, r.wy.at[0, i]) for i, w in enumerate((r.cq, r.ck, r.cv))] + [fetch(r.rin.at[pl.ds(0, 3)], r.wy.at[1])]
    r.xc[pl.ds(0, GS)] = r.acc[...].astype(bf16)
    push_c2 = push(r.xc.at[pl.ds(0, GS)], r.xc.at[pl.ds(GS, GS)])
    push_y.wait_recv()
    for i in range(3):
        grad_fold(r.sT, r.dq2.at[i], ROW_SQ + i * HALFW)

    for copy in load_x:
        copy.wait()
    out_back(r.xc, r.wxo)
    count = r.counts[core]
    attention_back(r.q, r.kv.at[0], r.kv.at[1], r.xl, count, 4, r.dqr, r.dkr, r.dvr)
    push_x = [push(r.dqr, r.dq.at[pl.ds(GS, GS)]), push(r.dkr, r.dk.at[pl.ds(IN, IN)]), push(r.dvr, r.dv.at[pl.ds(IN, IN)])]
    attention_back(r.q, r.kv.at[0], r.kv.at[1], r.xl, count, 0, r.dq, r.dk, r.dv)
    load_i = [fetch(r.lniT.at[:, pl.ds(0, IN)], r.kv.at[0]), fetch(r.lniT.at[:, pl.ds(IN, IN)], r.kv.at[1])]
    push_c2.wait_recv()

    def write_co(dst):
        dst[...] = nn(r.oT[...], r.xc[...]).astype(bf16)

    stage(write_co, ROW_CO)
    for copy in push_x:
        copy.wait_recv()
    load_l.wait()
    grad_fold(r.mT, r.dq, ROW_CQ)
    for copy in load_i:
        copy.wait()

    def grad_tall(right, row):
        def write(dst):
            for e in range(2):
                at = slice(e * HALFW, (e + 1) * HALFW)
                dst[:, at] = (nn(r.kv[0, at], right[:IN]) + nn(r.kv[1, at], right[IN:])).astype(bf16)

        stage(write, row)

    grad_tall(r.dk, ROW_CQ + HALFW)
    grad_tall(r.dv, ROW_CQ + 2 * HALFW)
    for copy in load_w:
        copy.wait()
    upstream = nt(r.dq[:GS], r.wy[0, 0]) + nt(r.dqr[...], r.wy[1, 0])
    grad, along, plain = norm_back(r.latents[...].astype(f32), r.gain_latent[...], upstream)
    r.small[0:1] = along
    r.small[1:2] = plain
    r.grad_latents[...] = r.acc[...] + grad
    r.small[2:4] = jnp.zeros((2, WIDE), f32)

    def x_in(b):
        slot = lax.rem(b, 2)
        return pltpu.make_async_copy(r.inputs.at[rows_at(b * GS, GS)], r.xin.at[slot], x_sem.at[0, slot])

    def x_out(b):
        slot = lax.rem(b, 2)
        return pltpu.make_async_copy(r.xout.at[slot], r.grad_inputs.at[rows_at(b * GS, GS)], x_sem.at[1, slot])

    x_in(jnp.int32(0)).start()

    def input_back(b, _):
        slot = lax.rem(b, 2)

        @pl.when(b + 1 < IN // GS)
        def _():
            x_in(b + 1).start()

        x_in(b).wait()

        @pl.when(b >= 2)
        def _():
            x_out(b - 2).wait()

        span = rows_at(b * GS, GS)
        up = nt(r.dk[span], r.wy[0, 1]) + nt(r.dkr[span], r.wy[1, 1]) + nt(r.dv[span], r.wy[0, 2]) + nt(r.dvr[span], r.wy[1, 2])
        grad, along, plain = norm_back(r.xin[slot].astype(f32), r.gain_input[...], up)
        r.small[2:3] += along
        r.small[3:4] += plain
        r.xout[slot] = grad
        x_out(b).start()
        return 0

    lax.fori_loop(0, IN // GS, input_back, 0)
    r.small[8:9] = jnp.sum(r.cot[...].astype(f32), axis=0, keepdims=True)
    r.small[13:16] = jnp.zeros((3, WIDE), f32)
    for i in range(4):
        half, odd = i // 2, i % 2 * 2
        mine = jnp.concatenate([r.bsum[odd:odd + 1], r.bsum[odd + 1:odd + 2]], axis=1)
        other = jnp.concatenate([r.bsum[odd + 4:odd + 5], r.bsum[odd + 5:odd + 6]], axis=1)
        r.small[9 + i:10 + i] = jnp.where(core == half, mine, other)
    x_out(jnp.int32(IN // GS - 2)).wait()
    x_out(jnp.int32(IN // GS - 1)).wait()
    for copy in staged[-2:]:
        copy.wait()
    for copy in (push_dh, push_c, push_y, push_c2, *push_x):
        copy.wait_send()


def backward(*args):
    return pl.pallas_call(
        backward_kernel,
        out_shape=[jax.ShapeDtypeStruct(shape, dtype) for _, shape, dtype, _ in BWD_OUT],
        in_specs=[spec for _, spec in BWD_IN],
        out_specs=[spec for _, _, _, spec in BWD_OUT],
        scratch_shapes=[pltpu.VMEM(shape, dtype) for _, shape, dtype in BWD_SCRATCH]
        + [pltpu.SemaphoreType.DMA((16,)), pltpu.SemaphoreType.DMA((16,)), pltpu.SemaphoreType.DMA((48,)),
           pltpu.SemaphoreType.DMA((2,)), pltpu.SemaphoreType.DMA((3, 2)), pltpu.SemaphoreType.DMA((2, 2))],
        compiler_params=pltpu.CompilerParams(collective_id=2, has_side_effects=True, vmem_limit_bytes=63 << 20),
    )(*args)

def fold(matrix):
    rows, width = matrix.shape
    if width < WIDE:
        return jnp.concatenate(jnp.split(matrix, WIDE // width, axis=0), axis=1)
    return jnp.concatenate(jnp.split(matrix, width // WIDE, axis=1), axis=0)


def unfold(block):
    height = block.shape[0]
    if height < WIDE:
        return jnp.concatenate(jnp.split(block, WIDE // height, axis=1), axis=0).astype(f32)
    return jnp.concatenate(jnp.split(block, height // WIDE, axis=0), axis=1).astype(f32)


def local(
    latents, inputs, valid_counts, cotangent,
    gain_latent, shift_latent, gain_input, shift_input,
    cross_query, cross_key, cross_value, cross_out,
    gain_self, shift_self,
    self_query, self_key, self_value, self_out,
    gain_mlp, shift_mlp,
    mlp_in, mlp_in_bias, mlp_out, mlp_out_bias,
):
    core = lax.axis_index("mp")

    def row(vector):
        return vector.reshape(1, -1)

    weights = (cross_query, cross_key, cross_value, cross_out, self_query, self_key, self_value, self_out)
    result, *kept = forward(
        latents, inputs, valid_counts, cotangent,
        row(gain_latent), row(shift_latent), row(gain_input), row(shift_input),
        row(gain_self), row(shift_self), row(gain_mlp), row(shift_mlp),
        *weights, mlp_in, mlp_in_bias.reshape(4, HALFW), mlp_out, row(mlp_out_bias))
    packed, small, grad_latents, grad_inputs = backward(
        latents, inputs, valid_counts, cotangent,
        row(gain_latent), row(gain_input), row(gain_self), row(gain_mlp),
        *weights, mlp_in, mlp_out, *kept)
    if lax.axis_size("dp") == 16:
        packed, small = reduce_all(packed, small)
    else:
        packed, small = lax.psum(packed, "dp"), lax.psum(small, ("dp", "mp"))

    def block(start, size):
        return lax.slice_in_dim(packed, start, start + size)

    grad_self = [unfold(block(ROW_SQ + i * HALFW, HALFW)) for i in range(3)]
    grad_cross = [unfold(block(ROW_CQ + i * HALFW, HALFW)) for i in range(3)]
    half = mlp_in_bias.shape[0]
    return (
        result,
        grad_latents,
        grad_inputs,
        *(small[i] for i in range(4)),
        *grad_cross,
        block(ROW_CO, HALFW).astype(f32),
        small[4],
        small[5],
        *grad_self,
        block(ROW_SO, HALFW).astype(f32),
        small[6],
        small[7],
        unfold(block(ROW_MI, 2048)),
        lax.dynamic_slice_in_dim(small[9:13].reshape(-1), core * half, half),
        block(ROW_MO, 2048).astype(f32),
        small[8],
    )


def solution(mesh):
    return jax.shard_map(
        local,
        mesh=mesh,
        in_specs=(
            P(("dp", "mp"), None),
            P(("dp", "mp"), None),
            P("dp"),
            P(("dp", "mp"), None),
            P(),
            P(),
            P(),
            P(),
            P(None, "mp"),
            P(None, "mp"),
            P(None, "mp"),
            P("mp", None),
            P(),
            P(),
            P(None, "mp"),
            P(None, "mp"),
            P(None, "mp"),
            P("mp", None),
            P(),
            P(),
            P(None, "mp"),
            P("mp"),
            P("mp", None),
            P(),
        ),
        out_specs=(
            P(("dp", "mp"), None),
            P(("dp", "mp"), None),
            P(("dp", "mp"), None),
            P(),
            P(),
            P(),
            P(),
            P(None, "mp"),
            P(None, "mp"),
            P(None, "mp"),
            P("mp", None),
            P(),
            P(),
            P(None, "mp"),
            P(None, "mp"),
            P(None, "mp"),
            P("mp", None),
            P(),
            P(),
            P(None, "mp"),
            P("mp"),
            P("mp", None),
            P(),
        ),
        check_vma=False,
    )
```

```python
import functools
import math

import jax
import jax.numpy as jnp
from jax import lax
from jax.experimental import pallas as pl
from jax.experimental.pallas import tpu as pltpu
from jax.sharding import PartitionSpec as P

MESH = pl.DeviceIdType.MESH
NS = 16
CH = 256
HALF = CH // 2
PIECE = HALF // 4
SUB = PIECE // 2
SMALL = 16
PARTS = (
    (("a", -2), ("b", 0), ("f", 2), ("j", 4)),
    (("d", 1), ("h", 3), ("c", 0)),
    (("g", 2), ("e", 1), ("i", 3), ("k", 6)),
)
BEHIND = 6
OWN = 3
HELD = 6
PAIRS = 16
REDUCE_SCRATCH = (
    ("own", (2 * OWN, HALF, 1024)), ("xr", (2 * HELD, HALF, 1024)), ("ur", (2 * HELD, HALF, 1024)), ("dr", (2 * HELD, HALF, 1024)),
    ("fb", (2 * HELD, PIECE, 1024)), ("yr", (2 * HELD, SUB, 1024)),
)


def reducer(r, send, recv, loc):
    g_ref, out_ref, own, xr, ur, dr, fb, yr = r.grads, r.summed, r.own, r.xr, r.ur, r.dr, r.fb, r.yr
    dp = lax.axis_index("dp")
    core = lax.axis_index("mp")
    z = dp // 4
    px = lax.rem(dp, 2)
    py = lax.rem(dp // 2, 2)
    x_dev = (dp + 1 - 2 * px, core)
    y_dev = (dp + 2 - 4 * py, core)
    c_dev = (dp, 1 - core)
    up_dev = (dp + 4, core)
    down_dev = (dp - 4, core)
    z1_dev = (dp + 4 - 8 * lax.rem(z, 2), core)
    z2_dev = (dp + 8 - 16 * (z // 2), core)
    has_up = z < 3
    has_down = z > 0

    barrier = pltpu.get_barrier_semaphore()
    for dev in (x_dev, y_dev, c_dev, z2_dev):
        pl.semaphore_signal(barrier, inc=1, device_id=dev, device_id_type=MESH)

    @pl.when(has_up)
    def _():
        pl.semaphore_signal(barrier, inc=1, device_id=up_dev, device_id_type=MESH)

    @pl.when(has_down)
    def _():
        pl.semaphore_signal(barrier, inc=1, device_id=down_dev, device_id_type=MESH)

    pl.semaphore_wait(barrier, 4 + has_up.astype(jnp.int32) + has_down.astype(jnp.int32))

    def remote(src, dst, kind, p, s, dev):
        slot = lax.rem(p, NS)
        return pltpu.make_async_remote_copy(
            src_ref=src, dst_ref=dst, send_sem=send.at[kind, s, slot], recv_sem=recv.at[kind, s, slot],
            device_id=dev, device_id_type=MESH)

    a_pos = (px, py)
    b_pos = (py, px)
    a_dev = (x_dev, y_dev)
    b_dev = (y_dev, x_dev)

    def base(p, s):
        return (2 * p + s) * CH

    def first(p, s):
        c = lax.rem(p, HELD) * 2 + s
        return remote(g_ref.at[pl.ds(base(p, s) + (1 - a_pos[s]) * HALF, HALF)], xr.at[c], 0, p, s, a_dev[s])

    def mine(p, s):
        c = lax.rem(p, OWN) * 2 + s
        return pltpu.make_async_copy(g_ref.at[pl.ds(base(p, s) + a_pos[s] * HALF, HALF)], own.at[c], loc.at[0, s, lax.rem(p, NS)])

    def up(p, s, lo):
        c = lax.rem(p, HELD) * 2 + s
        src = xr if lo == 1 else ur
        return remote(src.at[c, pl.ds(lo * PIECE, (4 - lo) * PIECE)], ur.at[c, pl.ds(lo * PIECE, (4 - lo) * PIECE)], 1, p, s, up_dev)

    def down(p, s, hi):
        c = lax.rem(p, HELD) * 2 + s
        src = xr if hi == 3 else dr
        return remote(src.at[c, pl.ds(0, hi * PIECE)], dr.at[c, pl.ds(0, hi * PIECE)], 2, p, s, down_dev)

    def last(p, s):
        c = lax.rem(p, HELD) * 2 + s
        return remote(fb.at[c, pl.ds((1 - b_pos[s]) * SUB, SUB)], yr.at[c], 3, p, s, b_dev[s])

    def sub_rows(p, s):
        return pl.ds(base(p, s) + a_pos[s] * HALF + z * PIECE + b_pos[s] * SUB, SUB)

    def last_back(p, s):
        c = lax.rem(p, HELD) * 2 + s
        return remote(fb.at[c, pl.ds(b_pos[s] * SUB, SUB)], out_ref.at[sub_rows(p, s)], 4, p, s, b_dev[s])

    def keep(p, s):
        c = lax.rem(p, HELD) * 2 + s
        return pltpu.make_async_copy(fb.at[c, pl.ds(b_pos[s] * SUB, SUB)], out_ref.at[sub_rows(p, s)], loc.at[1, s, lax.rem(p, NS)])

    def piece_of(p, s, k):
        return out_ref.at[pl.ds(base(p, s) + a_pos[s] * HALF + k * PIECE, PIECE)]

    def up_back(p, s, hop):
        k = jnp.maximum(z - hop, 0)
        return remote(piece_of(p, s, k), piece_of(p, s, k), 5 + hop, p, s, up_dev)

    def down_back(p, s, hop):
        k = jnp.minimum(z + hop, 3)
        return remote(piece_of(p, s, k), piece_of(p, s, k), 8 + hop, p, s, down_dev)

    def first_back(p, s):
        rows = out_ref.at[pl.ds(base(p, s) + a_pos[s] * HALF, HALF)]
        return remote(rows, rows, 11, p, s, a_dev[s])

    def add(*terms):
        total = terms[0].astype(jnp.float32)
        for term in terms[1:]:
            total = total + term.astype(jnp.float32)
        return total.astype(jnp.bfloat16)

    def step_a(p):
        for s in range(2):
            first(p, s).start()
            mine(p, s).start()

    def step_b(p):
        for s in range(2):
            c = lax.rem(p, HELD) * 2 + s
            first(p, s).wait_recv()
            mine(p, s).wait()
            xr[c] = add(own[lax.rem(p, OWN) * 2 + s], xr[c])

            @pl.when(z == 0)
            def _():
                up(p, s, 1).start()

            @pl.when(z == 3)
            def _():
                down(p, s, 3).start()

    def step_c(p):
        for s in range(2):
            c = lax.rem(p, HELD) * 2 + s

            @pl.when(z == 1)
            def _():
                up(p, s, 1).wait_recv()
                ur[c, 2 * PIECE:] = add(ur[c, 2 * PIECE:], xr[c, 2 * PIECE:])
                up(p, s, 2).start()

            @pl.when(z == 2)
            def _():
                down(p, s, 3).wait_recv()
                dr[c, : 2 * PIECE] = add(dr[c, : 2 * PIECE], xr[c, : 2 * PIECE])
                down(p, s, 2).start()

    def step_d(p):
        for s in range(2):
            c = lax.rem(p, HELD) * 2 + s

            @pl.when(z == 2)
            def _():
                up(p, s, 2).wait_recv()
                ur[c, 3 * PIECE:] = add(ur[c, 3 * PIECE:], xr[c, 3 * PIECE:])
                up(p, s, 3).start()

            @pl.when(z == 1)
            def _():
                down(p, s, 2).wait_recv()
                dr[c, :PIECE] = add(dr[c, :PIECE], xr[c, :PIECE])
                down(p, s, 1).start()

    def step_e(p):
        for s in range(2):
            c = lax.rem(p, HELD) * 2 + s

            @pl.when(z == 0)
            def _():
                down(p, s, 1).wait_recv()
                fb[c] = add(xr[c, :PIECE], dr[c, :PIECE])

            @pl.when(z == 1)
            def _():
                fb[c] = add(xr[c, PIECE: 2 * PIECE], ur[c, PIECE: 2 * PIECE], dr[c, PIECE: 2 * PIECE])

            @pl.when(z == 2)
            def _():
                fb[c] = add(xr[c, 2 * PIECE: 3 * PIECE], ur[c, 2 * PIECE: 3 * PIECE], dr[c, 2 * PIECE: 3 * PIECE])

            @pl.when(z == 3)
            def _():
                up(p, s, 3).wait_recv()
                fb[c] = add(xr[c, 3 * PIECE:], ur[c, 3 * PIECE:])

            last(p, s).start()

    def step_f(p):
        for s in range(2):
            for k in range(3):
                @pl.when(z == k)
                def _():
                    up(p, s, k + 1).wait_send()

                @pl.when(z == k + 1)
                def _():
                    down(p, s, k + 1).wait_send()

            c = lax.rem(p, HELD) * 2 + s
            last(p, s).wait_recv()
            rows = pl.ds(pl.multiple_of(b_pos[s] * SUB, SUB), SUB)
            fb[c, rows] = add(fb[c, rows], yr[c])
            last_back(p, s).start()
            keep(p, s).start()

    def step_g(p):
        for s in range(2):
            last_back(p, s).wait_recv()
            keep(p, s).wait()

            @pl.when(has_up)
            def _():
                up_back(p, s, 0).start()

            @pl.when(has_down)
            def _():
                down_back(p, s, 0).start()

    def step_h(p):
        for s in range(2):
            @pl.when(has_down)
            def _():
                up_back(p, s, 0).wait_recv()

            @pl.when(has_down & has_up)
            def _():
                up_back(p, s, 1).start()

            @pl.when(has_up)
            def _():
                down_back(p, s, 0).wait_recv()

            @pl.when(has_down & has_up)
            def _():
                down_back(p, s, 1).start()

    def step_i(p):
        for s in range(2):
            @pl.when(z >= 2)
            def _():
                up_back(p, s, 1).wait_recv()

            @pl.when(z == 2)
            def _():
                up_back(p, s, 2).start()

            @pl.when(z <= 1)
            def _():
                down_back(p, s, 1).wait_recv()

            @pl.when(z == 1)
            def _():
                down_back(p, s, 2).start()

    def step_j(p):
        for s in range(2):
            @pl.when(z == 3)
            def _():
                up_back(p, s, 2).wait_recv()

            @pl.when(z == 0)
            def _():
                down_back(p, s, 2).wait_recv()

            first_back(p, s).start()

    def step_k(p):
        for s in range(2):
            first_back(p, s).wait()
            first(p, s).wait_send()
            last(p, s).wait_send()
            last_back(p, s).wait_send()
            @pl.when(has_up)
            def _():
                up_back(p, s, 0).wait_send()

            @pl.when(has_down)
            def _():
                down_back(p, s, 0).wait_send()

            @pl.when(has_up & has_down)
            def _():
                up_back(p, s, 1).wait_send()
                down_back(p, s, 1).wait_send()

            @pl.when(z == 2)
            def _():
                up_back(p, s, 2).wait_send()

            @pl.when(z == 1)
            def _():
                down_back(p, s, 2).wait_send()

    steps = {"a": step_a, "b": step_b, "c": step_c, "d": step_d, "e": step_e, "f": step_f, "g": step_g, "h": step_h,
             "i": step_i, "j": step_j, "k": step_k}

    def part(t, k):
        for name, behind in PARTS[k]:
            p = t - behind
            if isinstance(p, int):
                if 0 <= p < PAIRS:
                    steps[name](jnp.int32(p))
            else:
                pl.when((p >= 0) & (p < PAIRS))(functools.partial(steps[name], p))

    return part, (c_dev, x_dev, y_dev, z1_dev, z2_dev)


HD = 32
GS = 256
IN = 1024
WIDE = 1024
HALFW = 512
NEG = -1e30
EPS = 1e-05
LOG2E = math.log2(math.e)
SCALE = HD ** -0.5
bf16 = jnp.bfloat16
f32 = jnp.float32
ANY = pl.BlockSpec(memory_space=pl.ANY)
VM = pl.BlockSpec(memory_space=pltpu.VMEM)
SM = pl.BlockSpec(memory_space=pltpu.SMEM)


def nn(left, right):
    return jnp.dot(left, right, preferred_element_type=f32)


def nt(left, right):
    return lax.dot_general(left, right, (((1,), (1,)), ((), ())), preferred_element_type=f32)


def lanes(start, size):
    return pl.ds(pl.multiple_of(start, 128), size)


def rows_at(start, size):
    return pl.ds(pl.multiple_of(start, size), size)


def head_block(tile):
    lane = lax.broadcasted_iota(jnp.int32, tile.shape, 1) // HD
    zero = jnp.zeros_like(tile)
    return jnp.concatenate([jnp.where(lane == j, tile, zero) for j in range(4)], axis=0)


def scores_of(keys, query_block, count):
    scores = nt(keys, query_block)
    if count is None:
        return scores
    place = lax.broadcasted_iota(jnp.int32, scores.shape, 0)
    return jnp.where(place < count, scores, NEG)


def attend(queries, keys, values, count):
    values_t = values.T
    scores = scores_of(keys, head_block(queries), count)
    top = jnp.max(scores, axis=0, keepdims=True)
    weights = jnp.exp2((scores - top) * (LOG2E * SCALE))
    total = jnp.sum(weights, axis=0, keepdims=True)
    low = weights.astype(bf16)
    log_total = top * (LOG2E * SCALE) + jnp.log2(total)
    inverse = 1.0 / total
    mixed, logs = [], []
    for j in range(4):
        span = slice(j * GS, (j + 1) * GS)
        mixed.append(nn(values_t[j * HD:(j + 1) * HD], low[:, span]) * inverse[:, span])
        logs.append(log_total[:, span])
    return jnp.concatenate(mixed, axis=0), jnp.concatenate(logs, axis=0)


def attend_back(queries, keys, values, grads, logs, count):
    keys_t = keys.T
    query_block = head_block(queries)
    grad_block = head_block(grads)
    grad_keys = grad_values = None
    grad_queries = []
    for j in range(4):
        own_query = query_block[j * GS:(j + 1) * GS]
        own_grad = grad_block[j * GS:(j + 1) * GS]
        weights = jnp.exp2(scores_of(keys, own_query, count) * (LOG2E * SCALE) - logs[j:j + 1])
        weighted = weights * nt(values, own_grad)
        inner = jnp.sum(weighted, axis=0, keepdims=True)
        grad_scores = (weighted - weights * inner).astype(bf16)
        value_part = nn(weights.astype(bf16), own_grad)
        key_part = nn(grad_scores, own_query)
        grad_values = value_part if j == 0 else grad_values + value_part
        grad_keys = key_part if j == 0 else grad_keys + key_part
        grad_queries.append(nn(keys_t[j * HD:(j + 1) * HD], grad_scores))
    return jnp.concatenate(grad_queries, axis=0) * SCALE, grad_keys * SCALE, grad_values


def centre(stream):
    centered = stream - jnp.mean(stream, axis=1, keepdims=True)
    inverse = lax.rsqrt(jnp.mean(centered * centered, axis=1, keepdims=True) + EPS)
    return centered * inverse, inverse


def normed(stream, gain, shift):
    return (centre(stream)[0] * gain + shift).astype(bf16)


def norm_back(stream, gain, upstream):
    xhat, inverse = centre(stream)
    scaled = upstream * gain
    along = upstream * xhat
    mean_scaled = jnp.mean(scaled, axis=1, keepdims=True)
    mean_along = jnp.mean(scaled * xhat, axis=1, keepdims=True)
    grad = inverse * (scaled - mean_scaled - xhat * mean_along)
    return grad, jnp.sum(along, axis=0, keepdims=True), jnp.sum(upstream, axis=0, keepdims=True)


def meet(partner):
    barrier = pltpu.get_barrier_semaphore()
    pl.semaphore_signal(barrier, inc=1, device_id=partner, device_id_type=MESH)
    pl.semaphore_wait(barrier, 1)


FWD_IN = (
    ("latents", VM), ("inputs", VM), ("counts", SM), ("cot", ANY),
    ("gain_latent", VM), ("shift_latent", VM), ("gain_input", VM), ("shift_input", VM),
    ("gain_self", VM), ("shift_self", VM), ("gain_mlp", VM), ("shift_mlp", VM),
    ("cq", ANY), ("ck", ANY), ("cv", ANY), ("co", ANY), ("sq", ANY), ("sk", ANY), ("sv", ANY), ("so", ANY),
    ("mi", ANY), ("mib", VM), ("mo", ANY), ("mob", VM),
)
FWD_OUT = (
    ("result", (GS, WIDE), bf16, VM),
    ("s1", (GS, WIDE), f32, VM), ("s2", (GS, WIDE), f32, VM),
    ("lnlT", (WIDE, 2 * GS), bf16, ANY), ("lniT", (WIDE, 2 * IN), bf16, ANY),
    ("snT", (WIDE, 2 * GS), bf16, ANY), ("mnT", (WIDE, 2 * GS), bf16, ANY),
    ("actT", (8, GS, 2 * GS), bf16, ANY), ("dg", (GS, 4096), bf16, ANY),
    ("xq", (GS, WIDE), bf16, ANY), ("xk", (IN, WIDE), bf16, ANY), ("xv", (IN, WIDE), bf16, ANY),
    ("xoT", (HALFW, 2 * GS), bf16, ANY), ("xl", (8, 4, GS), f32, VM),
    ("yq", (GS, WIDE), bf16, ANY), ("yk", (GS, WIDE), bf16, ANY), ("yv", (GS, WIDE), bf16, ANY),
    ("yoT", (HALFW, 2 * GS), bf16, ANY), ("yl", (8, 4, GS), f32, VM),
    ("cotp", (GS, WIDE), bf16, ANY),
    ("rin", (6, WIDE, HALFW), bf16, ANY), ("rout", (2, HALFW, WIDE), bf16, ANY),
    ("rmi", (WIDE, 2048), bf16, ANY), ("rmo", (2048, WIDE), bf16, ANY),
)
FWD_SCRATCH = (
    ("wx", (2, 3, WIDE, HALFW), bf16), ("wxo", (2, HALFW, WIDE), bf16),
    ("wy", (2, 3, WIDE, HALFW), bf16), ("wyo", (2, HALFW, WIDE), bf16),
    ("wmi", (2, WIDE, HALFW), bf16), ("wmo", (2, HALFW, WIDE), bf16),
    ("rbias", (4, HALFW), f32),
    ("n", (GS, WIDE), bf16), ("ln", (IN, WIDE), bf16),
    ("t_l", (WIDE, GS), bf16), ("t_i", (WIDE, IN), bf16), ("t_s", (WIDE, GS), bf16), ("t_m", (WIDE, GS), bf16),
    ("q", (GS, WIDE), bf16), ("k", (IN, WIDE), bf16), ("v", (IN, WIDE), bf16), ("o", (GS, WIDE), bf16), ("oT", (WIDE, GS), bf16),
    ("q2", (GS, WIDE), bf16), ("k2", (GS, WIDE), bf16), ("v2", (GS, WIDE), bf16), ("o2", (GS, WIDE), bf16), ("oT2", (WIDE, GS), bf16),
    ("aT", (8, 2, GS, GS), bf16), ("dgs", (8, GS, HALFW), bf16), ("acc", (GS, WIDE), f32),
)


class Names:
    pass


def named(refs, *tables):
    out = Names()
    place = 0
    for table in tables:
        for entry in table:
            setattr(out, entry[0], refs[place])
            place += 1
    out.rest = refs[place:]
    return out


def forward_kernel(*refs):
    r = named(refs, FWD_IN, FWD_OUT, FWD_SCRATCH)
    send, recv, local = r.rest
    core = lax.axis_index("mp")
    partner = (lax.axis_index("dp"), 1 - core)
    meet(partner)
    sent, kept = [], []

    def push(src, dst):
        i = len(sent)
        copy = pltpu.make_async_remote_copy(
            src_ref=src, dst_ref=dst, send_sem=send.at[i], recv_sem=recv.at[i], device_id=partner, device_id_type=MESH)
        copy.start()
        sent.append(copy)
        return copy

    def fetch(src, dst):
        i = len(kept)
        copy = pltpu.make_async_copy(src, dst, local.at[i])
        copy.start()
        kept.append([copy, False])
        return i

    def ready(i):
        kept[i][0].wait()
        kept[i][1] = True

    got = [push(r.ck, r.rin.at[1]), push(r.cv, r.rin.at[2]), push(r.cq, r.rin.at[0]), push(r.co, r.rout.at[0])]
    got.append(push(r.mib, r.rbias))
    near = [fetch(w, r.wx.at[0, i]) for i, w in ((1, r.ck), (2, r.cv), (0, r.cq))] + [fetch(r.co, r.wxo.at[0])]

    r.n[...] = normed(r.latents[...].astype(f32), r.gain_latent[...], r.shift_latent[...])
    r.t_l[...] = r.n[...].T
    fetch(r.t_l, r.lnlT.at[:, pl.ds(0, GS)])
    gain, shift = r.gain_input[...], r.shift_input[...]

    def input_norm(b, _):
        span = rows_at(b * GS, GS)
        block = normed(r.inputs[span].astype(f32), gain, shift)
        r.ln[span] = block
        r.t_i[:, lanes(b * GS, GS)] = block.T
        return 0

    lax.fori_loop(0, IN // GS, input_norm, 0)
    fetch(r.t_i, r.lniT.at[:, pl.ds(0, IN)])
    for i in near[:3]:
        ready(i)

    def project_inputs(half):
        def block(b, _):
            span = rows_at(b * GS, GS)
            rows = r.ln[span]
            r.k[span, half * HALFW:(half + 1) * HALFW] = nn(rows, r.wx[half, 1]).astype(bf16)
            r.v[span, half * HALFW:(half + 1) * HALFW] = nn(rows, r.wx[half, 2]).astype(bf16)
            return 0

        lax.fori_loop(0, IN // GS, block, 0)
        r.q[:, half * HALFW:(half + 1) * HALFW] = nn(r.n[...], r.wx[half, 0]).astype(bf16)

    project_inputs(0)
    got += [push(w, r.rin.at[i]) for i, w in ((3, r.sq), (4, r.sk), (5, r.sv))] + [push(r.so, r.rout.at[1])]
    far = []
    for copy, src, dst in (
        (got[0], r.rin.at[1], r.wx.at[1, 1]), (got[1], r.rin.at[2], r.wx.at[1, 2]),
        (got[2], r.rin.at[0], r.wx.at[1, 0]), (got[3], r.rout.at[0], r.wxo.at[1])):
        copy.wait_recv()
        far.append(fetch(src, dst))
    near2 = [fetch(w, r.wy.at[0, i]) for i, w in enumerate((r.sq, r.sk, r.sv))] + [fetch(r.so, r.wyo.at[0])]
    count = r.counts[core]

    def attention(queries, keys, values, mixed, mixed_t, logs, limit, first):
        def group(g, _):
            at = lanes(g * 128, 128)
            out_t, log_total = attend(queries[:, at], keys[:, at], values[:, at], limit)
            out_t = out_t.astype(bf16)
            mixed_t[rows_at(g * 128, 128)] = out_t
            mixed[:, at] = out_t.T
            logs[g] = log_total
            return 0

        lax.fori_loop(first, first + 4, group, 0)

    attention(r.q, r.k, r.v, r.o, r.oT, r.xl, count, 0)
    got.append(push(r.mi, r.rmi))
    got.append(push(r.mo, r.rmo))
    for i in far[:3]:
        ready(i)
    project_inputs(1)
    fetch(r.q, r.xq)
    fetch(r.k, r.xk)
    fetch(r.v, r.xv)
    attention(r.q, r.k, r.v, r.o, r.oT, r.xl, count, 4)
    fetch(r.oT.at[pl.ds(0, HALFW)], r.xoT.at[:, pl.ds(0, GS)])
    push(r.oT.at[pl.ds(HALFW, HALFW)], r.xoT.at[:, pl.ds(GS, GS)])
    push(r.t_l, r.lnlT.at[:, pl.ds(GS, GS)])
    push(r.t_i, r.lniT.at[:, pl.ds(IN, IN)])
    push(r.cot, r.cotp)
    ready(near[3])
    ready(far[3])

    def out_project(mixed, weight):
        return nn(mixed[:, :HALFW], weight[0]) + nn(mixed[:, HALFW:], weight[1])

    r.s1[...] = r.latents[...].astype(f32) + out_project(r.o, r.wxo)
    r.n[...] = normed(r.s1[...], r.gain_self[...], r.shift_self[...])
    far2 = []
    for copy, src, dst in (
        (got[5], r.rin.at[3], r.wy.at[1, 0]), (got[6], r.rin.at[4], r.wy.at[1, 1]),
        (got[7], r.rin.at[5], r.wy.at[1, 2]), (got[8], r.rout.at[1], r.wyo.at[1])):
        copy.wait_recv()
        far2.append(fetch(src, dst))
    r.t_s[...] = r.n[...].T
    fetch(r.t_s, r.snT.at[:, pl.ds(0, GS)])
    push(r.t_s, r.snT.at[:, pl.ds(GS, GS)])
    for i in near2 + far2:
        ready(i)
    for half in range(2):
        at = slice(half * HALFW, (half + 1) * HALFW)
        for i, dst in enumerate((r.q2, r.k2, r.v2)):
            dst[:, at] = nn(r.n[...], r.wy[half, i]).astype(bf16)
    fetch(r.q2, r.yq)
    fetch(r.k2, r.yk)
    fetch(r.v2, r.yv)
    attention(r.q2, r.k2, r.v2, r.o2, r.oT2, r.yl, None, 0)
    attention(r.q2, r.k2, r.v2, r.o2, r.oT2, r.yl, None, 4)
    fetch(r.oT2.at[pl.ds(0, HALFW)], r.yoT.at[:, pl.ds(0, GS)])
    push(r.oT2.at[pl.ds(HALFW, HALFW)], r.yoT.at[:, pl.ds(GS, GS)])

    chunk_sem = len(kept)

    def chunk_copies(src_in, src_out, c, slot):
        at = lanes(c * HALFW, HALFW)
        return (
            pltpu.make_async_copy(src_in.at[:, at], r.wmi.at[slot], local.at[chunk_sem + slot]),
            pltpu.make_async_copy(src_out.at[rows_at(c * HALFW, HALFW)], r.wmo.at[slot], local.at[chunk_sem + 2 + slot]),
        )

    def start_chunk(n):
        slot = lax.rem(n, 2)

        @pl.when(n < 4)
        def _():
            for copy in chunk_copies(r.mi, r.mo, n, slot):
                copy.start()

        @pl.when(n >= 4)
        def _():
            for copy in chunk_copies(r.rmi, r.rmo, n - 4, slot):
                copy.start()

    start_chunk(jnp.int32(0))
    r.s2[...] = r.s1[...] + out_project(r.o2, r.wyo)
    r.n[...] = normed(r.s2[...], r.gain_mlp[...], r.shift_mlp[...])
    r.t_m[...] = r.n[...].T
    kept += [None] * 4
    fetch(r.t_m, r.mnT.at[:, pl.ds(0, GS)])
    push(r.t_m, r.mnT.at[:, pl.ds(GS, GS)])
    r.acc[...] = jnp.zeros((GS, WIDE), f32)
    for copy in (got[4], got[9], got[10]):
        copy.wait_recv()

    def feed(n, _):
        slot = lax.rem(n, 2)

        @pl.when(n + 1 < 8)
        def _():
            start_chunk(n + 1)

        for copy in chunk_copies(r.mi, r.mo, 0, slot):
            copy.wait()
        bias = jnp.where(n < 4, r.mib[pl.ds(lax.rem(n, 4), 1)], r.rbias[pl.ds(lax.rem(n, 4), 1)])
        hidden = nn(r.n[...], r.wmi[slot]) + bias
        area = 0.5 + 0.5 * lax.erf(hidden * (0.5 ** 0.5))
        density = jnp.exp(-0.5 * hidden * hidden) * ((2 * math.pi) ** -0.5)
        act = (hidden * area).astype(bf16)
        r.dgs[n] = (area + hidden * density).astype(bf16)
        r.aT[n] = act.T.reshape(2, GS, GS)
        r.acc[...] += nn(act, r.wmo[slot])
        return 0

    lax.fori_loop(0, 8, feed, 0)
    for c in range(4):
        fetch(r.aT.at[c], r.actT.at[pl.ds(2 * c, 2), :, pl.ds(0, GS)])
        push(r.aT.at[4 + c], r.actT.at[pl.ds(2 * c, 2), :, pl.ds(GS, GS)])
    for c in range(8):
        fetch(r.dgs.at[c], r.dg.at[:, pl.ds(c * HALFW, HALFW)])
    r.result[...] = (r.s2[...] + (r.acc[...] + r.mob[...])).astype(bf16)
    for i, entry in enumerate(kept):
        if entry is not None and not entry[1]:
            ready(i)
    seen = [id(c) for c in got]
    for copy in sent:
        copy.wait_send()
        if id(copy) not in seen:
            copy.wait_recv()


def forward(*args):
    return pl.pallas_call(
        forward_kernel,
        out_shape=[jax.ShapeDtypeStruct(shape, dtype) for _, shape, dtype, _ in FWD_OUT],
        in_specs=[spec for _, spec in FWD_IN],
        out_specs=[spec for _, _, _, spec in FWD_OUT],
        scratch_shapes=[pltpu.VMEM(shape, dtype) for _, shape, dtype in FWD_SCRATCH]
        + [pltpu.SemaphoreType.DMA((24,)), pltpu.SemaphoreType.DMA((24,)), pltpu.SemaphoreType.DMA((64,))],
        compiler_params=pltpu.CompilerParams(collective_id=1, has_side_effects=True, vmem_limit_bytes=60 << 20),
    )(*args)


BWD_IN = (
    ("latents", VM), ("inputs", ANY), ("counts", SM), ("cot", VM),
    ("gain_latent", VM), ("gain_input", VM), ("gain_self", VM), ("gain_mlp", VM),
    ("cq", ANY), ("ck", ANY), ("cv", ANY), ("co", ANY), ("sq", ANY), ("sk", ANY), ("sv", ANY), ("so", ANY),
    ("mi", ANY), ("mo", ANY),
) + tuple((name, VM if name in ("xl", "yl") else ANY) for name, _, _, _ in FWD_OUT[1:])
ROWS_OUT = 8192
BWD_OUT = (
    ("grads", (ROWS_OUT, WIDE), bf16, ANY), ("summed", (ROWS_OUT, WIDE), bf16, ANY), ("small", (SMALL, WIDE), f32, VM),
    ("grad_latents", (GS, WIDE), f32, VM), ("grad_inputs", (IN, WIDE), f32, ANY),
)
BWD_SCRATCH = (
    ("wy", (2, 3, WIDE, HALFW), bf16), ("wyo", (2, HALFW, WIDE), bf16), ("wxo", (2, HALFW, WIDE), bf16),
    ("wmi", (2, WIDE, HALFW), bf16), ("wmo", (2, HALFW, WIDE), bf16),
    ("mc", (2 * GS, WIDE), bf16), ("sc", (2 * GS, WIDE), bf16),
    ("dk", (8, GS, HALFW), bf16), ("dgs", (2, GS, HALFW), bf16),
    ("mT", (WIDE, 2 * GS), bf16), ("big", (4, HALFW, HALFW), bf16), ("bigr", (4, GS, HALFW), bf16),
    ("sT", (WIDE, 2 * GS), bf16), ("kv", (2, IN, WIDE), bf16),
    ("q", (GS, WIDE), bf16), ("oT", (HALFW, 2 * GS), bf16),
    ("q2", (GS, WIDE), bf16), ("k2", (GS, WIDE), bf16), ("v2", (GS, WIDE), bf16), ("oT2", (HALFW, 2 * GS), bf16),
    ("g", (GS, WIDE), bf16),
    ("dq", (2 * GS, HALFW), bf16), ("dqr", (GS, HALFW), bf16), ("dvr", (2, HALFW, HALFW), bf16),
    ("dq2", (3, 2 * GS, HALFW), bf16), ("dqr2", (3, GS, HALFW), bf16),
    ("xin", (2, GS, WIDE), bf16), ("wide", (2, GS, WIDE), f32),
    ("stage", (2, HALFW, WIDE), bf16), ("bsum", (8, HALFW), f32), ("sacc", (SMALL, WIDE), f32), ("sbuf", (5, SMALL, WIDE), f32),
)
ROW_MO, ROW_MI, ROW_SO, ROW_SQ, ROW_CO, ROW_CQ = 0, 2048, 4096, 4608, 6144, 6656


def backward_kernel(reduce, *refs):
    r = named(refs, BWD_IN, BWD_OUT, BWD_SCRATCH, REDUCE_SCRATCH if reduce else ())
    send, recv, local, stage_sem, chunk_sem, x_sem, *reduce_sems = r.rest
    core = lax.axis_index("mp")
    partner = (lax.axis_index("dp"), 1 - core)
    if reduce:
        part, small_devs = reducer(r, *reduce_sems[:3])
    else:
        meet(partner)
    sent, kept, staged = [], [], []
    state = {"tick": 0, "settled": 0}

    def settle():
        for copy in staged[state["settled"]:]:
            copy.wait()
        state["settled"] = len(staged)

    def may_take(first, last):
        for n in range(first, last):
            if n % 3 == 0:
                assert min(n // 3 + 3, PAIRS) <= state["settled"]

    def tick(count=1):
        for _ in range(count):
            n = state["tick"]
            state["tick"] = n + 1
            if reduce:
                may_take(n, n + 1)
                part(n // 3, n % 3)

    def loop_tick(n):
        if reduce:
            for k in range(3):
                pl.when(lax.rem(n, 3) == k)(functools.partial(part, n // 3, k))

    def loop_ticks(count):
        n = state["tick"]
        state["tick"] = n + count
        if reduce:
            may_take(n, n + count)
        return n

    def push(src, dst):
        i = len(sent)
        copy = pltpu.make_async_remote_copy(
            src_ref=src, dst_ref=dst, send_sem=send.at[i], recv_sem=recv.at[i], device_id=partner, device_id_type=MESH)
        copy.start()
        sent.append(copy)
        return copy

    def fetch(src, dst):
        copy = pltpu.make_async_copy(src, dst, local.at[len(kept)])
        copy.start()
        kept.append(copy)
        return copy

    def stage(write, row):
        i = len(staged)
        slot = i % 2
        if i >= 2 and state["settled"] <= i - 2:
            staged[i - 2].wait()
            state["settled"] = i - 1
        write(r.stage.at[slot])
        copy = pltpu.make_async_copy(r.stage.at[slot], r.grads.at[pl.ds(row, HALFW)], stage_sem.at[slot])
        copy.start()
        staged.append(copy)

    early = [fetch(r.actT, r.dk), fetch(r.cotp, r.mc.at[pl.ds(GS, GS)])]

    def chunk_copies(src_in, src_out, c, n, slot):
        at = lanes(c * HALFW, HALFW)
        return (
            pltpu.make_async_copy(src_in.at[:, at], r.wmi.at[slot], chunk_sem.at[0, slot]),
            pltpu.make_async_copy(src_out.at[rows_at(c * HALFW, HALFW)], r.wmo.at[slot], chunk_sem.at[1, slot]),
            pltpu.make_async_copy(r.dg.at[:, lanes(n * HALFW, HALFW)], r.dgs.at[slot], chunk_sem.at[2, slot]),
        )

    def start_chunk(i):
        slot = lax.rem(i, 2)

        @pl.when(i < 4)
        def _():
            for copy in chunk_copies(r.rmi, r.rmo, i, 4 + i, slot):
                copy.start()

        @pl.when(i >= 4)
        def _():
            for copy in chunk_copies(r.mi, r.mo, i - 4, i - 4, slot):
                copy.start()

    start_chunk(jnp.int32(0))
    load_m = [fetch(r.mnT, r.mT), fetch(r.s2, r.wide.at[1])]
    load_y = [fetch(w, r.wy.at[0, i]) for i, w in enumerate((r.sq, r.sk, r.sv))]
    load_y += [fetch(r.rin.at[pl.ds(3, 3)], r.wy.at[1]), fetch(r.so, r.wyo.at[0]), fetch(r.rout.at[1], r.wyo.at[1])]
    load_y += [fetch(a, b) for a, b in ((r.yq, r.q2), (r.yk, r.k2), (r.yv, r.v2), (r.yoT, r.oT2), (r.snT, r.sT))]
    r.mc[pl.ds(0, GS)] = r.cot[...]
    for copy in early:
        copy.wait()
    for m in range(4):
        def write(dst, m=m):
            dst[...] = nn(r.dk[2 * m:2 * m + 2].reshape(HALFW, 2 * GS), r.mc[...]).astype(bf16)

        stage(write, ROW_MO + m * HALFW)
    settle()
    if reduce:
        part(-2, 0)
        part(-1, 0)
    r.wide[0] = jnp.zeros((GS, WIDE), f32)

    def feed(i, _):
        slot = lax.rem(i, 2)

        @pl.when(i + 1 < 8)
        def _():
            start_chunk(i + 1)

        for copy in chunk_copies(r.mi, r.mo, 0, 0, slot):
            copy.wait()
        grad = (nt(r.cot[...], r.wmo[slot]) * r.dgs[slot].astype(f32)).astype(bf16)
        r.bsum[pl.ds(lax.rem(i + 4, 8), 1)] = jnp.sum(grad.astype(f32), axis=0, keepdims=True)

        @pl.when(i < 4)
        def _():
            r.bigr[lax.rem(i, 4)] = grad

        @pl.when(i >= 4)
        def _():
            r.big[lax.rem(i, 4), pl.ds(0, GS)] = grad

        r.wide[0] += nt(grad, r.wmi[slot])
        return 0

    lax.fori_loop(0, 4, feed, 0)
    push_dh = push(r.bigr, r.big.at[:, pl.ds(GS, GS)])
    lax.fori_loop(4, 8, feed, 0)
    load_x = [fetch(r.co, r.wxo.at[0]), fetch(r.rout.at[0], r.wxo.at[1])]
    load_x += [fetch(a, b) for a, b in ((r.xq, r.q), (r.xk, r.kv.at[0]), (r.xv, r.kv.at[1]), (r.xoT, r.oT))]

    for copy in load_m:
        copy.wait()
    grad, along, plain = norm_back(r.wide[1], r.gain_mlp[...], r.wide[0])
    load_s = fetch(r.s1, r.wide.at[1])
    r.small[6:7] = along
    r.small[7:8] = plain
    r.wide[0] = r.cot[...].astype(f32) + grad
    r.sc[pl.ds(0, GS)] = r.wide[0].astype(bf16)
    push_c = push(r.sc.at[pl.ds(0, GS)], r.sc.at[pl.ds(GS, GS)])
    tick(2)
    push_dh.wait_recv()
    for c in range(4):
        def write(dst, c=c):
            dst[...] = jnp.concatenate(
                [nn(r.mT[c % 2 * HALFW:(c % 2 + 1) * HALFW], r.big[c // 2 * 2 + e]).astype(bf16)
                 for e in range(2)], axis=1)

        stage(write, ROW_MI + c * HALFW)
        if c % 2:
            tick()
    settle()
    load_l = fetch(r.lnlT, r.mT)

    def attention_back(queries, keys, values, logs, limit, take, own, other, hand_over, every):
        first = loop_ticks(8 // every)

        def group(i, _):
            g = lax.rem(i + 4, 8)
            at = lanes(g * 128, 128)
            to = lanes(lax.rem(i, 4) * 128, 128)
            pl.when(i == 4)(hand_over)
            grad_q, grad_k, grad_v = attend_back(queries[:, at], keys[:, at], values[:, at], r.g[:, at], logs[g], limit)
            grad_q, grad_k, grad_v = grad_q.astype(bf16).T, grad_k.astype(bf16), grad_v.astype(bf16)
            pl.when(i < 4)(lambda: take(other, to, grad_q, grad_k, grad_v))
            pl.when(i >= 4)(lambda: take(own, to, grad_q, grad_k, grad_v))
            if every == 1:
                loop_tick(first + i)
            else:
                pl.when(lax.rem(i, every) == every - 1)(lambda: loop_tick(first + i // every))
            return 0

        lax.fori_loop(0, 8, group, 0)

    def out_back(cots, weight):
        cot = cots[pl.ds(0, GS)]
        for half in range(2):
            r.g[:, half * HALFW:(half + 1) * HALFW] = nt(cot, weight[half]).astype(bf16)

    def grad_fold(left, right, row):
        def write(dst):
            for e in range(2):
                dst[:, e * HALFW:(e + 1) * HALFW] = nn(left[e * HALFW:(e + 1) * HALFW], right[...]).astype(bf16)

        stage(write, row)

    def crossing(i, src, dst):
        return pltpu.make_async_remote_copy(
            src_ref=src, dst_ref=dst, send_sem=send.at[i], recv_sem=recv.at[i], device_id=partner, device_id_type=MESH)

    push_y = crossing(12, r.dqr2, r.dq2.at[:, pl.ds(GS, GS)])
    push_x = [
        crossing(13, r.dqr, r.dq.at[pl.ds(GS, GS)]), crossing(14, r.bigr, r.dk.at[pl.ds(4, 4)]),
        crossing(15, r.dvr, r.big.at[pl.ds(2, 2)])]

    def take_y(dst, to, grad_q, grad_k, grad_v):
        for i, grad in enumerate((grad_q, grad_k, grad_v)):
            dst[i, pl.ds(0, GS), to] = grad

    def take_x(dst, to, grad_q, grad_k, grad_v):
        dst_q, dst_k, dst_v = dst
        dst_q[pl.ds(0, GS), to] = grad_q
        dst_k[pl.ds(0, 4), :, to] = grad_k.reshape(4, GS, 128)
        dst_v[pl.ds(0, 2), :, to] = grad_v.reshape(2, HALFW, 128)

    for copy in load_y:
        copy.wait()
    out_back(r.sc, r.wyo)
    tick()
    attention_back(r.q2, r.k2, r.v2, r.yl, None, take_y, r.dq2, r.dqr2, push_y.start, 2)
    push_c.wait_recv()

    def write_so(dst):
        dst[...] = nn(r.oT2[...], r.sc[...]).astype(bf16)

    stage(write_so, ROW_SO)
    tick()
    load_s.wait()
    upstream = None
    for i in range(3):
        term = nt(r.dq2[i, :GS], r.wy[0, i]) + nt(r.dqr2[i], r.wy[1, i])
        upstream = term if upstream is None else upstream + term
    grad, along, plain = norm_back(r.wide[1], r.gain_self[...], upstream)
    r.small[4:5] = along
    r.small[5:6] = plain
    r.wide[0] += grad
    load_w = [fetch(w, r.wy.at[0, i]) for i, w in enumerate((r.cq, r.ck, r.cv))] + [fetch(r.rin.at[pl.ds(0, 3)], r.wy.at[1])]
    r.mc[pl.ds(0, GS)] = r.wide[0].astype(bf16)
    push_c2 = push(r.mc.at[pl.ds(0, GS)], r.mc.at[pl.ds(GS, GS)])
    push_y.wait_recv()
    tick()
    for i in range(3):
        grad_fold(r.sT, r.dq2.at[i], ROW_SQ + i * HALFW)
        tick()
    settle()

    for copy in load_x:
        copy.wait()
    out_back(r.mc, r.wxo)
    tick()
    count = r.counts[core]
    push_dh.wait_send()

    def hand_over_x():
        for copy in push_x:
            copy.start()

    attention_back(r.q, r.kv.at[0], r.kv.at[1], r.xl, count, take_x, (r.dq, r.dk, r.big), (r.dqr, r.bigr, r.dvr), hand_over_x, 1)
    load_i = [fetch(r.lniT.at[:, pl.ds(0, IN)], r.kv.at[0]), fetch(r.lniT.at[:, pl.ds(IN, IN)], r.kv.at[1])]
    push_c2.wait_recv()

    def write_co(dst):
        dst[...] = nn(r.oT[...], r.mc[...]).astype(bf16)

    stage(write_co, ROW_CO)
    tick()
    for copy in push_x:
        copy.wait_recv()
    load_l.wait()
    grad_fold(r.mT, r.dq, ROW_CQ)
    tick()
    for copy in load_i:
        copy.wait()

    def tall(blocks):
        return blocks.reshape(IN, HALFW)

    def grad_tall(right, row):
        def write(dst):
            for e in range(2):
                at = slice(e * HALFW, (e + 1) * HALFW)
                dst[:, at] = (nn(r.kv[0, at], tall(right[0])) + nn(r.kv[1, at], tall(right[1]))).astype(bf16)

        stage(write, row)

    grad_tall((r.dk[:4], r.dk[4:]), ROW_CQ + HALFW)
    tick()
    grad_tall((r.big[:2], r.big[2:]), ROW_CQ + 2 * HALFW)
    settle()
    tick()
    for copy in load_w:
        copy.wait()
    upstream = nt(r.dq[:GS], r.wy[0, 0]) + nt(r.dqr[...], r.wy[1, 0])
    grad, along, plain = norm_back(r.latents[...].astype(f32), r.gain_latent[...], upstream)
    r.small[0:1] = along
    r.small[1:2] = plain
    r.grad_latents[...] = r.wide[0] + grad
    r.small[2:4] = jnp.zeros((2, WIDE), f32)

    def x_in(b):
        slot = lax.rem(b, 2)
        return pltpu.make_async_copy(r.inputs.at[rows_at(b * GS, GS)], r.xin.at[slot], x_sem.at[0, slot])

    def x_out(b):
        slot = lax.rem(b, 2)
        return pltpu.make_async_copy(r.wide.at[slot], r.grad_inputs.at[rows_at(b * GS, GS)], x_sem.at[1, slot])

    x_in(jnp.int32(0)).start()

    def input_back(b, _):
        slot = lax.rem(b, 2)

        @pl.when(b + 1 < IN // GS)
        def _():
            x_in(b + 1).start()

        x_in(b).wait()

        @pl.when(b >= 2)
        def _():
            x_out(b - 2).wait()

        half, at = b // 2, rows_at(lax.rem(b, 2) * GS, GS)
        up = nt(r.dk[b], r.wy[0, 1]) + nt(r.bigr[b], r.wy[1, 1]) + nt(r.big[half, at], r.wy[0, 2]) + nt(r.dvr[half, at], r.wy[1, 2])
        grad, along, plain = norm_back(r.xin[slot].astype(f32), r.gain_input[...], up)
        r.small[2:3] += along
        r.small[3:4] += plain
        r.wide[slot] = grad
        x_out(b).start()
        loop_tick(ticks + b)
        return 0

    ticks = loop_ticks(IN // GS)

    lax.fori_loop(0, IN // GS, input_back, 0)
    r.small[8:9] = jnp.sum(r.cot[...].astype(f32), axis=0, keepdims=True)
    r.small[13:16] = jnp.zeros((3, WIDE), f32)
    for i in range(4):
        half, odd = i // 2, i % 2 * 2
        mine = jnp.concatenate([r.bsum[odd:odd + 1], r.bsum[odd + 1:odd + 2]], axis=1)
        other = jnp.concatenate([r.bsum[odd + 4:odd + 5], r.bsum[odd + 5:odd + 6]], axis=1)
        r.small[9 + i:10 + i] = jnp.where(core == half, mine, other)
    x_out(jnp.int32(IN // GS - 2)).wait()
    x_out(jnp.int32(IN // GS - 1)).wait()
    for copy in (push_c, push_y, push_c2, *push_x):
        copy.wait_send()
    if not reduce:
        return
    tick(-state["tick"] % 3)
    begin = state["tick"] // 3
    small_send, small_recv = reduce_sems[3:]

    def small_copy(i):
        return pltpu.make_async_remote_copy(
            src_ref=r.sacc, dst_ref=r.sbuf.at[i], send_sem=small_send.at[i], recv_sem=small_recv.at[i],
            device_id=small_devs[i], device_id_type=MESH)

    r.sacc[...] = r.small[...]
    small_copy(0).start()

    def iteration(t, _):
        for k in range(3):
            part(t, k)
        for i in range(5):
            @pl.when(t == begin + i)
            def _():
                small_copy(i).wait()
                r.sacc[...] += r.sbuf[i]
                if i < 4:
                    small_copy(i + 1).start()
        return 0

    lax.fori_loop(begin, PAIRS + BEHIND, iteration, 0)
    r.small[...] = r.sacc[...]


def backward(reduce, *args):
    scratch = [pltpu.VMEM(shape, dtype) for _, shape, dtype in BWD_SCRATCH]
    sems = [(16,), (16,), (48,), (2,), (3, 2), (2, 2)]
    if reduce:
        scratch += [pltpu.VMEM(shape, bf16) for _, shape in REDUCE_SCRATCH]
        sems += [(12, 2, NS), (12, 2, NS), (2, 2, NS), (5,), (5,)]
    return pl.pallas_call(
        functools.partial(backward_kernel, reduce),
        out_shape=[jax.ShapeDtypeStruct(shape, dtype) for _, shape, dtype, _ in BWD_OUT],
        in_specs=[spec for _, spec in BWD_IN],
        out_specs=[spec for _, _, _, spec in BWD_OUT],
        scratch_shapes=scratch + [pltpu.SemaphoreType.DMA(shape) for shape in sems],
        compiler_params=pltpu.CompilerParams(
            collective_id=0 if reduce else 2, has_side_effects=True, vmem_limit_bytes=63 << 20),
    )(*args)

def fold(matrix):
    rows, width = matrix.shape
    if width < WIDE:
        return jnp.concatenate(jnp.split(matrix, WIDE // width, axis=0), axis=1)
    return jnp.concatenate(jnp.split(matrix, width // WIDE, axis=1), axis=0)


def unfold(block):
    height = block.shape[0]
    if height < WIDE:
        return jnp.concatenate(jnp.split(block, WIDE // height, axis=1), axis=0).astype(f32)
    return jnp.concatenate(jnp.split(block, height // WIDE, axis=0), axis=1).astype(f32)


def local(
    latents, inputs, valid_counts, cotangent,
    gain_latent, shift_latent, gain_input, shift_input,
    cross_query, cross_key, cross_value, cross_out,
    gain_self, shift_self,
    self_query, self_key, self_value, self_out,
    gain_mlp, shift_mlp,
    mlp_in, mlp_in_bias, mlp_out, mlp_out_bias,
):
    core = lax.axis_index("mp")

    def row(vector):
        return vector.reshape(1, -1)

    weights = (cross_query, cross_key, cross_value, cross_out, self_query, self_key, self_value, self_out)
    result, *kept = forward(
        latents, inputs, valid_counts, cotangent,
        row(gain_latent), row(shift_latent), row(gain_input), row(shift_input),
        row(gain_self), row(shift_self), row(gain_mlp), row(shift_mlp),
        *weights, mlp_in, mlp_in_bias.reshape(4, HALFW), mlp_out, row(mlp_out_bias))
    reduce = lax.axis_size("dp") == 16
    grads, packed, small, grad_latents, grad_inputs = backward(
        reduce, latents, inputs, valid_counts, cotangent,
        row(gain_latent), row(gain_input), row(gain_self), row(gain_mlp),
        *weights, mlp_in, mlp_out, *kept)
    if not reduce:
        packed, small = lax.psum(grads, "dp"), lax.psum(small, ("dp", "mp"))

    def block(start, size):
        return lax.slice_in_dim(packed, start, start + size)

    grad_self = [unfold(block(ROW_SQ + i * HALFW, HALFW)) for i in range(3)]
    grad_cross = [unfold(block(ROW_CQ + i * HALFW, HALFW)) for i in range(3)]
    half = mlp_in_bias.shape[0]
    return (
        result,
        grad_latents,
        grad_inputs,
        *(small[i] for i in range(4)),
        *grad_cross,
        block(ROW_CO, HALFW).astype(f32),
        small[4],
        small[5],
        *grad_self,
        block(ROW_SO, HALFW).astype(f32),
        small[6],
        small[7],
        unfold(block(ROW_MI, 2048)),
        lax.dynamic_slice_in_dim(small[9:13].reshape(-1), core * half, half),
        block(ROW_MO, 2048).astype(f32),
        small[8],
    )


def solution(mesh):
    return jax.shard_map(
        local,
        mesh=mesh,
        in_specs=(
            P(("dp", "mp"), None),
            P(("dp", "mp"), None),
            P("dp"),
            P(("dp", "mp"), None),
            P(),
            P(),
            P(),
            P(),
            P(None, "mp"),
            P(None, "mp"),
            P(None, "mp"),
            P("mp", None),
            P(),
            P(),
            P(None, "mp"),
            P(None, "mp"),
            P(None, "mp"),
            P("mp", None),
            P(),
            P(),
            P(None, "mp"),
            P("mp"),
            P("mp", None),
            P(),
        ),
        out_specs=(
            P(("dp", "mp"), None),
            P(("dp", "mp"), None),
            P(("dp", "mp"), None),
            P(),
            P(),
            P(),
            P(),
            P(None, "mp"),
            P(None, "mp"),
            P(None, "mp"),
            P("mp", None),
            P(),
            P(),
            P(None, "mp"),
            P(None, "mp"),
            P(None, "mp"),
            P("mp", None),
            P(),
            P(),
            P(None, "mp"),
            P("mp"),
            P("mp", None),
            P(),
        ),
        check_vma=False,
    )
```

```python
import functools
import math

import jax
import jax.numpy as jnp
from jax import lax
from jax.experimental import pallas as pl
from jax.experimental.pallas import tpu as pltpu
from jax.sharding import PartitionSpec as P

MESH = pl.DeviceIdType.MESH
NS = 16
CH = 256
HALF = CH // 2
PIECE = HALF // 4
SUB = PIECE // 2
SMALL = 16
PARTS = (
    (("a", -2), ("b", 0), ("f", 2), ("j", 4)),
    (("d", 1), ("h", 3), ("c", 0)),
    (("g", 2), ("e", 1), ("i", 3), ("k", 6)),
)
BEHIND = 6
AHEAD = 2
OWN = 3
HELD = 6
PAIRS = 16
REDUCE_SCRATCH = (
    ("own", (2 * OWN, HALF, 1024)), ("xr", (2 * HELD, HALF, 1024)), ("ur", (2 * HELD, HALF, 1024)), ("dr", (2 * HELD, HALF, 1024)),
    ("fb", (2 * HELD, PIECE, 1024)), ("yr", (2 * HELD, SUB, 1024)),
)


def reducer(r, send, recv, loc):
    g_ref, out_ref, own, xr, ur, dr, fb, yr = r.grads, r.summed, r.own, r.xr, r.ur, r.dr, r.fb, r.yr
    dp = lax.axis_index("dp")
    core = lax.axis_index("mp")
    z = dp // 4
    px = lax.rem(dp, 2)
    py = lax.rem(dp // 2, 2)
    x_dev = (dp + 1 - 2 * px, core)
    y_dev = (dp + 2 - 4 * py, core)
    c_dev = (dp, 1 - core)
    up_dev = (dp + 4, core)
    down_dev = (dp - 4, core)
    z1_dev = (dp + 4 - 8 * lax.rem(z, 2), core)
    z2_dev = (dp + 8 - 16 * (z // 2), core)
    has_up = z < 3
    has_down = z > 0

    barrier = pltpu.get_barrier_semaphore()
    for dev in (x_dev, y_dev, c_dev, z2_dev):
        pl.semaphore_signal(barrier, inc=1, device_id=dev, device_id_type=MESH)

    @pl.when(has_up)
    def _():
        pl.semaphore_signal(barrier, inc=1, device_id=up_dev, device_id_type=MESH)

    @pl.when(has_down)
    def _():
        pl.semaphore_signal(barrier, inc=1, device_id=down_dev, device_id_type=MESH)

    pl.semaphore_wait(barrier, 4 + has_up.astype(jnp.int32) + has_down.astype(jnp.int32))

    def remote(src, dst, kind, p, s, dev):
        slot = lax.rem(p, NS)
        return pltpu.make_async_remote_copy(
            src_ref=src, dst_ref=dst, send_sem=send.at[kind, s, slot], recv_sem=recv.at[kind, s, slot],
            device_id=dev, device_id_type=MESH)

    a_pos = (px, py)
    b_pos = (py, px)
    a_dev = (x_dev, y_dev)
    b_dev = (y_dev, x_dev)

    def base(p, s):
        return (2 * p + s) * CH

    def first(p, s):
        c = lax.rem(p, HELD) * 2 + s
        return remote(g_ref.at[pl.ds(base(p, s) + (1 - a_pos[s]) * HALF, HALF)], xr.at[c], 0, p, s, a_dev[s])

    def mine(p, s):
        c = lax.rem(p, OWN) * 2 + s
        return pltpu.make_async_copy(g_ref.at[pl.ds(base(p, s) + a_pos[s] * HALF, HALF)], own.at[c], loc.at[0, s, lax.rem(p, NS)])

    def up(p, s, lo):
        c = lax.rem(p, HELD) * 2 + s
        src = xr if lo == 1 else ur
        return remote(src.at[c, pl.ds(lo * PIECE, (4 - lo) * PIECE)], ur.at[c, pl.ds(lo * PIECE, (4 - lo) * PIECE)], 1, p, s, up_dev)

    def down(p, s, hi):
        c = lax.rem(p, HELD) * 2 + s
        src = xr if hi == 3 else dr
        return remote(src.at[c, pl.ds(0, hi * PIECE)], dr.at[c, pl.ds(0, hi * PIECE)], 2, p, s, down_dev)

    def last(p, s):
        c = lax.rem(p, HELD) * 2 + s
        return remote(fb.at[c, pl.ds((1 - b_pos[s]) * SUB, SUB)], yr.at[c], 3, p, s, b_dev[s])

    def sub_rows(p, s):
        return pl.ds(base(p, s) + a_pos[s] * HALF + z * PIECE + b_pos[s] * SUB, SUB)

    def last_back(p, s):
        c = lax.rem(p, HELD) * 2 + s
        return remote(fb.at[c, pl.ds(b_pos[s] * SUB, SUB)], out_ref.at[sub_rows(p, s)], 4, p, s, b_dev[s])

    def keep(p, s):
        c = lax.rem(p, HELD) * 2 + s
        return pltpu.make_async_copy(fb.at[c, pl.ds(b_pos[s] * SUB, SUB)], out_ref.at[sub_rows(p, s)], loc.at[1, s, lax.rem(p, NS)])

    def piece_of(p, s, k):
        return out_ref.at[pl.ds(base(p, s) + a_pos[s] * HALF + k * PIECE, PIECE)]

    def up_back(p, s, hop):
        k = jnp.maximum(z - hop, 0)
        return remote(piece_of(p, s, k), piece_of(p, s, k), 5 + hop, p, s, up_dev)

    def down_back(p, s, hop):
        k = jnp.minimum(z + hop, 3)
        return remote(piece_of(p, s, k), piece_of(p, s, k), 8 + hop, p, s, down_dev)

    def first_back(p, s):
        rows = out_ref.at[pl.ds(base(p, s) + a_pos[s] * HALF, HALF)]
        return remote(rows, rows, 11, p, s, a_dev[s])

    def add(*terms):
        total = terms[0].astype(jnp.float32)
        for term in terms[1:]:
            total = total + term.astype(jnp.float32)
        return total.astype(jnp.bfloat16)

    def step_a(p):
        for s in range(2):
            first(p, s).start()
            mine(p, s).start()

    def step_b(p):
        for s in range(2):
            c = lax.rem(p, HELD) * 2 + s
            first(p, s).wait_recv()
            mine(p, s).wait()
            xr[c] = add(own[lax.rem(p, OWN) * 2 + s], xr[c])

            @pl.when(z == 0)
            def _():
                up(p, s, 1).start()

            @pl.when(z == 3)
            def _():
                down(p, s, 3).start()

    def step_c(p):
        for s in range(2):
            c = lax.rem(p, HELD) * 2 + s

            @pl.when(z == 1)
            def _():
                up(p, s, 1).wait_recv()
                ur[c, 2 * PIECE:] = add(ur[c, 2 * PIECE:], xr[c, 2 * PIECE:])
                up(p, s, 2).start()

            @pl.when(z == 2)
            def _():
                down(p, s, 3).wait_recv()
                dr[c, : 2 * PIECE] = add(dr[c, : 2 * PIECE], xr[c, : 2 * PIECE])
                down(p, s, 2).start()

    def step_d(p):
        for s in range(2):
            c = lax.rem(p, HELD) * 2 + s

            @pl.when(z == 2)
            def _():
                up(p, s, 2).wait_recv()
                ur[c, 3 * PIECE:] = add(ur[c, 3 * PIECE:], xr[c, 3 * PIECE:])
                up(p, s, 3).start()

            @pl.when(z == 1)
            def _():
                down(p, s, 2).wait_recv()
                dr[c, :PIECE] = add(dr[c, :PIECE], xr[c, :PIECE])
                down(p, s, 1).start()

    def step_e(p):
        for s in range(2):
            c = lax.rem(p, HELD) * 2 + s

            @pl.when(z == 0)
            def _():
                down(p, s, 1).wait_recv()
                fb[c] = add(xr[c, :PIECE], dr[c, :PIECE])

            @pl.when(z == 1)
            def _():
                fb[c] = add(xr[c, PIECE: 2 * PIECE], ur[c, PIECE: 2 * PIECE], dr[c, PIECE: 2 * PIECE])

            @pl.when(z == 2)
            def _():
                fb[c] = add(xr[c, 2 * PIECE: 3 * PIECE], ur[c, 2 * PIECE: 3 * PIECE], dr[c, 2 * PIECE: 3 * PIECE])

            @pl.when(z == 3)
            def _():
                up(p, s, 3).wait_recv()
                fb[c] = add(xr[c, 3 * PIECE:], ur[c, 3 * PIECE:])

            last(p, s).start()

    def step_f(p):
        for s in range(2):
            for k in range(3):
                @pl.when(z == k)
                def _():
                    up(p, s, k + 1).wait_send()

                @pl.when(z == k + 1)
                def _():
                    down(p, s, k + 1).wait_send()

            c = lax.rem(p, HELD) * 2 + s
            last(p, s).wait_recv()
            rows = pl.ds(pl.multiple_of(b_pos[s] * SUB, SUB), SUB)
            fb[c, rows] = add(fb[c, rows], yr[c])
            last_back(p, s).start()
            keep(p, s).start()

    def step_g(p):
        for s in range(2):
            last_back(p, s).wait_recv()
            keep(p, s).wait()

            @pl.when(has_up)
            def _():
                up_back(p, s, 0).start()

            @pl.when(has_down)
            def _():
                down_back(p, s, 0).start()

    def step_h(p):
        for s in range(2):
            @pl.when(has_down)
            def _():
                up_back(p, s, 0).wait_recv()

            @pl.when(has_down & has_up)
            def _():
                up_back(p, s, 1).start()

            @pl.when(has_up)
            def _():
                down_back(p, s, 0).wait_recv()

            @pl.when(has_down & has_up)
            def _():
                down_back(p, s, 1).start()

    def step_i(p):
        for s in range(2):
            @pl.when(z >= 2)
            def _():
                up_back(p, s, 1).wait_recv()

            @pl.when(z == 2)
            def _():
                up_back(p, s, 2).start()

            @pl.when(z <= 1)
            def _():
                down_back(p, s, 1).wait_recv()

            @pl.when(z == 1)
            def _():
                down_back(p, s, 2).start()

    def step_j(p):
        for s in range(2):
            @pl.when(z == 3)
            def _():
                up_back(p, s, 2).wait_recv()

            @pl.when(z == 0)
            def _():
                down_back(p, s, 2).wait_recv()

            first_back(p, s).start()

    def step_k(p):
        for s in range(2):
            first_back(p, s).wait()
            first(p, s).wait_send()
            last(p, s).wait_send()
            last_back(p, s).wait_send()
            @pl.when(has_up)
            def _():
                up_back(p, s, 0).wait_send()

            @pl.when(has_down)
            def _():
                down_back(p, s, 0).wait_send()

            @pl.when(has_up & has_down)
            def _():
                up_back(p, s, 1).wait_send()
                down_back(p, s, 1).wait_send()

            @pl.when(z == 2)
            def _():
                up_back(p, s, 2).wait_send()

            @pl.when(z == 1)
            def _():
                down_back(p, s, 2).wait_send()

    steps = {"a": step_a, "b": step_b, "c": step_c, "d": step_d, "e": step_e, "f": step_f, "g": step_g, "h": step_h,
             "i": step_i, "j": step_j, "k": step_k}

    def part(t, k):
        for name, behind in PARTS[k]:
            p = t - behind
            if isinstance(p, int):
                if 0 <= p < PAIRS:
                    steps[name](jnp.int32(p))
            else:
                pl.when((p >= 0) & (p < PAIRS))(functools.partial(steps[name], p))

    return part, (c_dev, x_dev, y_dev, z1_dev, z2_dev)


HD = 32
GS = 256
IN = 1024
WIDE = 1024
HALFW = 512
NEG = -1e30
EPS = 1e-05
LOG2E = math.log2(math.e)
SCALE = HD ** -0.5
bf16 = jnp.bfloat16
f32 = jnp.float32
ANY = pl.BlockSpec(memory_space=pl.ANY)
VM = pl.BlockSpec(memory_space=pltpu.VMEM)
SM = pl.BlockSpec(memory_space=pltpu.SMEM)


def nn(left, right):
    return jnp.dot(left, right, preferred_element_type=f32)


def nt(left, right):
    return lax.dot_general(left, right, (((1,), (1,)), ((), ())), preferred_element_type=f32)


def lanes(start, size):
    return pl.ds(pl.multiple_of(start, 128), size)


def rows_at(start, size):
    return pl.ds(pl.multiple_of(start, size), size)


def head_block(tile):
    lane = lax.broadcasted_iota(jnp.int32, tile.shape, 1) // HD
    zero = jnp.zeros_like(tile)
    return jnp.concatenate([jnp.where(lane == j, tile, zero) for j in range(4)], axis=0)


def scores_of(keys, query_block, count):
    scores = nt(keys, query_block)
    if count is None:
        return scores
    place = lax.broadcasted_iota(jnp.int32, scores.shape, 0)
    return jnp.where(place < count, scores, NEG)


def attend(queries, keys, values, count):
    values_t = values.T
    scores = scores_of(keys, head_block(queries), count)
    top = jnp.max(scores, axis=0, keepdims=True)
    weights = jnp.exp2((scores - top) * (LOG2E * SCALE))
    total = jnp.sum(weights, axis=0, keepdims=True)
    low = weights.astype(bf16)
    log_total = top * (LOG2E * SCALE) + jnp.log2(total)
    inverse = 1.0 / total
    mixed, logs = [], []
    for j in range(4):
        span = slice(j * GS, (j + 1) * GS)
        mixed.append(nn(values_t[j * HD:(j + 1) * HD], low[:, span]) * inverse[:, span])
        logs.append(log_total[:, span])
    return jnp.concatenate(mixed, axis=0), jnp.concatenate(logs, axis=0)


def attend_back(queries, keys, values, grads, logs, count):
    keys_t = keys.T
    query_block = head_block(queries)
    grad_block = head_block(grads)
    grad_keys = grad_values = None
    grad_queries = []
    for j in range(4):
        own_query = query_block[j * GS:(j + 1) * GS]
        own_grad = grad_block[j * GS:(j + 1) * GS]
        weights = jnp.exp2(scores_of(keys, own_query, count) * (LOG2E * SCALE) - logs[j:j + 1])
        weighted = weights * nt(values, own_grad)
        inner = jnp.sum(weighted, axis=0, keepdims=True)
        grad_scores = (weighted - weights * inner).astype(bf16)
        value_part = nn(weights.astype(bf16), own_grad)
        key_part = nn(grad_scores, own_query)
        grad_values = value_part if j == 0 else grad_values + value_part
        grad_keys = key_part if j == 0 else grad_keys + key_part
        grad_queries.append(nn(keys_t[j * HD:(j + 1) * HD], grad_scores))
    return jnp.concatenate(grad_queries, axis=0) * SCALE, grad_keys * SCALE, grad_values


def centre(stream):
    centered = stream - jnp.mean(stream, axis=1, keepdims=True)
    inverse = lax.rsqrt(jnp.mean(centered * centered, axis=1, keepdims=True) + EPS)
    return centered * inverse, inverse


def normed(stream, gain, shift):
    return (centre(stream)[0] * gain + shift).astype(bf16)


def norm_back(stream, gain, upstream):
    xhat, inverse = centre(stream)
    scaled = upstream * gain
    along = upstream * xhat
    mean_scaled = jnp.mean(scaled, axis=1, keepdims=True)
    mean_along = jnp.mean(scaled * xhat, axis=1, keepdims=True)
    grad = inverse * (scaled - mean_scaled - xhat * mean_along)
    return grad, jnp.sum(along, axis=0, keepdims=True), jnp.sum(upstream, axis=0, keepdims=True)


def meet(partner):
    barrier = pltpu.get_barrier_semaphore()
    pl.semaphore_signal(barrier, inc=1, device_id=partner, device_id_type=MESH)
    pl.semaphore_wait(barrier, 1)


FWD_IN = (
    ("latents", VM), ("inputs", VM), ("counts", SM), ("cot", ANY),
    ("gain_latent", VM), ("shift_latent", VM), ("gain_input", VM), ("shift_input", VM),
    ("gain_self", VM), ("shift_self", VM), ("gain_mlp", VM), ("shift_mlp", VM),
    ("cq", ANY), ("ck", ANY), ("cv", ANY), ("co", ANY), ("sq", ANY), ("sk", ANY), ("sv", ANY), ("so", ANY),
    ("mi", ANY), ("mib", VM), ("mo", ANY), ("mob", VM),
)
FWD_OUT = (
    ("result", (GS, WIDE), bf16, VM),
    ("s1", (GS, WIDE), f32, VM), ("s2", (GS, WIDE), f32, VM),
    ("lnlT", (WIDE, 2 * GS), bf16, ANY), ("lniT", (WIDE, 2 * IN), bf16, ANY),
    ("snT", (WIDE, 2 * GS), bf16, ANY), ("mnT", (WIDE, 2 * GS), bf16, ANY),
    ("actT", (8, GS, 2 * GS), bf16, ANY), ("dg", (GS, 4096), bf16, ANY),
    ("xq", (GS, WIDE), bf16, ANY), ("xk", (IN, WIDE), bf16, ANY), ("xv", (IN, WIDE), bf16, ANY),
    ("xoT", (HALFW, 2 * GS), bf16, ANY), ("xl", (8, 4, GS), f32, VM),
    ("yq", (GS, WIDE), bf16, ANY), ("yk", (GS, WIDE), bf16, ANY), ("yv", (GS, WIDE), bf16, ANY),
    ("yoT", (HALFW, 2 * GS), bf16, ANY), ("yl", (8, 4, GS), f32, VM),
    ("cotp", (GS, WIDE), bf16, ANY),
    ("rin", (6, WIDE, HALFW), bf16, ANY), ("rout", (2, HALFW, WIDE), bf16, ANY),
    ("rmi", (WIDE, 2048), bf16, ANY), ("rmo", (2048, WIDE), bf16, ANY),
)
FWD_SCRATCH = (
    ("wx", (2, 3, WIDE, HALFW), bf16), ("wxo", (2, HALFW, WIDE), bf16),
    ("wy", (2, 3, WIDE, HALFW), bf16), ("wyo", (2, HALFW, WIDE), bf16),
    ("wmi", (2, WIDE, HALFW), bf16), ("wmo", (2, HALFW, WIDE), bf16),
    ("rbias", (1, 2048), f32),
    ("n", (GS, WIDE), bf16), ("ln", (IN, WIDE), bf16),
    ("t_l", (WIDE, GS), bf16), ("t_i", (WIDE, IN), bf16), ("t_s", (WIDE, GS), bf16), ("t_m", (WIDE, GS), bf16),
    ("q", (GS, WIDE), bf16), ("k", (IN, WIDE), bf16), ("v", (IN, WIDE), bf16), ("o", (GS, WIDE), bf16), ("oT", (WIDE, GS), bf16),
    ("q2", (GS, WIDE), bf16), ("k2", (GS, WIDE), bf16), ("v2", (GS, WIDE), bf16), ("o2", (GS, WIDE), bf16), ("oT2", (WIDE, GS), bf16),
    ("aT", (8, 2, GS, GS), bf16), ("dgs", (8, GS, HALFW), bf16), ("acc", (GS, WIDE), f32),
)


class Names:
    pass


def named(refs, *tables):
    out = Names()
    place = 0
    for table in tables:
        for entry in table:
            setattr(out, entry[0], refs[place])
            place += 1
    out.rest = refs[place:]
    return out


def forward_kernel(*refs):
    r = named(refs, FWD_IN, FWD_OUT, FWD_SCRATCH)
    send, recv, local = r.rest
    core = lax.axis_index("mp")
    partner = (lax.axis_index("dp"), 1 - core)
    meet(partner)
    sent, kept = [], []

    def push(src, dst):
        i = len(sent)
        copy = pltpu.make_async_remote_copy(
            src_ref=src, dst_ref=dst, send_sem=send.at[i], recv_sem=recv.at[i], device_id=partner, device_id_type=MESH)
        copy.start()
        sent.append(copy)
        return copy

    def fetch(src, dst):
        i = len(kept)
        copy = pltpu.make_async_copy(src, dst, local.at[i])
        copy.start()
        kept.append([copy, False])
        return i

    def ready(i):
        kept[i][0].wait()
        kept[i][1] = True

    got = [push(r.ck, r.rin.at[1]), push(r.cv, r.rin.at[2]), push(r.cq, r.rin.at[0]), push(r.co, r.rout.at[0])]
    got.append(push(r.mib, r.rbias))
    near = [fetch(w, r.wx.at[0, i]) for i, w in ((1, r.ck), (2, r.cv), (0, r.cq))] + [fetch(r.co, r.wxo.at[0])]

    r.n[...] = normed(r.latents[...].astype(f32), r.gain_latent[...], r.shift_latent[...])
    r.t_l[...] = r.n[...].T
    fetch(r.t_l, r.lnlT.at[:, pl.ds(0, GS)])
    gain, shift = r.gain_input[...], r.shift_input[...]

    def input_norm(b, _):
        span = rows_at(b * GS, GS)
        block = normed(r.inputs[span].astype(f32), gain, shift)
        r.ln[span] = block
        r.t_i[:, lanes(b * GS, GS)] = block.T
        return 0

    lax.fori_loop(0, IN // GS, input_norm, 0)
    fetch(r.t_i, r.lniT.at[:, pl.ds(0, IN)])
    for i in near[:3]:
        ready(i)

    def project_inputs(half):
        def block(b, _):
            span = rows_at(b * GS, GS)
            rows = r.ln[span]
            r.k[span, half * HALFW:(half + 1) * HALFW] = nn(rows, r.wx[half, 1]).astype(bf16)
            r.v[span, half * HALFW:(half + 1) * HALFW] = nn(rows, r.wx[half, 2]).astype(bf16)
            return 0

        lax.fori_loop(0, IN // GS, block, 0)
        r.q[:, half * HALFW:(half + 1) * HALFW] = nn(r.n[...], r.wx[half, 0]).astype(bf16)

    project_inputs(0)
    got += [push(w, r.rin.at[i]) for i, w in ((3, r.sq), (4, r.sk), (5, r.sv))] + [push(r.so, r.rout.at[1])]
    far = []
    for copy, src, dst in (
        (got[0], r.rin.at[1], r.wx.at[1, 1]), (got[1], r.rin.at[2], r.wx.at[1, 2]),
        (got[2], r.rin.at[0], r.wx.at[1, 0]), (got[3], r.rout.at[0], r.wxo.at[1])):
        copy.wait_recv()
        far.append(fetch(src, dst))
    near2 = [fetch(w, r.wy.at[0, i]) for i, w in enumerate((r.sq, r.sk, r.sv))] + [fetch(r.so, r.wyo.at[0])]
    count = r.counts[core]

    def attention(queries, keys, values, mixed, mixed_t, logs, limit, first):
        def group(g, _):
            at = lanes(g * 128, 128)
            out_t, log_total = attend(queries[:, at], keys[:, at], values[:, at], limit)
            out_t = out_t.astype(bf16)
            mixed_t[rows_at(g * 128, 128)] = out_t
            mixed[:, at] = out_t.T
            logs[g] = log_total
            return 0

        lax.fori_loop(first, first + 4, group, 0)

    attention(r.q, r.k, r.v, r.o, r.oT, r.xl, count, 0)
    got.append(push(r.mi, r.rmi))
    got.append(push(r.mo, r.rmo))
    for i in far[:3]:
        ready(i)
    project_inputs(1)
    fetch(r.q, r.xq)
    fetch(r.k, r.xk)
    fetch(r.v, r.xv)
    attention(r.q, r.k, r.v, r.o, r.oT, r.xl, count, 4)
    fetch(r.oT.at[pl.ds(0, HALFW)], r.xoT.at[:, pl.ds(0, GS)])
    push(r.oT.at[pl.ds(HALFW, HALFW)], r.xoT.at[:, pl.ds(GS, GS)])
    push(r.t_l, r.lnlT.at[:, pl.ds(GS, GS)])
    push(r.t_i, r.lniT.at[:, pl.ds(IN, IN)])
    push(r.cot, r.cotp)
    ready(near[3])
    ready(far[3])

    def out_project(mixed, weight):
        return nn(mixed[:, :HALFW], weight[0]) + nn(mixed[:, HALFW:], weight[1])

    r.s1[...] = r.latents[...].astype(f32) + out_project(r.o, r.wxo)
    r.n[...] = normed(r.s1[...], r.gain_self[...], r.shift_self[...])
    far2 = []
    for copy, src, dst in (
        (got[5], r.rin.at[3], r.wy.at[1, 0]), (got[6], r.rin.at[4], r.wy.at[1, 1]),
        (got[7], r.rin.at[5], r.wy.at[1, 2]), (got[8], r.rout.at[1], r.wyo.at[1])):
        copy.wait_recv()
        far2.append(fetch(src, dst))
    r.t_s[...] = r.n[...].T
    fetch(r.t_s, r.snT.at[:, pl.ds(0, GS)])
    push(r.t_s, r.snT.at[:, pl.ds(GS, GS)])
    for i in near2 + far2:
        ready(i)
    for half in range(2):
        at = slice(half * HALFW, (half + 1) * HALFW)
        for i, dst in enumerate((r.q2, r.k2, r.v2)):
            dst[:, at] = nn(r.n[...], r.wy[half, i]).astype(bf16)
    fetch(r.q2, r.yq)
    fetch(r.k2, r.yk)
    fetch(r.v2, r.yv)
    attention(r.q2, r.k2, r.v2, r.o2, r.oT2, r.yl, None, 0)
    attention(r.q2, r.k2, r.v2, r.o2, r.oT2, r.yl, None, 4)
    fetch(r.oT2.at[pl.ds(0, HALFW)], r.yoT.at[:, pl.ds(0, GS)])
    push(r.oT2.at[pl.ds(HALFW, HALFW)], r.yoT.at[:, pl.ds(GS, GS)])

    chunk_sem = len(kept)

    def chunk_copies(src_in, src_out, c, slot):
        at = lanes(c * HALFW, HALFW)
        return (
            pltpu.make_async_copy(src_in.at[:, at], r.wmi.at[slot], local.at[chunk_sem + slot]),
            pltpu.make_async_copy(src_out.at[rows_at(c * HALFW, HALFW)], r.wmo.at[slot], local.at[chunk_sem + 2 + slot]),
        )

    def start_chunk(n):
        slot = lax.rem(n, 2)

        @pl.when(n < 4)
        def _():
            for copy in chunk_copies(r.mi, r.mo, n, slot):
                copy.start()

        @pl.when(n >= 4)
        def _():
            for copy in chunk_copies(r.rmi, r.rmo, n - 4, slot):
                copy.start()

    start_chunk(jnp.int32(0))
    r.s2[...] = r.s1[...] + out_project(r.o2, r.wyo)
    r.n[...] = normed(r.s2[...], r.gain_mlp[...], r.shift_mlp[...])
    r.t_m[...] = r.n[...].T
    kept += [None] * 4
    fetch(r.t_m, r.mnT.at[:, pl.ds(0, GS)])
    push(r.t_m, r.mnT.at[:, pl.ds(GS, GS)])
    r.acc[...] = jnp.zeros((GS, WIDE), f32)
    for copy in (got[4], got[9], got[10]):
        copy.wait_recv()

    def feed(n, _):
        slot = lax.rem(n, 2)

        @pl.when(n + 1 < 8)
        def _():
            start_chunk(n + 1)

        for copy in chunk_copies(r.mi, r.mo, 0, slot):
            copy.wait()
        at = lanes(lax.rem(n, 4) * HALFW, HALFW)
        bias = jnp.where(n < 4, r.mib[:, at], r.rbias[:, at])
        hidden = nn(r.n[...], r.wmi[slot]) + bias
        area = 0.5 + 0.5 * lax.erf(hidden * (0.5 ** 0.5))
        density = jnp.exp(-0.5 * hidden * hidden) * ((2 * math.pi) ** -0.5)
        act = (hidden * area).astype(bf16)
        r.dgs[n] = (area + hidden * density).astype(bf16)
        r.aT[n] = act.T.reshape(2, GS, GS)
        r.acc[...] += nn(act, r.wmo[slot])
        return 0

    lax.fori_loop(0, 8, feed, 0)
    for c in range(4):
        fetch(r.aT.at[c], r.actT.at[pl.ds(2 * c, 2), :, pl.ds(0, GS)])
        push(r.aT.at[4 + c], r.actT.at[pl.ds(2 * c, 2), :, pl.ds(GS, GS)])
    for c in range(8):
        fetch(r.dgs.at[c], r.dg.at[:, pl.ds(c * HALFW, HALFW)])
    r.result[...] = (r.s2[...] + (r.acc[...] + r.mob[...])).astype(bf16)
    for i, entry in enumerate(kept):
        if entry is not None and not entry[1]:
            ready(i)
    seen = [id(c) for c in got]
    for copy in sent:
        copy.wait_send()
        if id(copy) not in seen:
            copy.wait_recv()


def forward(*args):
    return pl.pallas_call(
        forward_kernel,
        out_shape=[jax.ShapeDtypeStruct(shape, dtype) for _, shape, dtype, _ in FWD_OUT],
        in_specs=[spec for _, spec in FWD_IN],
        out_specs=[spec for _, _, _, spec in FWD_OUT],
        scratch_shapes=[pltpu.VMEM(shape, dtype) for _, shape, dtype in FWD_SCRATCH]
        + [pltpu.SemaphoreType.DMA((24,)), pltpu.SemaphoreType.DMA((24,)), pltpu.SemaphoreType.DMA((64,))],
        compiler_params=pltpu.CompilerParams(collective_id=1, has_side_effects=True, vmem_limit_bytes=60 << 20),
    )(*args)


BWD_IN = (
    ("latents", VM), ("inputs", ANY), ("counts", SM), ("cot", VM),
    ("gain_latent", VM), ("gain_input", VM), ("gain_self", VM), ("gain_mlp", VM),
    ("cq", ANY), ("ck", ANY), ("cv", ANY), ("co", ANY), ("sq", ANY), ("sk", ANY), ("sv", ANY), ("so", ANY),
    ("mi", ANY), ("mo", ANY),
) + tuple((name, VM if name in ("xl", "yl") else ANY) for name, _, _, _ in FWD_OUT[1:])
ROWS_OUT = 8192
BWD_OUT = (
    ("grads", (ROWS_OUT, WIDE), bf16, ANY), ("summed", (ROWS_OUT, WIDE), bf16, ANY), ("small", (SMALL, WIDE), f32, VM),
    ("grad_latents", (GS, WIDE), f32, VM), ("grad_inputs", (IN, WIDE), f32, ANY),
)
BWD_SCRATCH = (
    ("wy", (2, 3, WIDE, HALFW), bf16), ("wyo", (2, HALFW, WIDE), bf16), ("wxo", (2, HALFW, WIDE), bf16),
    ("wmi", (2, WIDE, HALFW), bf16), ("wmo", (2, HALFW, WIDE), bf16),
    ("mc", (2 * GS, WIDE), bf16), ("sc", (2 * GS, WIDE), bf16),
    ("dk", (8, GS, HALFW), bf16), ("dgs", (2, GS, HALFW), bf16),
    ("mT", (WIDE, 2 * GS), bf16), ("big", (4, HALFW, HALFW), bf16), ("bigr", (4, GS, HALFW), bf16),
    ("sT", (WIDE, 2 * GS), bf16), ("kv", (2, IN, WIDE), bf16),
    ("q", (GS, WIDE), bf16), ("oT", (HALFW, 2 * GS), bf16),
    ("q2", (GS, WIDE), bf16), ("k2", (GS, WIDE), bf16), ("v2", (GS, WIDE), bf16), ("oT2", (HALFW, 2 * GS), bf16),
    ("g", (GS, WIDE), bf16),
    ("dq", (2 * GS, HALFW), bf16), ("dqr", (GS, HALFW), bf16), ("dvr", (2, HALFW, HALFW), bf16),
    ("dq2", (3, 2 * GS, HALFW), bf16), ("dqr2", (3, GS, HALFW), bf16),
    ("xin", (2, GS, WIDE), bf16), ("wide", (2, GS, WIDE), f32),
    ("stage", (2, HALFW, WIDE), bf16), ("bsum", (8, HALFW), f32), ("sacc", (SMALL, WIDE), f32), ("sbuf", (5, SMALL, WIDE), f32),
)
ROW_MO, ROW_MI, ROW_SO, ROW_SQ, ROW_CO, ROW_CQ = 0, 2048, 4096, 4608, 6144, 6656


def backward_kernel(reduce, *refs):
    r = named(refs, BWD_IN, BWD_OUT, BWD_SCRATCH, REDUCE_SCRATCH if reduce else ())
    send, recv, local, stage_sem, chunk_sem, x_sem, *reduce_sems = r.rest
    core = lax.axis_index("mp")
    partner = (lax.axis_index("dp"), 1 - core)
    if reduce:
        part, small_devs = reducer(r, *reduce_sems[:3])
    else:
        meet(partner)
    sent, kept, staged = [], [], []
    state = {"tick": 0, "settled": 0}

    def settle(upto=None):
        upto = len(staged) if upto is None else upto
        for copy in staged[state["settled"]:upto]:
            copy.wait()
        state["settled"] = max(state["settled"], upto)

    def may_take(first, last):
        for n in range(first, last):
            if n % 3 == 0:
                assert min(n // 3 + AHEAD + 1, PAIRS) <= state["settled"]

    def tick(count=1):
        for _ in range(count):
            n = state["tick"]
            state["tick"] = n + 1
            if reduce:
                may_take(n, n + 1)
                part(n // 3, n % 3)

    def loop_tick(n):
        if reduce:
            for k in range(3):
                pl.when(lax.rem(n, 3) == k)(functools.partial(part, n // 3, k))

    def loop_ticks(count):
        n = state["tick"]
        state["tick"] = n + count
        if reduce:
            may_take(n, n + count)
        return n

    def push(src, dst):
        i = len(sent)
        copy = pltpu.make_async_remote_copy(
            src_ref=src, dst_ref=dst, send_sem=send.at[i], recv_sem=recv.at[i], device_id=partner, device_id_type=MESH)
        copy.start()
        sent.append(copy)
        return copy

    def fetch(src, dst):
        copy = pltpu.make_async_copy(src, dst, local.at[len(kept)])
        copy.start()
        kept.append(copy)
        return copy

    def stage(write, row):
        i = len(staged)
        slot = i % 2
        if i >= 2 and state["settled"] <= i - 2:
            staged[i - 2].wait()
            state["settled"] = i - 1
        write(r.stage.at[slot])
        copy = pltpu.make_async_copy(r.stage.at[slot], r.grads.at[pl.ds(row, HALFW)], stage_sem.at[slot])
        copy.start()
        staged.append(copy)

    early = [fetch(r.actT, r.dk), fetch(r.cotp, r.mc.at[pl.ds(GS, GS)])]

    def chunk_copies(src_in, src_out, c, n, slot):
        at = lanes(c * HALFW, HALFW)
        return (
            pltpu.make_async_copy(src_in.at[:, at], r.wmi.at[slot], chunk_sem.at[0, slot]),
            pltpu.make_async_copy(src_out.at[rows_at(c * HALFW, HALFW)], r.wmo.at[slot], chunk_sem.at[1, slot]),
            pltpu.make_async_copy(r.dg.at[:, lanes(n * HALFW, HALFW)], r.dgs.at[slot], chunk_sem.at[2, slot]),
        )

    def start_chunk(i):
        slot = lax.rem(i, 2)

        @pl.when(i < 4)
        def _():
            for copy in chunk_copies(r.rmi, r.rmo, i, 4 + i, slot):
                copy.start()

        @pl.when(i >= 4)
        def _():
            for copy in chunk_copies(r.mi, r.mo, i - 4, i - 4, slot):
                copy.start()

    start_chunk(jnp.int32(0))
    load_m = [fetch(r.mnT, r.mT), fetch(r.s2, r.wide.at[1])]
    load_y = [fetch(w, r.wy.at[0, i]) for i, w in enumerate((r.sq, r.sk, r.sv))]
    load_y += [fetch(r.rin.at[pl.ds(3, 3)], r.wy.at[1]), fetch(r.so, r.wyo.at[0]), fetch(r.rout.at[1], r.wyo.at[1])]
    load_y += [fetch(a, b) for a, b in ((r.yq, r.q2), (r.yk, r.k2), (r.yv, r.v2), (r.yoT, r.oT2), (r.snT, r.sT))]
    r.mc[pl.ds(0, GS)] = r.cot[...]
    for copy in early:
        copy.wait()
    for m in range(4):
        def write(dst, m=m):
            dst[...] = nn(r.dk[2 * m:2 * m + 2].reshape(HALFW, 2 * GS), r.mc[...]).astype(bf16)

        stage(write, ROW_MO + m * HALFW)
    settle()
    if reduce:
        for t in range(-AHEAD, 0):
            part(t, 0)
    r.wide[0] = jnp.zeros((GS, WIDE), f32)

    def feed(i, ticks=None):
        slot = lax.rem(i, 2)

        @pl.when(i + 1 < 8)
        def _():
            start_chunk(i + 1)

        for copy in chunk_copies(r.mi, r.mo, 0, 0, slot):
            copy.wait()
        grad = (nt(r.cot[...], r.wmo[slot]) * r.dgs[slot].astype(f32)).astype(bf16)
        r.bsum[pl.ds(lax.rem(i + 4, 8), 1)] = jnp.sum(grad.astype(f32), axis=0, keepdims=True)

        @pl.when(i < 4)
        def _():
            r.bigr[lax.rem(i, 4)] = grad

        @pl.when(i >= 4)
        def _():
            r.big[lax.rem(i, 4), pl.ds(0, GS)] = grad

        r.wide[0] += nt(grad, r.wmi[slot])
        if ticks is not None:
            loop_tick(i + ticks)
        return 0

    lax.fori_loop(0, 4, lambda i, _: feed(i), 0)
    push_dh = push(r.bigr, r.big.at[:, pl.ds(GS, GS)])
    lax.fori_loop(4, 5, lambda i, _: feed(i), 0)
    first_tick = loop_ticks(3)
    lax.fori_loop(5, 8, lambda i, _: feed(i, first_tick - 5), 0)
    load_x = [fetch(r.co, r.wxo.at[0]), fetch(r.rout.at[0], r.wxo.at[1])]
    load_x += [fetch(a, b) for a, b in ((r.xq, r.q), (r.xk, r.kv.at[0]), (r.xv, r.kv.at[1]), (r.xoT, r.oT))]

    for copy in load_m:
        copy.wait()
    grad, along, plain = norm_back(r.wide[1], r.gain_mlp[...], r.wide[0])
    load_s = fetch(r.s1, r.wide.at[1])
    r.small[6:7] = along
    r.small[7:8] = plain
    r.wide[0] = r.cot[...].astype(f32) + grad
    r.sc[pl.ds(0, GS)] = r.wide[0].astype(bf16)
    push_c = push(r.sc.at[pl.ds(0, GS)], r.sc.at[pl.ds(GS, GS)])
    tick()
    push_dh.wait_recv()
    for c in range(4):
        def write(dst, c=c):
            dst[...] = jnp.concatenate(
                [nn(r.mT[c % 2 * HALFW:(c % 2 + 1) * HALFW], r.big[c // 2 * 2 + e]).astype(bf16)
                 for e in range(2)], axis=1)

        stage(write, ROW_MI + c * HALFW)
        settle(3 + c)
        tick()
    settle()
    load_l = fetch(r.lnlT, r.mT)

    def attention_back(queries, keys, values, logs, limit, take, own, other, hand_over, every):
        first = loop_ticks(8 // every)

        def group(i, _):
            g = lax.rem(i + 4, 8)
            at = lanes(g * 128, 128)
            to = lanes(lax.rem(i, 4) * 128, 128)
            pl.when(i == 4)(hand_over)
            grad_q, grad_k, grad_v = attend_back(queries[:, at], keys[:, at], values[:, at], r.g[:, at], logs[g], limit)
            grad_q, grad_k, grad_v = grad_q.astype(bf16).T, grad_k.astype(bf16), grad_v.astype(bf16)
            pl.when(i < 4)(lambda: take(other, to, grad_q, grad_k, grad_v))
            pl.when(i >= 4)(lambda: take(own, to, grad_q, grad_k, grad_v))
            if every == 1:
                loop_tick(first + i)
            else:
                pl.when(lax.rem(i, every) == every - 1)(lambda: loop_tick(first + i // every))
            return 0

        lax.fori_loop(0, 8, group, 0)

    def out_back(cots, weight):
        cot = cots[pl.ds(0, GS)]
        for half in range(2):
            r.g[:, half * HALFW:(half + 1) * HALFW] = nt(cot, weight[half]).astype(bf16)

    def grad_fold(left, right, row):
        def write(dst):
            for e in range(2):
                dst[:, e * HALFW:(e + 1) * HALFW] = nn(left[e * HALFW:(e + 1) * HALFW], right[...]).astype(bf16)

        stage(write, row)

    def crossing(i, src, dst):
        return pltpu.make_async_remote_copy(
            src_ref=src, dst_ref=dst, send_sem=send.at[i], recv_sem=recv.at[i], device_id=partner, device_id_type=MESH)

    push_y = crossing(12, r.dqr2, r.dq2.at[:, pl.ds(GS, GS)])
    push_x = [
        crossing(13, r.dqr, r.dq.at[pl.ds(GS, GS)]), crossing(14, r.bigr, r.dk.at[pl.ds(4, 4)]),
        crossing(15, r.dvr, r.big.at[pl.ds(2, 2)])]

    def take_y(dst, to, grad_q, grad_k, grad_v):
        for i, grad in enumerate((grad_q, grad_k, grad_v)):
            dst[i, pl.ds(0, GS), to] = grad

    def take_x(dst, to, grad_q, grad_k, grad_v):
        dst_q, dst_k, dst_v = dst
        dst_q[pl.ds(0, GS), to] = grad_q
        dst_k[pl.ds(0, 4), :, to] = grad_k.reshape(4, GS, 128)
        dst_v[pl.ds(0, 2), :, to] = grad_v.reshape(2, HALFW, 128)

    for copy in load_y:
        copy.wait()
    out_back(r.sc, r.wyo)
    tick()
    attention_back(r.q2, r.k2, r.v2, r.yl, None, take_y, r.dq2, r.dqr2, push_y.start, 1)
    push_c.wait_recv()

    def write_so(dst):
        dst[...] = nn(r.oT2[...], r.sc[...]).astype(bf16)

    stage(write_so, ROW_SO)
    tick()
    settle()
    load_s.wait()
    upstream = None
    for i in range(3):
        term = nt(r.dq2[i, :GS], r.wy[0, i]) + nt(r.dqr2[i], r.wy[1, i])
        upstream = term if upstream is None else upstream + term
    grad, along, plain = norm_back(r.wide[1], r.gain_self[...], upstream)
    r.small[4:5] = along
    r.small[5:6] = plain
    r.wide[0] += grad
    load_w = [fetch(w, r.wy.at[0, i]) for i, w in enumerate((r.cq, r.ck, r.cv))] + [fetch(r.rin.at[pl.ds(0, 3)], r.wy.at[1])]
    r.mc[pl.ds(0, GS)] = r.wide[0].astype(bf16)
    push_c2 = push(r.mc.at[pl.ds(0, GS)], r.mc.at[pl.ds(GS, GS)])
    push_y.wait_recv()
    tick()
    for i in range(3):
        grad_fold(r.sT, r.dq2.at[i], ROW_SQ + i * HALFW)
        settle(9 + i)
        tick()

    for copy in load_x:
        copy.wait()
    out_back(r.mc, r.wxo)
    tick()
    count = r.counts[core]
    push_dh.wait_send()
    push_c2.wait_recv()

    def write_co(dst):
        dst[...] = nn(r.oT[...], r.mc[...]).astype(bf16)

    stage(write_co, ROW_CO)
    tick()
    settle()

    def hand_over_x():
        for copy in push_x:
            copy.start()

    attention_back(r.q, r.kv.at[0], r.kv.at[1], r.xl, count, take_x, (r.dq, r.dk, r.big), (r.dqr, r.bigr, r.dvr), hand_over_x, 1)
    load_i = [fetch(r.lniT.at[:, pl.ds(0, IN)], r.kv.at[0]), fetch(r.lniT.at[:, pl.ds(IN, IN)], r.kv.at[1])]
    for copy in push_x:
        copy.wait_recv()
    load_l.wait()
    grad_fold(r.mT, r.dq, ROW_CQ)
    settle()
    tick()
    for copy in load_i:
        copy.wait()

    def tall(blocks):
        return blocks.reshape(IN, HALFW)

    def grad_tall(right, row):
        def write(dst):
            for e in range(2):
                at = slice(e * HALFW, (e + 1) * HALFW)
                dst[:, at] = (nn(r.kv[0, at], tall(right[0])) + nn(r.kv[1, at], tall(right[1]))).astype(bf16)

        stage(write, row)

    grad_tall((r.dk[:4], r.dk[4:]), ROW_CQ + HALFW)
    tick()
    grad_tall((r.big[:2], r.big[2:]), ROW_CQ + 2 * HALFW)
    settle()
    tick()
    for copy in load_w:
        copy.wait()
    upstream = nt(r.dq[:GS], r.wy[0, 0]) + nt(r.dqr[...], r.wy[1, 0])
    grad, along, plain = norm_back(r.latents[...].astype(f32), r.gain_latent[...], upstream)
    r.small[0:1] = along
    r.small[1:2] = plain
    r.grad_latents[...] = r.wide[0] + grad
    r.small[2:4] = jnp.zeros((2, WIDE), f32)

    def x_in(b):
        slot = lax.rem(b, 2)
        return pltpu.make_async_copy(r.inputs.at[rows_at(b * GS, GS)], r.xin.at[slot], x_sem.at[0, slot])

    def x_out(b):
        slot = lax.rem(b, 2)
        return pltpu.make_async_copy(r.wide.at[slot], r.grad_inputs.at[rows_at(b * GS, GS)], x_sem.at[1, slot])

    x_in(jnp.int32(0)).start()

    def input_back(b, _):
        slot = lax.rem(b, 2)

        @pl.when(b + 1 < IN // GS)
        def _():
            x_in(b + 1).start()

        x_in(b).wait()

        @pl.when(b >= 2)
        def _():
            x_out(b - 2).wait()

        half, at = b // 2, rows_at(lax.rem(b, 2) * GS, GS)
        up = nt(r.dk[b], r.wy[0, 1]) + nt(r.bigr[b], r.wy[1, 1]) + nt(r.big[half, at], r.wy[0, 2]) + nt(r.dvr[half, at], r.wy[1, 2])
        grad, along, plain = norm_back(r.xin[slot].astype(f32), r.gain_input[...], up)
        r.small[2:3] += along
        r.small[3:4] += plain
        r.wide[slot] = grad
        x_out(b).start()
        loop_tick(ticks + b)
        return 0

    ticks = loop_ticks(IN // GS)

    lax.fori_loop(0, IN // GS, input_back, 0)
    r.small[8:9] = jnp.sum(r.cot[...].astype(f32), axis=0, keepdims=True)
    r.small[13:16] = jnp.zeros((3, WIDE), f32)
    for i in range(4):
        half, odd = i // 2, i % 2 * 2
        mine = jnp.concatenate([r.bsum[odd:odd + 1], r.bsum[odd + 1:odd + 2]], axis=1)
        other = jnp.concatenate([r.bsum[odd + 4:odd + 5], r.bsum[odd + 5:odd + 6]], axis=1)
        r.small[9 + i:10 + i] = jnp.where(core == half, mine, other)
    x_out(jnp.int32(IN // GS - 2)).wait()
    x_out(jnp.int32(IN // GS - 1)).wait()
    for copy in (push_c, push_y, push_c2, *push_x):
        copy.wait_send()
    if not reduce:
        return
    tick(-state["tick"] % 3)
    begin = state["tick"] // 3
    small_send, small_recv = reduce_sems[3:]

    def small_copy(i):
        return pltpu.make_async_remote_copy(
            src_ref=r.sacc, dst_ref=r.sbuf.at[i], send_sem=small_send.at[i], recv_sem=small_recv.at[i],
            device_id=small_devs[i], device_id_type=MESH)

    r.sacc[...] = r.small[...]
    small_copy(0).start()

    def iteration(t, _):
        for k in range(3):
            part(t, k)
        for i in range(5):
            @pl.when(t == begin + i)
            def _():
                small_copy(i).wait()
                r.sacc[...] += r.sbuf[i]
                if i < 4:
                    small_copy(i + 1).start()
        return 0

    lax.fori_loop(begin, PAIRS + BEHIND, iteration, 0)
    r.small[...] = r.sacc[...]


def backward(reduce, *args):
    scratch = [pltpu.VMEM(shape, dtype) for _, shape, dtype in BWD_SCRATCH]
    sems = [(16,), (16,), (48,), (2,), (3, 2), (2, 2)]
    if reduce:
        scratch += [pltpu.VMEM(shape, bf16) for _, shape in REDUCE_SCRATCH]
        sems += [(12, 2, NS), (12, 2, NS), (2, 2, NS), (5,), (5,)]
    return pl.pallas_call(
        functools.partial(backward_kernel, reduce),
        out_shape=[jax.ShapeDtypeStruct(shape, dtype) for _, shape, dtype, _ in BWD_OUT],
        in_specs=[spec for _, spec in BWD_IN],
        out_specs=[spec for _, _, _, spec in BWD_OUT],
        scratch_shapes=scratch + [pltpu.SemaphoreType.DMA(shape) for shape in sems],
        compiler_params=pltpu.CompilerParams(
            collective_id=0 if reduce else 2, has_side_effects=True, vmem_limit_bytes=63 << 20),
    )(*args)


FINISH_OUT = (
    ("cq", (WIDE, HALFW)), ("ck", (WIDE, HALFW)), ("cv", (WIDE, HALFW)), ("co", (HALFW, WIDE)),
    ("sq", (WIDE, HALFW)), ("sk", (WIDE, HALFW)), ("sv", (WIDE, HALFW)), ("so", (HALFW, WIDE)),
    ("mi", (WIDE, 2048)), ("mo", (2048, WIDE)), ("gi", (IN, WIDE)), ("gl", (GS, WIDE)), ("result", (GS, WIDE)),
)


def finish_kernel(packed, gi, gl, result, *refs):
    r = named(refs, FINISH_OUT)
    low, high, mid_gi, mid_gl, mid_result, sem_in, sem_out, sem_copy = r.rest
    through = [
        [pltpu.make_async_copy(src, mid, sem_copy.at[0, i]), pltpu.make_async_copy(mid, dst, sem_copy.at[1, i])]
        for i, (src, mid, dst) in enumerate(((gi, mid_gi, r.gi), (gl, mid_gl, r.gl), (result, mid_result, r.result)))]
    plan = []
    for c in range(4):
        plan.append((ROW_MO + c * HALFW, [(r.mo.at[pl.ds(c * HALFW, HALFW)], 0, WIDE)]))
    for c in range(4):
        plan.append((ROW_MI + c * HALFW, [(r.mi.at[pl.ds(c % 2 * HALFW, HALFW), pl.ds(c // 2 * WIDE, WIDE)], 0, WIDE)]))
    for start, out, tall in ((ROW_SO, r.so, (r.sq, r.sk, r.sv)), (ROW_CO, r.co, (r.cq, r.ck, r.cv))):
        plan.append((start, [(out, 0, WIDE)]))
        for i, dst in enumerate(tall):
            plan.append((start + (i + 1) * HALFW, [(dst.at[pl.ds(e * HALFW, HALFW)], e * HALFW, HALFW) for e in range(2)]))
    slots = low.shape[0]

    def load(n):
        return pltpu.make_async_copy(packed.at[pl.ds(plan[n][0], HALFW)], low.at[n % slots], sem_in.at[n % slots])

    def stores(n):
        return [
            pltpu.make_async_copy(high.at[n % slots, :, pl.ds(at, size)], dst, sem_out.at[n % slots, e])
            for e, (dst, at, size) in enumerate(plan[n][1])]

    for n in range(slots - 1):
        load(n).start()
    for pair in through:
        pair[0].start()
    for n in range(len(plan)):
        if n + slots - 1 < len(plan):
            load(n + slots - 1).start()
        load(n).wait()
        if n >= slots:
            for copy in stores(n - slots):
                copy.wait()
        high[n % slots] = low[n % slots].astype(f32)
        for copy in stores(n):
            copy.start()
        if 4 <= n < 7:
            through[n - 4][0].wait()
            through[n - 4][1].start()
    for n in range(len(plan) - slots, len(plan)):
        for copy in stores(n):
            copy.wait()
    for pair in through:
        pair[1].wait()


def finish(*args):
    slots = 4
    return pl.pallas_call(
        finish_kernel,
        out_shape=[jax.ShapeDtypeStruct(shape, bf16 if name == "result" else f32) for name, shape in FINISH_OUT],
        in_specs=[ANY] * 4,
        out_specs=[ANY] * len(FINISH_OUT),
        scratch_shapes=[pltpu.VMEM((slots, HALFW, WIDE), bf16), pltpu.VMEM((slots, HALFW, WIDE), f32),
                        pltpu.VMEM((IN, WIDE), f32), pltpu.VMEM((GS, WIDE), f32), pltpu.VMEM((GS, WIDE), bf16)]
        + [pltpu.SemaphoreType.DMA((slots,)), pltpu.SemaphoreType.DMA((slots, 2)), pltpu.SemaphoreType.DMA((2, 3))],
        compiler_params=pltpu.CompilerParams(vmem_limit_bytes=60 << 20),
    )(*args)


def local(
    latents, inputs, valid_counts, cotangent,
    gain_latent, shift_latent, gain_input, shift_input,
    cross_query, cross_key, cross_value, cross_out,
    gain_self, shift_self,
    self_query, self_key, self_value, self_out,
    gain_mlp, shift_mlp,
    mlp_in, mlp_in_bias, mlp_out, mlp_out_bias,
):
    core = lax.axis_index("mp")

    def row(vector):
        return vector.reshape(1, -1)

    weights = (cross_query, cross_key, cross_value, cross_out, self_query, self_key, self_value, self_out)
    result, *kept = forward(
        latents, inputs, valid_counts, cotangent,
        row(gain_latent), row(shift_latent), row(gain_input), row(shift_input),
        row(gain_self), row(shift_self), row(gain_mlp), row(shift_mlp),
        *weights, mlp_in, row(mlp_in_bias), mlp_out, row(mlp_out_bias))
    reduce = lax.axis_size("dp") == 16
    grads, packed, small, grad_latents, grad_inputs = backward(
        reduce, latents, inputs, valid_counts, cotangent,
        row(gain_latent), row(gain_input), row(gain_self), row(gain_mlp),
        *weights, mlp_in, mlp_out, *kept)
    if not reduce:
        packed, small = lax.psum(grads, "dp"), lax.psum(small, ("dp", "mp"))

    cq, ck, cv, co, sq, sk, sv, so, mi, mo, grad_inputs, grad_latents, result = finish(
        packed, grad_inputs, grad_latents, result)
    half = mlp_in_bias.shape[0]
    hidden_bias = lax.dynamic_slice_in_dim(small[9:13].reshape(-1), core * half, half)
    return (
        result, grad_latents, grad_inputs, *(small[i] for i in range(4)), cq, ck, cv, co,
        small[4], small[5], sq, sk, sv, so, small[6], small[7], mi, hidden_bias, mo, small[8],
    )


def solution(mesh):
    return jax.shard_map(
        local,
        mesh=mesh,
        in_specs=(
            P(("dp", "mp"), None),
            P(("dp", "mp"), None),
            P("dp"),
            P(("dp", "mp"), None),
            P(),
            P(),
            P(),
            P(),
            P(None, "mp"),
            P(None, "mp"),
            P(None, "mp"),
            P("mp", None),
            P(),
            P(),
            P(None, "mp"),
            P(None, "mp"),
            P(None, "mp"),
            P("mp", None),
            P(),
            P(),
            P(None, "mp"),
            P("mp"),
            P("mp", None),
            P(),
        ),
        out_specs=(
            P(("dp", "mp"), None),
            P(("dp", "mp"), None),
            P(("dp", "mp"), None),
            P(),
            P(),
            P(),
            P(),
            P(None, "mp"),
            P(None, "mp"),
            P(None, "mp"),
            P("mp", None),
            P(),
            P(),
            P(None, "mp"),
            P(None, "mp"),
            P(None, "mp"),
            P("mp", None),
            P(),
            P(),
            P(None, "mp"),
            P("mp"),
            P("mp", None),
            P(),
        ),
        check_vma=False,
    )
```

```python
import functools
import math

import jax
import jax.numpy as jnp
from jax import lax
from jax.experimental import pallas as pl
from jax.experimental.pallas import tpu as pltpu
from jax.sharding import PartitionSpec as P

MESH = pl.DeviceIdType.MESH
NS = 16
CH = 256
HALF = CH // 2
PIECE = HALF // 4
SUB = PIECE // 2
SMALL = 16
PARTS = (
    (("a", -2), ("b", 0), ("d", 2)),
    (("j", 6), ("i", 5), ("c", 1)),
    (("h", 4), ("f", 3), ("e", 2), ("k", 8)),
)
BEHIND = 8
AHEAD = 2
OWN = 3
HELD = 6
PAIRS = 16
REDUCE_SCRATCH = (
    ("own", (2 * OWN, HALF, 1024)), ("xr", (2 * HELD, HALF, 1024)), ("ur", (2 * HELD, HALF, 1024)), ("dr", (2 * HELD, HALF, 1024)),
    ("fb", (2 * HELD, PIECE, 1024)), ("yr", (2 * HELD, PIECE, 1024)),
)


def reducer(r, send, recv, loc):
    g_ref, out_ref, own, xr, ur, dr, fb, yr = r.grads, r.summed, r.own, r.xr, r.ur, r.dr, r.fb, r.yr
    dp = lax.axis_index("dp")
    core = lax.axis_index("mp")
    z = dp // 4
    px = lax.rem(dp, 2)
    py = lax.rem(dp // 2, 2)
    x_dev = (dp + 1 - 2 * px, core)
    y_dev = (dp + 2 - 4 * py, core)
    c_dev = (dp, 1 - core)
    up_dev = (dp + 4, core)
    down_dev = (dp - 4, core)
    z1_dev = (dp + 4 - 8 * lax.rem(z, 2), core)
    z2_dev = (dp + 8 - 16 * (z // 2), core)
    has_up = z < 3
    has_down = z > 0

    barrier = pltpu.get_barrier_semaphore()
    for dev in (x_dev, y_dev, c_dev, z2_dev):
        pl.semaphore_signal(barrier, inc=1, device_id=dev, device_id_type=MESH)

    @pl.when(has_up)
    def _():
        pl.semaphore_signal(barrier, inc=1, device_id=up_dev, device_id_type=MESH)

    @pl.when(has_down)
    def _():
        pl.semaphore_signal(barrier, inc=1, device_id=down_dev, device_id_type=MESH)

    pl.semaphore_wait(barrier, 4 + has_up.astype(jnp.int32) + has_down.astype(jnp.int32))

    def remote(src, dst, kind, p, s, dev):
        slot = lax.rem(p, NS)
        return pltpu.make_async_remote_copy(
            src_ref=src, dst_ref=dst, send_sem=send.at[kind, s, slot], recv_sem=recv.at[kind, s, slot],
            device_id=dev, device_id_type=MESH)

    a_pos = (px, py)
    b_pos = (py, px)
    a_dev = (x_dev, y_dev)
    b_dev = (y_dev, x_dev)

    def base(p, s):
        return (2 * p + s) * CH

    def first(p, s):
        c = lax.rem(p, HELD) * 2 + s
        return remote(g_ref.at[pl.ds(base(p, s) + (1 - a_pos[s]) * HALF, HALF)], xr.at[c], 0, p, s, a_dev[s])

    def mine(p, s):
        c = lax.rem(p, OWN) * 2 + s
        return pltpu.make_async_copy(g_ref.at[pl.ds(base(p, s) + a_pos[s] * HALF, HALF)], own.at[c], loc.at[0, s, lax.rem(p, NS)])

    def up(p, s, lo):
        c = lax.rem(p, HELD) * 2 + s
        src = xr if lo == 1 else ur
        return remote(src.at[c, pl.ds(lo * PIECE, (4 - lo) * PIECE)], ur.at[c, pl.ds(lo * PIECE, (4 - lo) * PIECE)], 1, p, s, up_dev)

    def down(p, s, hi):
        c = lax.rem(p, HELD) * 2 + s
        src = xr if hi == 3 else dr
        return remote(src.at[c, pl.ds(0, hi * PIECE)], dr.at[c, pl.ds(0, hi * PIECE)], 2, p, s, down_dev)

    def last(p, s):
        c = lax.rem(p, HELD) * 2 + s
        return remote(fb.at[c], yr.at[c], 3, p, s, b_dev[s])

    def keep(p, s):
        c = lax.rem(p, HELD) * 2 + s
        return pltpu.make_async_copy(yr.at[c], piece_of(p, s, z), loc.at[1, s, lax.rem(p, NS)])

    def piece_of(p, s, k):
        return out_ref.at[pl.ds(base(p, s) + a_pos[s] * HALF + k * PIECE, PIECE)]

    def back(p, s, hop, k, kind, dev):
        src = yr.at[lax.rem(p, HELD) * 2 + s] if hop == 0 else piece_of(p, s, k)
        return remote(src, piece_of(p, s, k), kind, p, s, dev)

    def up_back(p, s, hop):
        return back(p, s, hop, jnp.maximum(z - hop, 0), 5 + hop, up_dev)

    def down_back(p, s, hop):
        return back(p, s, hop, jnp.minimum(z + hop, 3), 8 + hop, down_dev)

    def first_back(p, s):
        rows = out_ref.at[pl.ds(base(p, s) + a_pos[s] * HALF, HALF)]
        return remote(rows, rows, 11, p, s, a_dev[s])

    def add(*terms):
        total = terms[0].astype(jnp.float32)
        for term in terms[1:]:
            total = total + term.astype(jnp.float32)
        return total.astype(jnp.bfloat16)

    def step_a(p):
        for s in range(2):
            first(p, s).start()
            mine(p, s).start()

    def step_b(p):
        for s in range(2):
            c = lax.rem(p, HELD) * 2 + s
            first(p, s).wait_recv()
            mine(p, s).wait()
            xr[c] = add(own[lax.rem(p, OWN) * 2 + s], xr[c])

            @pl.when(z == 0)
            def _():
                up(p, s, 1).start()

            @pl.when(z == 3)
            def _():
                down(p, s, 3).start()

    def step_c(p):
        for s in range(2):
            c = lax.rem(p, HELD) * 2 + s

            @pl.when(z == 1)
            def _():
                up(p, s, 1).wait_recv()
                ur[c, 2 * PIECE:] = add(ur[c, 2 * PIECE:], xr[c, 2 * PIECE:])
                up(p, s, 2).start()

            @pl.when(z == 2)
            def _():
                down(p, s, 3).wait_recv()
                dr[c, : 2 * PIECE] = add(dr[c, : 2 * PIECE], xr[c, : 2 * PIECE])
                down(p, s, 2).start()

    def step_d(p):
        for s in range(2):
            c = lax.rem(p, HELD) * 2 + s

            @pl.when(z == 2)
            def _():
                up(p, s, 2).wait_recv()
                ur[c, 3 * PIECE:] = add(ur[c, 3 * PIECE:], xr[c, 3 * PIECE:])
                up(p, s, 3).start()

            @pl.when(z == 1)
            def _():
                down(p, s, 2).wait_recv()
                dr[c, :PIECE] = add(dr[c, :PIECE], xr[c, :PIECE])
                down(p, s, 1).start()

    def step_e(p):
        for s in range(2):
            c = lax.rem(p, HELD) * 2 + s

            @pl.when(z == 0)
            def _():
                down(p, s, 1).wait_recv()
                up(p, s, 1).wait_send()
                fb[c] = add(xr[c, :PIECE], dr[c, :PIECE])

            @pl.when(z == 1)
            def _():
                fb[c] = add(xr[c, PIECE: 2 * PIECE], ur[c, PIECE: 2 * PIECE], dr[c, PIECE: 2 * PIECE])

            @pl.when(z == 2)
            def _():
                fb[c] = add(xr[c, 2 * PIECE: 3 * PIECE], ur[c, 2 * PIECE: 3 * PIECE], dr[c, 2 * PIECE: 3 * PIECE])

            @pl.when(z == 3)
            def _():
                up(p, s, 3).wait_recv()
                down(p, s, 3).wait_send()
                fb[c] = add(xr[c, 3 * PIECE:], ur[c, 3 * PIECE:])

        for s in range(2):
            last(p, s).start()

    def step_f(p):
        for s in range(2):
            c = lax.rem(p, HELD) * 2 + s

            @pl.when(z == 1)
            def _():
                up(p, s, 2).wait_send()
                down(p, s, 1).wait_send()

            @pl.when(z == 2)
            def _():
                up(p, s, 3).wait_send()
                down(p, s, 2).wait_send()

            last(p, s).wait()
            yr[c] = add(fb[c], yr[c])
            keep(p, s).start()

            @pl.when(has_up)
            def _():
                up_back(p, s, 0).start()

            @pl.when(has_down)
            def _():
                down_back(p, s, 0).start()

    def step_h(p):
        for s in range(2):
            @pl.when(has_down)
            def _():
                up_back(p, s, 0).wait_recv()

            @pl.when(has_down & has_up)
            def _():
                up_back(p, s, 1).start()

            @pl.when(has_up)
            def _():
                down_back(p, s, 0).wait_recv()

            @pl.when(has_down & has_up)
            def _():
                down_back(p, s, 1).start()

    def step_i(p):
        for s in range(2):
            @pl.when(has_up)
            def _():
                up_back(p, s, 0).wait_send()

            @pl.when(has_down)
            def _():
                down_back(p, s, 0).wait_send()

            @pl.when(z >= 2)
            def _():
                up_back(p, s, 1).wait_recv()

            @pl.when(z == 2)
            def _():
                up_back(p, s, 2).start()

            @pl.when(z <= 1)
            def _():
                down_back(p, s, 1).wait_recv()

            @pl.when(z == 1)
            def _():
                down_back(p, s, 2).start()

    def step_j(p):
        for s in range(2):
            @pl.when(z == 3)
            def _():
                up_back(p, s, 2).wait_recv()

            @pl.when(z == 0)
            def _():
                down_back(p, s, 2).wait_recv()

            keep(p, s).wait()
            first_back(p, s).start()

    def step_k(p):
        for s in range(2):
            first_back(p, s).wait()
            first(p, s).wait_send()

            @pl.when(has_up & has_down)
            def _():
                up_back(p, s, 1).wait_send()
                down_back(p, s, 1).wait_send()

            @pl.when(z == 2)
            def _():
                up_back(p, s, 2).wait_send()

            @pl.when(z == 1)
            def _():
                down_back(p, s, 2).wait_send()

    steps = {"a": step_a, "b": step_b, "c": step_c, "d": step_d, "e": step_e, "f": step_f, "h": step_h,
             "i": step_i, "j": step_j, "k": step_k}

    def part(t, k):
        for name, behind in PARTS[k]:
            p = t - behind
            if isinstance(p, int):
                if 0 <= p < PAIRS:
                    steps[name](jnp.int32(p))
            else:
                pl.when((p >= 0) & (p < PAIRS))(functools.partial(steps[name], p))

    return part, (c_dev, x_dev, y_dev, z1_dev, z2_dev)


HD = 32
GS = 256
IN = 1024
WIDE = 1024
HALFW = 512
NEG = -1e30
EPS = 1e-05
LOG2E = math.log2(math.e)
SCALE = HD ** -0.5
bf16 = jnp.bfloat16
f32 = jnp.float32
ANY = pl.BlockSpec(memory_space=pl.ANY)
VM = pl.BlockSpec(memory_space=pltpu.VMEM)
SM = pl.BlockSpec(memory_space=pltpu.SMEM)


def nn(left, right):
    return jnp.dot(left, right, preferred_element_type=f32)


def nt(left, right):
    return lax.dot_general(left, right, (((1,), (1,)), ((), ())), preferred_element_type=f32)


def lanes(start, size):
    return pl.ds(pl.multiple_of(start, 128), size)


def rows_at(start, size):
    return pl.ds(pl.multiple_of(start, size), size)


def head_block(tile):
    lane = lax.broadcasted_iota(jnp.int32, tile.shape, 1) // HD
    zero = jnp.zeros_like(tile)
    return jnp.concatenate([jnp.where(lane == j, tile, zero) for j in range(4)], axis=0)


def scores_of(keys, query_block, count):
    scores = nt(keys, query_block)
    if count is None:
        return scores
    place = lax.broadcasted_iota(jnp.int32, scores.shape, 0)
    return jnp.where(place < count, scores, NEG)


def attend(queries, keys, values, count):
    values_t = values.T
    scores = scores_of(keys, head_block(queries), count)
    top = jnp.max(scores, axis=0, keepdims=True)
    weights = jnp.exp2((scores - top) * (LOG2E * SCALE))
    total = jnp.sum(weights, axis=0, keepdims=True)
    low = weights.astype(bf16)
    log_total = top * (LOG2E * SCALE) + jnp.log2(total)
    inverse = 1.0 / total
    mixed, logs = [], []
    for j in range(4):
        span = slice(j * GS, (j + 1) * GS)
        mixed.append(nn(values_t[j * HD:(j + 1) * HD], low[:, span]) * inverse[:, span])
        logs.append(log_total[:, span])
    return jnp.concatenate(mixed, axis=0), jnp.concatenate(logs, axis=0)


def attend_back(queries, keys, values, grads, logs, count):
    keys_t = keys.T
    query_block = head_block(queries)
    grad_block = head_block(grads)
    grad_keys = grad_values = None
    grad_queries = []
    for j in range(4):
        own_query = query_block[j * GS:(j + 1) * GS]
        own_grad = grad_block[j * GS:(j + 1) * GS]
        weights = jnp.exp2(scores_of(keys, own_query, count) * (LOG2E * SCALE) - logs[j:j + 1])
        weighted = weights * nt(values, own_grad)
        inner = jnp.sum(weighted, axis=0, keepdims=True)
        grad_scores = (weighted - weights * inner).astype(bf16)
        value_part = nn(weights.astype(bf16), own_grad)
        key_part = nn(grad_scores, own_query)
        grad_values = value_part if j == 0 else grad_values + value_part
        grad_keys = key_part if j == 0 else grad_keys + key_part
        grad_queries.append(nn(keys_t[j * HD:(j + 1) * HD], grad_scores))
    return jnp.concatenate(grad_queries, axis=0) * SCALE, grad_keys * SCALE, grad_values


def centre(stream):
    centered = stream - jnp.mean(stream, axis=1, keepdims=True)
    inverse = lax.rsqrt(jnp.mean(centered * centered, axis=1, keepdims=True) + EPS)
    return centered * inverse, inverse


def normed(stream, gain, shift):
    return (centre(stream)[0] * gain + shift).astype(bf16)


def norm_back(stream, gain, upstream):
    xhat, inverse = centre(stream)
    scaled = upstream * gain
    along = upstream * xhat
    mean_scaled = jnp.mean(scaled, axis=1, keepdims=True)
    mean_along = jnp.mean(scaled * xhat, axis=1, keepdims=True)
    grad = inverse * (scaled - mean_scaled - xhat * mean_along)
    return grad, jnp.sum(along, axis=0, keepdims=True), jnp.sum(upstream, axis=0, keepdims=True)


def meet(partner):
    barrier = pltpu.get_barrier_semaphore()
    pl.semaphore_signal(barrier, inc=1, device_id=partner, device_id_type=MESH)
    pl.semaphore_wait(barrier, 1)


FWD_IN = (
    ("latents", VM), ("inputs", VM), ("counts", SM), ("cot", ANY),
    ("gain_latent", VM), ("shift_latent", VM), ("gain_input", VM), ("shift_input", VM),
    ("gain_self", VM), ("shift_self", VM), ("gain_mlp", VM), ("shift_mlp", VM),
    ("cq", ANY), ("ck", ANY), ("cv", ANY), ("co", ANY), ("sq", ANY), ("sk", ANY), ("sv", ANY), ("so", ANY),
    ("mi", ANY), ("mib", VM), ("mo", ANY), ("mob", VM),
)
FWD_OUT = (
    ("result", (GS, WIDE), bf16, VM),
    ("s1", (GS, WIDE), f32, VM), ("s2", (GS, WIDE), f32, VM),
    ("lnlT", (WIDE, 2 * GS), bf16, ANY), ("lniT", (WIDE, 2 * IN), bf16, ANY),
    ("snT", (WIDE, 2 * GS), bf16, ANY), ("mnT", (WIDE, 2 * GS), bf16, ANY),
    ("actT", (8, GS, 2 * GS), bf16, ANY), ("dg", (GS, 4096), bf16, ANY),
    ("xq", (GS, WIDE), bf16, ANY), ("xk", (IN, WIDE), bf16, ANY), ("xv", (IN, WIDE), bf16, ANY),
    ("xoT", (HALFW, 2 * GS), bf16, ANY), ("xl", (8, 4, GS), f32, VM),
    ("yq", (GS, WIDE), bf16, ANY), ("yk", (GS, WIDE), bf16, ANY), ("yv", (GS, WIDE), bf16, ANY),
    ("yoT", (HALFW, 2 * GS), bf16, ANY), ("yl", (8, 4, GS), f32, VM),
    ("cotp", (GS, WIDE), bf16, ANY),
    ("rin", (6, WIDE, HALFW), bf16, ANY), ("rout", (2, HALFW, WIDE), bf16, ANY),
    ("rmi", (WIDE, 2048), bf16, ANY), ("rmo", (2048, WIDE), bf16, ANY),
)
FWD_SCRATCH = (
    ("wx", (2, 3, WIDE, HALFW), bf16), ("wxo", (2, HALFW, WIDE), bf16),
    ("wy", (2, 3, WIDE, HALFW), bf16), ("wyo", (2, HALFW, WIDE), bf16),
    ("wmi", (2, WIDE, HALFW), bf16), ("wmo", (2, HALFW, WIDE), bf16),
    ("rbias", (1, 2048), f32),
    ("n", (GS, WIDE), bf16), ("ln", (IN, WIDE), bf16),
    ("t_l", (WIDE, GS), bf16), ("t_i", (WIDE, IN), bf16), ("t_s", (WIDE, GS), bf16), ("t_m", (WIDE, GS), bf16),
    ("q", (GS, WIDE), bf16), ("k", (IN, WIDE), bf16), ("v", (IN, WIDE), bf16), ("o", (GS, WIDE), bf16), ("oT", (WIDE, GS), bf16),
    ("q2", (GS, WIDE), bf16), ("k2", (GS, WIDE), bf16), ("v2", (GS, WIDE), bf16), ("o2", (GS, WIDE), bf16), ("oT2", (WIDE, GS), bf16),
    ("aT", (8, 2, GS, GS), bf16), ("dgs", (8, GS, HALFW), bf16), ("acc", (GS, WIDE), f32),
)


class Names:
    pass


def named(refs, *tables):
    out = Names()
    place = 0
    for table in tables:
        for entry in table:
            setattr(out, entry[0], refs[place])
            place += 1
    out.rest = refs[place:]
    return out


def forward_kernel(*refs):
    r = named(refs, FWD_IN, FWD_OUT, FWD_SCRATCH)
    send, recv, local = r.rest
    core = lax.axis_index("mp")
    partner = (lax.axis_index("dp"), 1 - core)
    meet(partner)
    sent, kept = [], []

    def push(src, dst):
        i = len(sent)
        copy = pltpu.make_async_remote_copy(
            src_ref=src, dst_ref=dst, send_sem=send.at[i], recv_sem=recv.at[i], device_id=partner, device_id_type=MESH)
        copy.start()
        sent.append(copy)
        return copy

    def fetch(src, dst):
        i = len(kept)
        copy = pltpu.make_async_copy(src, dst, local.at[i])
        copy.start()
        kept.append([copy, False])
        return i

    def ready(i):
        kept[i][0].wait()
        kept[i][1] = True

    got = [push(r.ck, r.rin.at[1]), push(r.cv, r.rin.at[2]), push(r.cq, r.rin.at[0]), push(r.co, r.rout.at[0])]
    got.append(push(r.mib, r.rbias))
    near = [fetch(w, r.wx.at[0, i]) for i, w in ((1, r.ck), (2, r.cv), (0, r.cq))] + [fetch(r.co, r.wxo.at[0])]

    r.n[...] = normed(r.latents[...].astype(f32), r.gain_latent[...], r.shift_latent[...])
    r.t_l[...] = r.n[...].T
    fetch(r.t_l, r.lnlT.at[:, pl.ds(0, GS)])
    gain, shift = r.gain_input[...], r.shift_input[...]

    def input_norm(b, _):
        span = rows_at(b * GS, GS)
        block = normed(r.inputs[span].astype(f32), gain, shift)
        r.ln[span] = block
        r.t_i[:, lanes(b * GS, GS)] = block.T
        return 0

    lax.fori_loop(0, IN // GS, input_norm, 0)
    fetch(r.t_i, r.lniT.at[:, pl.ds(0, IN)])
    for i in near[:3]:
        ready(i)

    def project_inputs(half):
        def block(b, _):
            span = rows_at(b * GS, GS)
            rows = r.ln[span]
            r.k[span, half * HALFW:(half + 1) * HALFW] = nn(rows, r.wx[half, 1]).astype(bf16)
            r.v[span, half * HALFW:(half + 1) * HALFW] = nn(rows, r.wx[half, 2]).astype(bf16)
            return 0

        lax.fori_loop(0, IN // GS, block, 0)
        r.q[:, half * HALFW:(half + 1) * HALFW] = nn(r.n[...], r.wx[half, 0]).astype(bf16)

    project_inputs(0)
    got += [push(w, r.rin.at[i]) for i, w in ((3, r.sq), (4, r.sk), (5, r.sv))] + [push(r.so, r.rout.at[1])]
    far = []
    for copy, src, dst in (
        (got[0], r.rin.at[1], r.wx.at[1, 1]), (got[1], r.rin.at[2], r.wx.at[1, 2]),
        (got[2], r.rin.at[0], r.wx.at[1, 0]), (got[3], r.rout.at[0], r.wxo.at[1])):
        copy.wait_recv()
        far.append(fetch(src, dst))
    near2 = [fetch(w, r.wy.at[0, i]) for i, w in enumerate((r.sq, r.sk, r.sv))] + [fetch(r.so, r.wyo.at[0])]
    count = r.counts[core]

    def attention(queries, keys, values, mixed, mixed_t, logs, limit, first):
        def group(g, _):
            at = lanes(g * 128, 128)
            out_t, log_total = attend(queries[:, at], keys[:, at], values[:, at], limit)
            out_t = out_t.astype(bf16)
            mixed_t[rows_at(g * 128, 128)] = out_t
            mixed[:, at] = out_t.T
            logs[g] = log_total
            return 0

        lax.fori_loop(first, first + 4, group, 0)

    attention(r.q, r.k, r.v, r.o, r.oT, r.xl, count, 0)
    got.append(push(r.mi, r.rmi))
    got.append(push(r.mo, r.rmo))
    for i in far[:3]:
        ready(i)
    project_inputs(1)
    fetch(r.q, r.xq)
    fetch(r.k, r.xk)
    fetch(r.v, r.xv)
    attention(r.q, r.k, r.v, r.o, r.oT, r.xl, count, 4)
    fetch(r.oT.at[pl.ds(0, HALFW)], r.xoT.at[:, pl.ds(0, GS)])
    push(r.oT.at[pl.ds(HALFW, HALFW)], r.xoT.at[:, pl.ds(GS, GS)])
    push(r.t_l, r.lnlT.at[:, pl.ds(GS, GS)])
    push(r.t_i, r.lniT.at[:, pl.ds(IN, IN)])
    push(r.cot, r.cotp)
    ready(near[3])
    ready(far[3])

    def out_project(mixed, weight):
        return nn(mixed[:, :HALFW], weight[0]) + nn(mixed[:, HALFW:], weight[1])

    r.s1[...] = r.latents[...].astype(f32) + out_project(r.o, r.wxo)
    r.n[...] = normed(r.s1[...], r.gain_self[...], r.shift_self[...])
    far2 = []
    for copy, src, dst in (
        (got[5], r.rin.at[3], r.wy.at[1, 0]), (got[6], r.rin.at[4], r.wy.at[1, 1]),
        (got[7], r.rin.at[5], r.wy.at[1, 2]), (got[8], r.rout.at[1], r.wyo.at[1])):
        copy.wait_recv()
        far2.append(fetch(src, dst))
    r.t_s[...] = r.n[...].T
    fetch(r.t_s, r.snT.at[:, pl.ds(0, GS)])
    push(r.t_s, r.snT.at[:, pl.ds(GS, GS)])
    for i in near2 + far2:
        ready(i)
    for half in range(2):
        at = slice(half * HALFW, (half + 1) * HALFW)
        for i, dst in enumerate((r.q2, r.k2, r.v2)):
            dst[:, at] = nn(r.n[...], r.wy[half, i]).astype(bf16)
    fetch(r.q2, r.yq)
    fetch(r.k2, r.yk)
    fetch(r.v2, r.yv)
    attention(r.q2, r.k2, r.v2, r.o2, r.oT2, r.yl, None, 0)
    attention(r.q2, r.k2, r.v2, r.o2, r.oT2, r.yl, None, 4)
    fetch(r.oT2.at[pl.ds(0, HALFW)], r.yoT.at[:, pl.ds(0, GS)])
    push(r.oT2.at[pl.ds(HALFW, HALFW)], r.yoT.at[:, pl.ds(GS, GS)])

    chunk_sem = len(kept)

    def chunk_copies(src_in, src_out, c, slot):
        at = lanes(c * HALFW, HALFW)
        return (
            pltpu.make_async_copy(src_in.at[:, at], r.wmi.at[slot], local.at[chunk_sem + slot]),
            pltpu.make_async_copy(src_out.at[rows_at(c * HALFW, HALFW)], r.wmo.at[slot], local.at[chunk_sem + 2 + slot]),
        )

    def start_chunk(n):
        slot = lax.rem(n, 2)

        @pl.when(n < 4)
        def _():
            for copy in chunk_copies(r.mi, r.mo, n, slot):
                copy.start()

        @pl.when(n >= 4)
        def _():
            for copy in chunk_copies(r.rmi, r.rmo, n - 4, slot):
                copy.start()

    start_chunk(jnp.int32(0))
    r.s2[...] = r.s1[...] + out_project(r.o2, r.wyo)
    r.n[...] = normed(r.s2[...], r.gain_mlp[...], r.shift_mlp[...])
    r.t_m[...] = r.n[...].T
    kept += [None] * 4
    fetch(r.t_m, r.mnT.at[:, pl.ds(0, GS)])
    push(r.t_m, r.mnT.at[:, pl.ds(GS, GS)])
    r.acc[...] = jnp.zeros((GS, WIDE), f32)
    for copy in (got[4], got[9], got[10]):
        copy.wait_recv()

    def feed(n, _):
        slot = lax.rem(n, 2)

        @pl.when(n + 1 < 8)
        def _():
            start_chunk(n + 1)

        for copy in chunk_copies(r.mi, r.mo, 0, slot):
            copy.wait()
        at = lanes(lax.rem(n, 4) * HALFW, HALFW)
        bias = jnp.where(n < 4, r.mib[:, at], r.rbias[:, at])
        hidden = nn(r.n[...], r.wmi[slot]) + bias
        area = 0.5 + 0.5 * lax.erf(hidden * (0.5 ** 0.5))
        density = jnp.exp(-0.5 * hidden * hidden) * ((2 * math.pi) ** -0.5)
        act = (hidden * area).astype(bf16)
        r.dgs[n] = (area + hidden * density).astype(bf16)
        r.aT[n] = act.T.reshape(2, GS, GS)
        r.acc[...] += nn(act, r.wmo[slot])
        return 0

    lax.fori_loop(0, 8, feed, 0)
    for c in range(4):
        fetch(r.aT.at[c], r.actT.at[pl.ds(2 * c, 2), :, pl.ds(0, GS)])
        push(r.aT.at[4 + c], r.actT.at[pl.ds(2 * c, 2), :, pl.ds(GS, GS)])
    for c in range(8):
        fetch(r.dgs.at[c], r.dg.at[:, pl.ds(c * HALFW, HALFW)])
    r.result[...] = (r.s2[...] + (r.acc[...] + r.mob[...])).astype(bf16)
    for i, entry in enumerate(kept):
        if entry is not None and not entry[1]:
            ready(i)
    seen = [id(c) for c in got]
    for copy in sent:
        copy.wait_send()
        if id(copy) not in seen:
            copy.wait_recv()


def forward(*args):
    return pl.pallas_call(
        forward_kernel,
        out_shape=[jax.ShapeDtypeStruct(shape, dtype) for _, shape, dtype, _ in FWD_OUT],
        in_specs=[spec for _, spec in FWD_IN],
        out_specs=[spec for _, _, _, spec in FWD_OUT],
        scratch_shapes=[pltpu.VMEM(shape, dtype) for _, shape, dtype in FWD_SCRATCH]
        + [pltpu.SemaphoreType.DMA((24,)), pltpu.SemaphoreType.DMA((24,)), pltpu.SemaphoreType.DMA((64,))],
        compiler_params=pltpu.CompilerParams(collective_id=1, has_side_effects=True, vmem_limit_bytes=60 << 20),
    )(*args)


BWD_IN = (
    ("latents", VM), ("inputs", ANY), ("counts", SM), ("cot", VM),
    ("gain_latent", VM), ("gain_input", VM), ("gain_self", VM), ("gain_mlp", VM),
    ("cq", ANY), ("ck", ANY), ("cv", ANY), ("co", ANY), ("sq", ANY), ("sk", ANY), ("sv", ANY), ("so", ANY),
    ("mi", ANY), ("mo", ANY),
) + tuple((name, VM if name in ("xl", "yl") else ANY) for name, _, _, _ in FWD_OUT[1:])
ROWS_OUT = 8192
BWD_OUT = (
    ("grads", (ROWS_OUT, WIDE), bf16, ANY), ("summed", (ROWS_OUT, WIDE), bf16, ANY), ("small", (SMALL, WIDE), f32, VM),
    ("grad_latents", (GS, WIDE), f32, VM), ("grad_inputs", (IN, WIDE), f32, ANY),
)
BWD_SCRATCH = (
    ("wy", (2, 3, WIDE, HALFW), bf16), ("wyo", (2, HALFW, WIDE), bf16), ("wxo", (2, HALFW, WIDE), bf16),
    ("wmi", (2, WIDE, HALFW), bf16), ("wmo", (2, HALFW, WIDE), bf16),
    ("mc", (2 * GS, WIDE), bf16), ("sc", (2 * GS, WIDE), bf16),
    ("dk", (8, GS, HALFW), bf16), ("dgs", (2, GS, HALFW), bf16),
    ("mT", (WIDE, 2 * GS), bf16), ("big", (4, HALFW, HALFW), bf16), ("bigr", (4, GS, HALFW), bf16),
    ("sT", (WIDE, 2 * GS), bf16), ("kv", (2, IN, WIDE), bf16),
    ("q", (GS, WIDE), bf16), ("oT", (HALFW, 2 * GS), bf16),
    ("qkv2", (3, GS, WIDE), bf16), ("oT2", (HALFW, 2 * GS), bf16),
    ("g", (GS, WIDE), bf16),
    ("dq", (2 * GS, HALFW), bf16), ("dqr", (GS, HALFW), bf16), ("dvr", (2, HALFW, HALFW), bf16),
    ("dq2", (3, 2 * GS, HALFW), bf16), ("dqr2", (3, GS, HALFW), bf16),
    ("wide", (2, GS, WIDE), f32),
    ("stage", (2, HALFW, WIDE), bf16), ("bsum", (8, HALFW), f32), ("sacc", (SMALL, WIDE), f32), ("sbuf", (5, SMALL, WIDE), f32),
)
ROW_MO, ROW_MI, ROW_SO, ROW_SQ, ROW_CO, ROW_CQ = 0, 2048, 4096, 4608, 6144, 6656


def backward_kernel(reduce, *refs):
    r = named(refs, BWD_IN, BWD_OUT, BWD_SCRATCH, REDUCE_SCRATCH if reduce else ())
    send, recv, local, stage_sem, chunk_sem, x_sem, *reduce_sems = r.rest
    core = lax.axis_index("mp")
    partner = (lax.axis_index("dp"), 1 - core)
    if reduce:
        part, small_devs = reducer(r, *reduce_sems[:3])
    else:
        meet(partner)
    sent, kept, staged = [], [], []
    state = {"tick": 0, "settled": 0}

    def settle(upto=None):
        upto = len(staged) if upto is None else upto
        for copy in staged[state["settled"]:upto]:
            copy.wait()
        state["settled"] = max(state["settled"], upto)

    def may_take(first, last):
        for n in range(first, last):
            if n % 3 == 0:
                assert min(n // 3 + AHEAD + 1, PAIRS) <= state["settled"]

    def tick(count=1):
        for _ in range(count):
            n = state["tick"]
            state["tick"] = n + 1
            if reduce:
                may_take(n, n + 1)
                part(n // 3, n % 3)

    def loop_tick(n):
        if reduce:
            for k in range(3):
                pl.when(lax.rem(n, 3) == k)(functools.partial(part, n // 3, k))

    def loop_ticks(count):
        n = state["tick"]
        state["tick"] = n + count
        if reduce:
            may_take(n, n + count)
        return n

    def push(src, dst):
        i = len(sent)
        copy = pltpu.make_async_remote_copy(
            src_ref=src, dst_ref=dst, send_sem=send.at[i], recv_sem=recv.at[i], device_id=partner, device_id_type=MESH)
        copy.start()
        sent.append(copy)
        return copy

    def fetch(src, dst):
        copy = pltpu.make_async_copy(src, dst, local.at[len(kept)])
        copy.start()
        kept.append(copy)
        return copy

    def stage(write, row):
        i = len(staged)
        slot = i % 2
        if i >= 2 and state["settled"] <= i - 2:
            staged[i - 2].wait()
            state["settled"] = i - 1
        write(r.stage.at[slot])
        copy = pltpu.make_async_copy(r.stage.at[slot], r.grads.at[pl.ds(row, HALFW)], stage_sem.at[slot])
        copy.start()
        staged.append(copy)

    early = [fetch(r.actT, r.dk), fetch(r.cotp, r.mc.at[pl.ds(GS, GS)])]

    def chunk_copies(src_in, src_out, c, n, slot):
        at = lanes(c * HALFW, HALFW)
        return (
            pltpu.make_async_copy(src_in.at[:, at], r.wmi.at[slot], chunk_sem.at[0, slot]),
            pltpu.make_async_copy(src_out.at[rows_at(c * HALFW, HALFW)], r.wmo.at[slot], chunk_sem.at[1, slot]),
            pltpu.make_async_copy(r.dg.at[:, lanes(n * HALFW, HALFW)], r.dgs.at[slot], chunk_sem.at[2, slot]),
        )

    def start_chunk(i):
        slot = lax.rem(i, 2)

        @pl.when(i < 4)
        def _():
            for copy in chunk_copies(r.rmi, r.rmo, i, 4 + i, slot):
                copy.start()

        @pl.when(i >= 4)
        def _():
            for copy in chunk_copies(r.mi, r.mo, i - 4, i - 4, slot):
                copy.start()

    start_chunk(jnp.int32(0))
    load_m = [fetch(r.mnT, r.mT), fetch(r.s2, r.wide.at[1])]
    load_y = [fetch(w, r.wy.at[0, i]) for i, w in enumerate((r.sq, r.sk, r.sv))]
    load_y += [fetch(r.rin.at[pl.ds(3, 3)], r.wy.at[1]), fetch(r.so, r.wyo.at[0]), fetch(r.rout.at[1], r.wyo.at[1])]
    load_y += [fetch(a, b) for a, b in ((r.yq, r.qkv2.at[0]), (r.yk, r.qkv2.at[1]), (r.yv, r.qkv2.at[2]), (r.yoT, r.oT2), (r.snT, r.sT))]
    r.mc[pl.ds(0, GS)] = r.cot[...]
    for copy in early:
        copy.wait()
    for m in range(4):
        def write(dst, m=m):
            dst[...] = nn(r.dk[2 * m:2 * m + 2].reshape(HALFW, 2 * GS), r.mc[...]).astype(bf16)

        stage(write, ROW_MO + m * HALFW)
    settle()
    if reduce:
        for t in range(-AHEAD, 0):
            part(t, 0)
    r.wide[0] = jnp.zeros((GS, WIDE), f32)

    def feed(i, ticks=None):
        slot = lax.rem(i, 2)

        @pl.when(i + 1 < 8)
        def _():
            start_chunk(i + 1)

        for copy in chunk_copies(r.mi, r.mo, 0, 0, slot):
            copy.wait()
        grad = (nt(r.cot[...], r.wmo[slot]) * r.dgs[slot].astype(f32)).astype(bf16)
        r.bsum[pl.ds(lax.rem(i + 4, 8), 1)] = jnp.sum(grad.astype(f32), axis=0, keepdims=True)

        @pl.when(i < 4)
        def _():
            r.bigr[lax.rem(i, 4)] = grad

        @pl.when(i >= 4)
        def _():
            r.big[lax.rem(i, 4), pl.ds(0, GS)] = grad

        r.wide[0] += nt(grad, r.wmi[slot])
        if ticks is not None:
            loop_tick(i + ticks)
        return 0

    lax.fori_loop(0, 4, lambda i, _: feed(i), 0)
    push_dh = push(r.bigr, r.big.at[:, pl.ds(GS, GS)])
    lax.fori_loop(4, 5, lambda i, _: feed(i), 0)
    first_tick = loop_ticks(3)
    lax.fori_loop(5, 8, lambda i, _: feed(i, first_tick - 5), 0)
    load_x = [fetch(r.co, r.wxo.at[0]), fetch(r.rout.at[0], r.wxo.at[1])]
    load_x += [fetch(a, b) for a, b in ((r.xq, r.q), (r.xk, r.kv.at[0]), (r.xv, r.kv.at[1]), (r.xoT, r.oT))]

    for copy in load_m:
        copy.wait()
    grad, along, plain = norm_back(r.wide[1], r.gain_mlp[...], r.wide[0])
    load_s = fetch(r.s1, r.wide.at[1])
    r.small[6:7] = along
    r.small[7:8] = plain
    r.wide[0] = r.cot[...].astype(f32) + grad
    r.sc[pl.ds(0, GS)] = r.wide[0].astype(bf16)
    push_c = push(r.sc.at[pl.ds(0, GS)], r.sc.at[pl.ds(GS, GS)])
    tick()
    push_dh.wait_recv()
    for c in range(4):
        def write(dst, c=c):
            dst[...] = jnp.concatenate(
                [nn(r.mT[c % 2 * HALFW:(c % 2 + 1) * HALFW], r.big[c // 2 * 2 + e]).astype(bf16)
                 for e in range(2)], axis=1)

        stage(write, ROW_MI + c * HALFW)
        settle(3 + c)
        tick()
    settle()
    load_l = fetch(r.lnlT, r.mT)

    def attention_back(queries, keys, values, logs, limit, take, own, other, hand_over, every):
        first = loop_ticks(8 // every)

        def group(i, _):
            g = lax.rem(i + 4, 8)
            at = lanes(g * 128, 128)
            to = lanes(lax.rem(i, 4) * 128, 128)
            pl.when(i == 4)(hand_over)
            grad_q, grad_k, grad_v = attend_back(queries[:, at], keys[:, at], values[:, at], r.g[:, at], logs[g], limit)
            grad_q, grad_k, grad_v = grad_q.astype(bf16).T, grad_k.astype(bf16), grad_v.astype(bf16)
            pl.when(i < 4)(lambda: take(other, to, grad_q, grad_k, grad_v))
            pl.when(i >= 4)(lambda: take(own, to, grad_q, grad_k, grad_v))
            if every == 1:
                loop_tick(first + i)
            else:
                pl.when(lax.rem(i, every) == every - 1)(lambda: loop_tick(first + i // every))
            return 0

        lax.fori_loop(0, 8, group, 0)

    def out_back(cots, weight):
        cot = cots[pl.ds(0, GS)]
        for half in range(2):
            r.g[:, half * HALFW:(half + 1) * HALFW] = nt(cot, weight[half]).astype(bf16)

    def grad_fold(left, right, row):
        def write(dst):
            for e in range(2):
                dst[:, e * HALFW:(e + 1) * HALFW] = nn(left[e * HALFW:(e + 1) * HALFW], right[...]).astype(bf16)

        stage(write, row)

    def crossing(i, src, dst):
        return pltpu.make_async_remote_copy(
            src_ref=src, dst_ref=dst, send_sem=send.at[i], recv_sem=recv.at[i], device_id=partner, device_id_type=MESH)

    push_y = crossing(12, r.dqr2, r.dq2.at[:, pl.ds(GS, GS)])
    push_x = [
        crossing(13, r.dqr, r.dq.at[pl.ds(GS, GS)]), crossing(14, r.bigr, r.dk.at[pl.ds(4, 4)]),
        crossing(15, r.dvr, r.big.at[pl.ds(2, 2)])]

    def take_y(dst, to, grad_q, grad_k, grad_v):
        for i, grad in enumerate((grad_q, grad_k, grad_v)):
            dst[i, pl.ds(0, GS), to] = grad

    def take_x(dst, to, grad_q, grad_k, grad_v):
        dst_q, dst_k, dst_v = dst
        dst_q[pl.ds(0, GS), to] = grad_q
        dst_k[pl.ds(0, 4), :, to] = grad_k.reshape(4, GS, 128)
        dst_v[pl.ds(0, 2), :, to] = grad_v.reshape(2, HALFW, 128)

    for copy in load_y:
        copy.wait()
    out_back(r.sc, r.wyo)
    tick()
    attention_back(r.qkv2.at[0], r.qkv2.at[1], r.qkv2.at[2], r.yl, None, take_y, r.dq2, r.dqr2, push_y.start, 1)
    push_c.wait_recv()

    def write_so(dst):
        dst[...] = nn(r.oT2[...], r.sc[...]).astype(bf16)

    stage(write_so, ROW_SO)
    tick()
    settle()
    load_s.wait()
    upstream = None
    for i in range(3):
        term = nt(r.dq2[i, :GS], r.wy[0, i]) + nt(r.dqr2[i], r.wy[1, i])
        upstream = term if upstream is None else upstream + term
    grad, along, plain = norm_back(r.wide[1], r.gain_self[...], upstream)
    r.small[4:5] = along
    r.small[5:6] = plain
    r.wide[0] += grad
    load_w = [fetch(w, r.wy.at[0, i]) for i, w in enumerate((r.cq, r.ck, r.cv))] + [fetch(r.rin.at[pl.ds(0, 3)], r.wy.at[1])]
    r.mc[pl.ds(0, GS)] = r.wide[0].astype(bf16)
    push_c2 = push(r.mc.at[pl.ds(0, GS)], r.mc.at[pl.ds(GS, GS)])
    push_y.wait_recv()
    tick()
    for i in range(3):
        grad_fold(r.sT, r.dq2.at[i], ROW_SQ + i * HALFW)
        settle(9 + i)
        tick()

    for copy in load_x:
        copy.wait()
    out_back(r.mc, r.wxo)
    tick()
    count = r.counts[core]
    push_dh.wait_send()
    push_c2.wait_recv()

    def write_co(dst):
        dst[...] = nn(r.oT[...], r.mc[...]).astype(bf16)

    stage(write_co, ROW_CO)
    tick()
    settle()

    def hand_over_x():
        for copy in push_x:
            copy.start()

    attention_back(r.q, r.kv.at[0], r.kv.at[1], r.xl, count, take_x, (r.dq, r.dk, r.big), (r.dqr, r.bigr, r.dvr), hand_over_x, 1)
    load_i = [fetch(r.lniT.at[:, pl.ds(0, IN)], r.kv.at[0]), fetch(r.lniT.at[:, pl.ds(IN, IN)], r.kv.at[1])]
    for copy in push_x:
        copy.wait_recv()
    load_l.wait()
    grad_fold(r.mT, r.dq, ROW_CQ)
    settle()
    tick()
    for copy in load_i:
        copy.wait()

    def tall(blocks):
        return blocks.reshape(IN, HALFW)

    def grad_tall(right, row):
        def write(dst):
            for e in range(2):
                at = slice(e * HALFW, (e + 1) * HALFW)
                dst[:, at] = (nn(r.kv[0, at], tall(right[0])) + nn(r.kv[1, at], tall(right[1]))).astype(bf16)

        stage(write, row)

    grad_tall((r.dk[:4], r.dk[4:]), ROW_CQ + HALFW)
    tick()
    grad_tall((r.big[:2], r.big[2:]), ROW_CQ + 2 * HALFW)
    settle()
    tick()
    for copy in load_w:
        copy.wait()
    upstream = nt(r.dq[:GS], r.wy[0, 0]) + nt(r.dqr[...], r.wy[1, 0])
    grad, along, plain = norm_back(r.latents[...].astype(f32), r.gain_latent[...], upstream)
    r.small[0:1] = along
    r.small[1:2] = plain
    r.grad_latents[...] = r.wide[0] + grad
    r.small[2:4] = jnp.zeros((2, WIDE), f32)

    def x_in(b):
        slot = lax.rem(b, 2)
        return pltpu.make_async_copy(r.inputs.at[rows_at(b * GS, GS)], r.qkv2.at[slot], x_sem.at[0, slot])

    def x_out(b):
        slot = lax.rem(b, 2)
        return pltpu.make_async_copy(r.wide.at[slot], r.grad_inputs.at[rows_at(b * GS, GS)], x_sem.at[1, slot])

    x_in(jnp.int32(0)).start()

    def input_back(b, _):
        slot = lax.rem(b, 2)

        @pl.when(b + 1 < IN // GS)
        def _():
            x_in(b + 1).start()

        x_in(b).wait()

        @pl.when(b >= 2)
        def _():
            x_out(b - 2).wait()

        half, at = b // 2, rows_at(lax.rem(b, 2) * GS, GS)
        up = nt(r.dk[b], r.wy[0, 1]) + nt(r.bigr[b], r.wy[1, 1]) + nt(r.big[half, at], r.wy[0, 2]) + nt(r.dvr[half, at], r.wy[1, 2])
        grad, along, plain = norm_back(r.qkv2[slot].astype(f32), r.gain_input[...], up)
        r.small[2:3] += along
        r.small[3:4] += plain
        r.wide[slot] = grad
        x_out(b).start()
        loop_tick(ticks + b)
        return 0

    ticks = loop_ticks(IN // GS)

    lax.fori_loop(0, IN // GS, input_back, 0)
    r.small[8:9] = jnp.sum(r.cot[...].astype(f32), axis=0, keepdims=True)
    r.small[13:16] = jnp.zeros((3, WIDE), f32)
    for i in range(4):
        half, odd = i // 2, i % 2 * 2
        mine = jnp.concatenate([r.bsum[odd:odd + 1], r.bsum[odd + 1:odd + 2]], axis=1)
        other = jnp.concatenate([r.bsum[odd + 4:odd + 5], r.bsum[odd + 5:odd + 6]], axis=1)
        r.small[9 + i:10 + i] = jnp.where(core == half, mine, other)
    x_out(jnp.int32(IN // GS - 2)).wait()
    x_out(jnp.int32(IN // GS - 1)).wait()
    for copy in (push_c, push_y, push_c2, *push_x):
        copy.wait_send()
    if not reduce:
        return
    tick(-state["tick"] % 3)
    begin = state["tick"] // 3
    small_send, small_recv = reduce_sems[3:]

    def small_copy(i):
        return pltpu.make_async_remote_copy(
            src_ref=r.sacc, dst_ref=r.sbuf.at[i], send_sem=small_send.at[i], recv_sem=small_recv.at[i],
            device_id=small_devs[i], device_id_type=MESH)

    r.sacc[...] = r.small[...]
    small_copy(0).start()

    def iteration(t, _):
        for k in range(3):
            part(t, k)
        for i in range(5):
            @pl.when(t == begin + i)
            def _():
                small_copy(i).wait()
                r.sacc[...] += r.sbuf[i]
                if i < 4:
                    small_copy(i + 1).start()
        return 0

    lax.fori_loop(begin, PAIRS + BEHIND, iteration, 0)
    r.small[...] = r.sacc[...]


def backward(reduce, *args):
    scratch = [pltpu.VMEM(shape, dtype) for _, shape, dtype in BWD_SCRATCH]
    sems = [(16,), (16,), (48,), (2,), (3, 2), (2, 2)]
    if reduce:
        scratch += [pltpu.VMEM(shape, bf16) for _, shape in REDUCE_SCRATCH]
        sems += [(12, 2, NS), (12, 2, NS), (2, 2, NS), (5,), (5,)]
    return pl.pallas_call(
        functools.partial(backward_kernel, reduce),
        out_shape=[jax.ShapeDtypeStruct(shape, dtype) for _, shape, dtype, _ in BWD_OUT],
        in_specs=[spec for _, spec in BWD_IN],
        out_specs=[spec for _, _, _, spec in BWD_OUT],
        scratch_shapes=scratch + [pltpu.SemaphoreType.DMA(shape) for shape in sems],
        compiler_params=pltpu.CompilerParams(
            collective_id=0 if reduce else 2, has_side_effects=True, vmem_limit_bytes=63 << 20),
    )(*args)


FINISH_OUT = (
    ("cq", (WIDE, HALFW)), ("ck", (WIDE, HALFW)), ("cv", (WIDE, HALFW)), ("co", (HALFW, WIDE)),
    ("sq", (WIDE, HALFW)), ("sk", (WIDE, HALFW)), ("sv", (WIDE, HALFW)), ("so", (HALFW, WIDE)),
    ("mi", (WIDE, 2048)), ("mo", (2048, WIDE)), ("gi", (IN, WIDE)), ("gl", (GS, WIDE)), ("result", (GS, WIDE)),
)


def finish_kernel(packed, gi, gl, result, *refs):
    r = named(refs, FINISH_OUT)
    low, high, mid_gi, mid_gl, mid_result, sem_in, sem_out, sem_copy = r.rest
    through = [
        [pltpu.make_async_copy(src, mid, sem_copy.at[0, i]), pltpu.make_async_copy(mid, dst, sem_copy.at[1, i])]
        for i, (src, mid, dst) in enumerate(((gi, mid_gi, r.gi), (gl, mid_gl, r.gl), (result, mid_result, r.result)))]
    plan = []
    for c in range(4):
        plan.append((ROW_MO + c * HALFW, [(r.mo.at[pl.ds(c * HALFW, HALFW)], 0, WIDE)]))
    for c in range(4):
        plan.append((ROW_MI + c * HALFW, [(r.mi.at[pl.ds(c % 2 * HALFW, HALFW), pl.ds(c // 2 * WIDE, WIDE)], 0, WIDE)]))
    for start, out, tall in ((ROW_SO, r.so, (r.sq, r.sk, r.sv)), (ROW_CO, r.co, (r.cq, r.ck, r.cv))):
        plan.append((start, [(out, 0, WIDE)]))
        for i, dst in enumerate(tall):
            plan.append((start + (i + 1) * HALFW, [(dst.at[pl.ds(e * HALFW, HALFW)], e * HALFW, HALFW) for e in range(2)]))
    slots = low.shape[0]

    def load(n):
        return pltpu.make_async_copy(packed.at[pl.ds(plan[n][0], HALFW)], low.at[n % slots], sem_in.at[n % slots])

    def stores(n):
        return [
            pltpu.make_async_copy(high.at[n % slots, :, pl.ds(at, size)], dst, sem_out.at[n % slots, e])
            for e, (dst, at, size) in enumerate(plan[n][1])]

    for n in range(slots - 1):
        load(n).start()
    for pair in through:
        pair[0].start()
    for n in range(len(plan)):
        if n + slots - 1 < len(plan):
            load(n + slots - 1).start()
        load(n).wait()
        if n >= slots:
            for copy in stores(n - slots):
                copy.wait()
        high[n % slots] = low[n % slots].astype(f32)
        for copy in stores(n):
            copy.start()
        if 4 <= n < 7:
            through[n - 4][0].wait()
            through[n - 4][1].start()
    for n in range(len(plan) - slots, len(plan)):
        for copy in stores(n):
            copy.wait()
    for pair in through:
        pair[1].wait()


def finish(*args):
    slots = 4
    return pl.pallas_call(
        finish_kernel,
        out_shape=[jax.ShapeDtypeStruct(shape, bf16 if name == "result" else f32) for name, shape in FINISH_OUT],
        in_specs=[ANY] * 4,
        out_specs=[ANY] * len(FINISH_OUT),
        scratch_shapes=[pltpu.VMEM((slots, HALFW, WIDE), bf16), pltpu.VMEM((slots, HALFW, WIDE), f32),
                        pltpu.VMEM((IN, WIDE), f32), pltpu.VMEM((GS, WIDE), f32), pltpu.VMEM((GS, WIDE), bf16)]
        + [pltpu.SemaphoreType.DMA((slots,)), pltpu.SemaphoreType.DMA((slots, 2)), pltpu.SemaphoreType.DMA((2, 3))],
        compiler_params=pltpu.CompilerParams(vmem_limit_bytes=60 << 20),
    )(*args)


def local(
    latents, inputs, valid_counts, cotangent,
    gain_latent, shift_latent, gain_input, shift_input,
    cross_query, cross_key, cross_value, cross_out,
    gain_self, shift_self,
    self_query, self_key, self_value, self_out,
    gain_mlp, shift_mlp,
    mlp_in, mlp_in_bias, mlp_out, mlp_out_bias,
):
    core = lax.axis_index("mp")

    def row(vector):
        return vector.reshape(1, -1)

    weights = (cross_query, cross_key, cross_value, cross_out, self_query, self_key, self_value, self_out)
    result, *kept = forward(
        latents, inputs, valid_counts, cotangent,
        row(gain_latent), row(shift_latent), row(gain_input), row(shift_input),
        row(gain_self), row(shift_self), row(gain_mlp), row(shift_mlp),
        *weights, mlp_in, row(mlp_in_bias), mlp_out, row(mlp_out_bias))
    reduce = lax.axis_size("dp") == 16
    grads, packed, small, grad_latents, grad_inputs = backward(
        reduce, latents, inputs, valid_counts, cotangent,
        row(gain_latent), row(gain_input), row(gain_self), row(gain_mlp),
        *weights, mlp_in, mlp_out, *kept)
    if not reduce:
        packed, small = lax.psum(grads, "dp"), lax.psum(small, ("dp", "mp"))

    cq, ck, cv, co, sq, sk, sv, so, mi, mo, grad_inputs, grad_latents, result = finish(
        packed, grad_inputs, grad_latents, result)
    half = mlp_in_bias.shape[0]
    hidden_bias = lax.dynamic_slice_in_dim(small[9:13].reshape(-1), core * half, half)
    return (
        result, grad_latents, grad_inputs, *(small[i] for i in range(4)), cq, ck, cv, co,
        small[4], small[5], sq, sk, sv, so, small[6], small[7], mi, hidden_bias, mo, small[8],
    )


def solution(mesh):
    return jax.shard_map(
        local,
        mesh=mesh,
        in_specs=(
            P(("dp", "mp"), None),
            P(("dp", "mp"), None),
            P("dp"),
            P(("dp", "mp"), None),
            P(),
            P(),
            P(),
            P(),
            P(None, "mp"),
            P(None, "mp"),
            P(None, "mp"),
            P("mp", None),
            P(),
            P(),
            P(None, "mp"),
            P(None, "mp"),
            P(None, "mp"),
            P("mp", None),
            P(),
            P(),
            P(None, "mp"),
            P("mp"),
            P("mp", None),
            P(),
        ),
        out_specs=(
            P(("dp", "mp"), None),
            P(("dp", "mp"), None),
            P(("dp", "mp"), None),
            P(),
            P(),
            P(),
            P(),
            P(None, "mp"),
            P(None, "mp"),
            P(None, "mp"),
            P("mp", None),
            P(),
            P(),
            P(None, "mp"),
            P(None, "mp"),
            P(None, "mp"),
            P("mp", None),
            P(),
            P(),
            P(None, "mp"),
            P("mp"),
            P("mp", None),
            P(),
        ),
        check_vma=False,
    )
```

```python
import functools
import math

import jax
import jax.numpy as jnp
from jax import lax
from jax.experimental import pallas as pl
from jax.experimental.pallas import tpu as pltpu
from jax.sharding import PartitionSpec as P

MESH = pl.DeviceIdType.MESH
NS = 16
CH = 256
HALF = CH // 2
PIECE = HALF // 4
SUB = PIECE // 2
SMALL = 16
PARTS = (
    (("a", -2), ("b", 0), ("d", 2)),
    (("j", 6), ("i", 5), ("c", 1)),
    (("h", 4), ("f", 3), ("e", 2), ("k", 8)),
)
BEHIND = 8
AHEAD = 2
OWN = 3
HELD = 6
PAIRS = 16
REDUCE_SCRATCH = (
    ("own", (2 * OWN, HALF, 1024)), ("xr", (2 * HELD, HALF, 1024)), ("ur", (2 * HELD, HALF, 1024)), ("dr", (2 * HELD, HALF, 1024)),
    ("fb", (2 * HELD, PIECE, 1024)), ("yr", (2 * HELD, PIECE, 1024)),
)


def reducer(r, send, recv, loc):
    g_ref, out_ref, own, xr, ur, dr, fb, yr = r.grads, r.summed, r.own, r.xr, r.ur, r.dr, r.fb, r.yr
    dp = lax.axis_index("dp")
    core = lax.axis_index("mp")
    z = dp // 4
    px = lax.rem(dp, 2)
    py = lax.rem(dp // 2, 2)
    x_dev = (dp + 1 - 2 * px, core)
    y_dev = (dp + 2 - 4 * py, core)
    c_dev = (dp, 1 - core)
    up_dev = (dp + 4, core)
    down_dev = (dp - 4, core)
    z1_dev = (dp + 4 - 8 * lax.rem(z, 2), core)
    z2_dev = (dp + 8 - 16 * (z // 2), core)
    has_up = z < 3
    has_down = z > 0

    barrier = pltpu.get_barrier_semaphore()
    for dev in (x_dev, y_dev, c_dev, z2_dev):
        pl.semaphore_signal(barrier, inc=1, device_id=dev, device_id_type=MESH)

    @pl.when(has_up)
    def _():
        pl.semaphore_signal(barrier, inc=1, device_id=up_dev, device_id_type=MESH)

    @pl.when(has_down)
    def _():
        pl.semaphore_signal(barrier, inc=1, device_id=down_dev, device_id_type=MESH)

    def met():
        pl.semaphore_wait(barrier, 4 + has_up.astype(jnp.int32) + has_down.astype(jnp.int32))

    def remote(src, dst, kind, p, s, dev):
        slot = lax.rem(p, NS)
        return pltpu.make_async_remote_copy(
            src_ref=src, dst_ref=dst, send_sem=send.at[kind, s, slot], recv_sem=recv.at[kind, s, slot],
            device_id=dev, device_id_type=MESH)

    a_pos = (px, py)
    b_pos = (py, px)
    a_dev = (x_dev, y_dev)
    b_dev = (y_dev, x_dev)

    def base(p, s):
        return (2 * p + s) * CH

    def first(p, s):
        c = lax.rem(p, HELD) * 2 + s
        return remote(g_ref.at[pl.ds(base(p, s) + (1 - a_pos[s]) * HALF, HALF)], xr.at[c], 0, p, s, a_dev[s])

    def mine(p, s):
        c = lax.rem(p, OWN) * 2 + s
        return pltpu.make_async_copy(g_ref.at[pl.ds(base(p, s) + a_pos[s] * HALF, HALF)], own.at[c], loc.at[0, s, lax.rem(p, NS)])

    def up(p, s, lo):
        c = lax.rem(p, HELD) * 2 + s
        src = xr if lo == 1 else ur
        return remote(src.at[c, pl.ds(lo * PIECE, (4 - lo) * PIECE)], ur.at[c, pl.ds(lo * PIECE, (4 - lo) * PIECE)], 1, p, s, up_dev)

    def down(p, s, hi):
        c = lax.rem(p, HELD) * 2 + s
        src = xr if hi == 3 else dr
        return remote(src.at[c, pl.ds(0, hi * PIECE)], dr.at[c, pl.ds(0, hi * PIECE)], 2, p, s, down_dev)

    def last(p, s):
        c = lax.rem(p, HELD) * 2 + s
        return remote(fb.at[c], yr.at[c], 3, p, s, b_dev[s])

    def keep(p, s):
        c = lax.rem(p, HELD) * 2 + s
        return pltpu.make_async_copy(yr.at[c], piece_of(p, s, z), loc.at[1, s, lax.rem(p, NS)])

    def piece_of(p, s, k):
        return out_ref.at[pl.ds(base(p, s) + a_pos[s] * HALF + k * PIECE, PIECE)]

    def back(p, s, hop, k, kind, dev):
        src = yr.at[lax.rem(p, HELD) * 2 + s] if hop == 0 else piece_of(p, s, k)
        return remote(src, piece_of(p, s, k), kind, p, s, dev)

    def up_back(p, s, hop):
        return back(p, s, hop, jnp.maximum(z - hop, 0), 5 + hop, up_dev)

    def down_back(p, s, hop):
        return back(p, s, hop, jnp.minimum(z + hop, 3), 8 + hop, down_dev)

    def first_back(p, s):
        rows = out_ref.at[pl.ds(base(p, s) + a_pos[s] * HALF, HALF)]
        return remote(rows, rows, 11, p, s, a_dev[s])

    def add(*terms):
        total = terms[0].astype(jnp.float32)
        for term in terms[1:]:
            total = total + term.astype(jnp.float32)
        return total.astype(jnp.bfloat16)

    def step_a(p):
        for s in range(2):
            first(p, s).start()
            mine(p, s).start()

    def step_b(p):
        for s in range(2):
            c = lax.rem(p, HELD) * 2 + s
            first(p, s).wait_recv()
            mine(p, s).wait()
            xr[c] = add(own[lax.rem(p, OWN) * 2 + s], xr[c])

            @pl.when(z == 0)
            def _():
                up(p, s, 1).start()

            @pl.when(z == 3)
            def _():
                down(p, s, 3).start()

    def step_c(p):
        for s in range(2):
            c = lax.rem(p, HELD) * 2 + s

            @pl.when(z == 1)
            def _():
                up(p, s, 1).wait_recv()
                ur[c, 2 * PIECE:] = add(ur[c, 2 * PIECE:], xr[c, 2 * PIECE:])
                up(p, s, 2).start()

            @pl.when(z == 2)
            def _():
                down(p, s, 3).wait_recv()
                dr[c, : 2 * PIECE] = add(dr[c, : 2 * PIECE], xr[c, : 2 * PIECE])
                down(p, s, 2).start()

    def step_d(p):
        for s in range(2):
            c = lax.rem(p, HELD) * 2 + s

            @pl.when(z == 2)
            def _():
                up(p, s, 2).wait_recv()
                ur[c, 3 * PIECE:] = add(ur[c, 3 * PIECE:], xr[c, 3 * PIECE:])
                up(p, s, 3).start()

            @pl.when(z == 1)
            def _():
                down(p, s, 2).wait_recv()
                dr[c, :PIECE] = add(dr[c, :PIECE], xr[c, :PIECE])
                down(p, s, 1).start()

    def step_e(p):
        for s in range(2):
            c = lax.rem(p, HELD) * 2 + s

            @pl.when(z == 0)
            def _():
                down(p, s, 1).wait_recv()
                up(p, s, 1).wait_send()
                fb[c] = add(xr[c, :PIECE], dr[c, :PIECE])

            @pl.when(z == 1)
            def _():
                fb[c] = add(xr[c, PIECE: 2 * PIECE], ur[c, PIECE: 2 * PIECE], dr[c, PIECE: 2 * PIECE])

            @pl.when(z == 2)
            def _():
                fb[c] = add(xr[c, 2 * PIECE: 3 * PIECE], ur[c, 2 * PIECE: 3 * PIECE], dr[c, 2 * PIECE: 3 * PIECE])

            @pl.when(z == 3)
            def _():
                up(p, s, 3).wait_recv()
                down(p, s, 3).wait_send()
                fb[c] = add(xr[c, 3 * PIECE:], ur[c, 3 * PIECE:])

        for s in range(2):
            last(p, s).start()

    def step_f(p):
        for s in range(2):
            c = lax.rem(p, HELD) * 2 + s

            @pl.when(z == 1)
            def _():
                up(p, s, 2).wait_send()
                down(p, s, 1).wait_send()

            @pl.when(z == 2)
            def _():
                up(p, s, 3).wait_send()
                down(p, s, 2).wait_send()

            last(p, s).wait()
            yr[c] = add(fb[c], yr[c])
            keep(p, s).start()

            @pl.when(has_up)
            def _():
                up_back(p, s, 0).start()

            @pl.when(has_down)
            def _():
                down_back(p, s, 0).start()

    def step_h(p):
        for s in range(2):
            @pl.when(has_down)
            def _():
                up_back(p, s, 0).wait_recv()

            @pl.when(has_down & has_up)
            def _():
                up_back(p, s, 1).start()

            @pl.when(has_up)
            def _():
                down_back(p, s, 0).wait_recv()

            @pl.when(has_down & has_up)
            def _():
                down_back(p, s, 1).start()

    def step_i(p):
        for s in range(2):
            @pl.when(has_up)
            def _():
                up_back(p, s, 0).wait_send()

            @pl.when(has_down)
            def _():
                down_back(p, s, 0).wait_send()

            @pl.when(z >= 2)
            def _():
                up_back(p, s, 1).wait_recv()

            @pl.when(z == 2)
            def _():
                up_back(p, s, 2).start()

            @pl.when(z <= 1)
            def _():
                down_back(p, s, 1).wait_recv()

            @pl.when(z == 1)
            def _():
                down_back(p, s, 2).start()

    def step_j(p):
        for s in range(2):
            @pl.when(z == 3)
            def _():
                up_back(p, s, 2).wait_recv()

            @pl.when(z == 0)
            def _():
                down_back(p, s, 2).wait_recv()

            keep(p, s).wait()
            first_back(p, s).start()

    def step_k(p):
        for s in range(2):
            first_back(p, s).wait()
            first(p, s).wait_send()

            @pl.when(has_up & has_down)
            def _():
                up_back(p, s, 1).wait_send()
                down_back(p, s, 1).wait_send()

            @pl.when(z == 2)
            def _():
                up_back(p, s, 2).wait_send()

            @pl.when(z == 1)
            def _():
                down_back(p, s, 2).wait_send()

    steps = {"a": step_a, "b": step_b, "c": step_c, "d": step_d, "e": step_e, "f": step_f, "h": step_h,
             "i": step_i, "j": step_j, "k": step_k}

    def part(t, k):
        for name, behind in PARTS[k]:
            p = t - behind
            if isinstance(p, int):
                if 0 <= p < PAIRS:
                    steps[name](jnp.int32(p))
            else:
                pl.when((p >= 0) & (p < PAIRS))(functools.partial(steps[name], p))

    return met, part, (c_dev, x_dev, y_dev, z1_dev, z2_dev)


HD = 32
GS = 256
IN = 1024
WIDE = 1024
HALFW = 512
NEG = -1e30
EPS = 1e-05
LOG2E = math.log2(math.e)
SCALE = HD ** -0.5
bf16 = jnp.bfloat16
f32 = jnp.float32
ANY = pl.BlockSpec(memory_space=pl.ANY)
VM = pl.BlockSpec(memory_space=pltpu.VMEM)
SM = pl.BlockSpec(memory_space=pltpu.SMEM)


def nn(left, right):
    return jnp.dot(left, right, preferred_element_type=f32)


def nt(left, right):
    return lax.dot_general(left, right, (((1,), (1,)), ((), ())), preferred_element_type=f32)


def lanes(start, size):
    return pl.ds(pl.multiple_of(start, 128), size)


def rows_at(start, size):
    return pl.ds(pl.multiple_of(start, size), size)


def head_block(tile):
    lane = lax.broadcasted_iota(jnp.int32, tile.shape, 1) // HD
    zero = jnp.zeros_like(tile)
    return jnp.concatenate([jnp.where(lane == j, tile, zero) for j in range(4)], axis=0)


def scores_of(keys, query_block, count):
    scores = nt(keys, query_block)
    if count is None:
        return scores
    place = lax.broadcasted_iota(jnp.int32, scores.shape, 0)
    return jnp.where(place < count, scores, NEG)


def attend(queries, keys, values, count):
    values_t = values.T
    scores = scores_of(keys, head_block(queries), count)
    top = jnp.max(scores, axis=0, keepdims=True)
    weights = jnp.exp2((scores - top) * (LOG2E * SCALE))
    total = jnp.sum(weights, axis=0, keepdims=True)
    low = weights.astype(bf16)
    log_total = top * (LOG2E * SCALE) + jnp.log2(total)
    inverse = 1.0 / total
    mixed, logs = [], []
    for j in range(4):
        span = slice(j * GS, (j + 1) * GS)
        mixed.append(nn(values_t[j * HD:(j + 1) * HD], low[:, span]) * inverse[:, span])
        logs.append(log_total[:, span])
    return jnp.concatenate(mixed, axis=0), jnp.concatenate(logs, axis=0)


def attend_back(queries, keys, values, grads, logs, count):
    keys_t = keys.T
    query_block = head_block(queries)
    grad_block = head_block(grads)
    grad_keys = grad_values = None
    grad_queries = []
    for j in range(4):
        own_query = query_block[j * GS:(j + 1) * GS]
        own_grad = grad_block[j * GS:(j + 1) * GS]
        weights = jnp.exp2(scores_of(keys, own_query, count) * (LOG2E * SCALE) - logs[j:j + 1])
        weighted = weights * nt(values, own_grad)
        inner = jnp.sum(weighted, axis=0, keepdims=True)
        grad_scores = (weighted - weights * inner).astype(bf16)
        value_part = nn(weights.astype(bf16), own_grad)
        key_part = nn(grad_scores, own_query)
        grad_values = value_part if j == 0 else grad_values + value_part
        grad_keys = key_part if j == 0 else grad_keys + key_part
        grad_queries.append(nn(keys_t[j * HD:(j + 1) * HD], grad_scores))
    return jnp.concatenate(grad_queries, axis=0) * SCALE, grad_keys * SCALE, grad_values


def centre(stream):
    centered = stream - jnp.mean(stream, axis=1, keepdims=True)
    inverse = lax.rsqrt(jnp.mean(centered * centered, axis=1, keepdims=True) + EPS)
    return centered * inverse, inverse


def normed(stream, gain, shift):
    return (centre(stream)[0] * gain + shift).astype(bf16)


def norm_back(stream, gain, upstream):
    xhat, inverse = centre(stream)
    scaled = upstream * gain
    along = upstream * xhat
    mean_scaled = jnp.mean(scaled, axis=1, keepdims=True)
    mean_along = jnp.mean(scaled * xhat, axis=1, keepdims=True)
    grad = inverse * (scaled - mean_scaled - xhat * mean_along)
    return grad, jnp.sum(along, axis=0, keepdims=True), jnp.sum(upstream, axis=0, keepdims=True)


def meet(partner):
    barrier = pltpu.get_barrier_semaphore()
    pl.semaphore_signal(barrier, inc=1, device_id=partner, device_id_type=MESH)
    return lambda: pl.semaphore_wait(barrier, 1)


FWD_IN = (
    ("latents", VM), ("inputs", VM), ("counts", SM), ("cot", ANY),
    ("gain_latent", VM), ("shift_latent", VM), ("gain_input", VM), ("shift_input", VM),
    ("gain_self", VM), ("shift_self", VM), ("gain_mlp", VM), ("shift_mlp", VM),
    ("cq", ANY), ("ck", ANY), ("cv", ANY), ("co", ANY), ("sq", ANY), ("sk", ANY), ("sv", ANY), ("so", ANY),
    ("mi", ANY), ("mib", VM), ("mo", ANY), ("mob", VM),
)
FWD_OUT = (
    ("result", (GS, WIDE), bf16, VM),
    ("s1", (GS, WIDE), f32, VM), ("s2", (GS, WIDE), f32, VM),
    ("lnlT", (WIDE, 2 * GS), bf16, ANY), ("lniT", (WIDE, 2 * IN), bf16, ANY),
    ("snT", (WIDE, 2 * GS), bf16, ANY), ("mnT", (WIDE, 2 * GS), bf16, ANY),
    ("actT", (8, GS, 2 * GS), bf16, ANY), ("dg", (8, GS, HALFW), bf16, ANY),
    ("xq", (GS, WIDE), bf16, ANY), ("xk", (IN, WIDE), bf16, ANY), ("xv", (IN, WIDE), bf16, ANY),
    ("xoT", (HALFW, 2 * GS), bf16, ANY), ("xl", (8, 4, GS), f32, VM),
    ("yq", (GS, WIDE), bf16, ANY), ("yk", (GS, WIDE), bf16, ANY), ("yv", (GS, WIDE), bf16, ANY),
    ("yoT", (HALFW, 2 * GS), bf16, ANY), ("yl", (8, 4, GS), f32, VM),
    ("cotp", (GS, WIDE), bf16, ANY),
    ("rin", (6, WIDE, HALFW), bf16, ANY), ("rout", (2, HALFW, WIDE), bf16, ANY),
)
FWD_SCRATCH = (
    ("wx", (2, 3, WIDE, HALFW), bf16), ("wxo", (2, HALFW, WIDE), bf16),
    ("wy", (2, 3, WIDE, HALFW), bf16), ("wyo", (2, HALFW, WIDE), bf16),
    ("wmi", (2, WIDE, HALFW), bf16), ("wmo", (2, HALFW, WIDE), bf16),
    ("n", (GS, WIDE), bf16), ("ln", (IN, WIDE), bf16),
    ("t_l", (WIDE, GS), bf16), ("t_i", (WIDE, IN), bf16), ("t_s", (WIDE, GS), bf16), ("t_m", (WIDE, GS), bf16),
    ("q", (GS, WIDE), bf16), ("k", (IN, WIDE), bf16), ("v", (IN, WIDE), bf16), ("o", (GS, WIDE), bf16), ("oT", (WIDE, GS), bf16),
    ("q2", (GS, WIDE), bf16), ("k2", (GS, WIDE), bf16), ("v2", (GS, WIDE), bf16), ("o2", (GS, WIDE), bf16), ("oT2", (WIDE, GS), bf16),
    ("aT", (8, 2, GS, GS), bf16), ("dgs", (8, GS, HALFW), bf16), ("acc", (2, GS, WIDE), f32),
    ("np", (GS, WIDE), bf16), ("part", (2, GS, WIDE), bf16),
)


class Names:
    pass


def named(refs, *tables):
    out = Names()
    place = 0
    for table in tables:
        for entry in table:
            setattr(out, entry[0], refs[place])
            place += 1
    out.rest = refs[place:]
    return out


def forward_kernel(*refs):
    r = named(refs, FWD_IN, FWD_OUT, FWD_SCRATCH)
    send, recv, local = r.rest
    core = lax.axis_index("mp")
    partner = (lax.axis_index("dp"), 1 - core)
    met = meet(partner)
    sent, kept = [], []

    def push(src, dst):
        i = len(sent)
        copy = pltpu.make_async_remote_copy(
            src_ref=src, dst_ref=dst, send_sem=send.at[i], recv_sem=recv.at[i], device_id=partner, device_id_type=MESH)
        copy.start()
        sent.append(copy)
        return copy

    def fetch(src, dst):
        i = len(kept)
        copy = pltpu.make_async_copy(src, dst, local.at[i])
        copy.start()
        kept.append([copy, False])
        return i

    def ready(i):
        kept[i][0].wait()
        kept[i][1] = True

    near = [fetch(w, r.wx.at[0, i]) for i, w in ((1, r.ck), (2, r.cv), (0, r.cq))] + [fetch(r.co, r.wxo.at[0])]

    met()
    got = [push(r.ck, r.rin.at[1]), push(r.cv, r.rin.at[2]), push(r.cq, r.rin.at[0]), push(r.co, r.rout.at[0])]
    r.n[...] = normed(r.latents[...].astype(f32), r.gain_latent[...], r.shift_latent[...])
    r.t_l[...] = r.n[...].T
    fetch(r.t_l, r.lnlT.at[:, pl.ds(0, GS)])
    gain, shift = r.gain_input[...], r.shift_input[...]

    def input_norm(b, _):
        span = rows_at(b * GS, GS)
        block = normed(r.inputs[span].astype(f32), gain, shift)
        r.ln[span] = block
        r.t_i[:, lanes(b * GS, GS)] = block.T
        return 0

    lax.fori_loop(0, IN // GS, input_norm, 0)
    fetch(r.t_i, r.lniT.at[:, pl.ds(0, IN)])
    for i in near[:3]:
        ready(i)

    def project_inputs(half):
        def block(b, _):
            span = rows_at(b * GS, GS)
            rows = r.ln[span]
            r.k[span, half * HALFW:(half + 1) * HALFW] = nn(rows, r.wx[half, 1]).astype(bf16)
            r.v[span, half * HALFW:(half + 1) * HALFW] = nn(rows, r.wx[half, 2]).astype(bf16)
            return 0

        lax.fori_loop(0, IN // GS, block, 0)
        r.q[:, half * HALFW:(half + 1) * HALFW] = nn(r.n[...], r.wx[half, 0]).astype(bf16)

    project_inputs(0)
    got += [push(w, r.rin.at[i]) for i, w in ((3, r.sq), (4, r.sk), (5, r.sv))] + [push(r.so, r.rout.at[1])]
    near2 = [fetch(w, r.wy.at[0, i]) for i, w in enumerate((r.sq, r.sk, r.sv))] + [fetch(r.so, r.wyo.at[0])]
    count = r.counts[core]

    def attention(queries, keys, values, mixed, mixed_t, logs, limit, first, last):
        def group(g, _):
            at = lanes(g * 128, 128)
            out_t, log_total = attend(queries[:, at], keys[:, at], values[:, at], limit)
            out_t = out_t.astype(bf16)
            mixed_t[rows_at(g * 128, 128)] = out_t
            mixed[:, at] = out_t.T
            logs[g] = log_total
            return 0

        lax.fori_loop(first, last, group, 0)

    attention(r.q, r.k, r.v, r.o, r.oT, r.xl, count, 0, 3)
    far = []
    for copy, src, dst in (
        (got[0], r.rin.at[1], r.wx.at[1, 1]), (got[1], r.rin.at[2], r.wx.at[1, 2]),
        (got[2], r.rin.at[0], r.wx.at[1, 0]), (got[3], r.rout.at[0], r.wxo.at[1])):
        copy.wait_recv()
        far.append(fetch(src, dst))
    attention(r.q, r.k, r.v, r.o, r.oT, r.xl, count, 3, 4)
    for i in far[:3]:
        ready(i)
    project_inputs(1)
    fetch(r.q, r.xq)
    fetch(r.k, r.xk)
    fetch(r.v, r.xv)
    attention(r.q, r.k, r.v, r.o, r.oT, r.xl, count, 4, 8)
    fetch(r.oT.at[pl.ds(0, HALFW)], r.xoT.at[:, pl.ds(0, GS)])
    push(r.oT.at[pl.ds(HALFW, HALFW)], r.xoT.at[:, pl.ds(GS, GS)])
    push(r.t_l, r.lnlT.at[:, pl.ds(GS, GS)])
    push(r.t_i, r.lniT.at[:, pl.ds(IN, IN)])
    push(r.cot, r.cotp)
    ready(near[3])
    ready(far[3])

    def out_project(mixed, weight):
        return nn(mixed[:, :HALFW], weight[0]) + nn(mixed[:, HALFW:], weight[1])

    r.s1[...] = r.latents[...].astype(f32) + out_project(r.o, r.wxo)
    r.n[...] = normed(r.s1[...], r.gain_self[...], r.shift_self[...])
    far2 = []
    for copy, src, dst in (
        (got[4], r.rin.at[3], r.wy.at[1, 0]), (got[5], r.rin.at[4], r.wy.at[1, 1]),
        (got[6], r.rin.at[5], r.wy.at[1, 2]), (got[7], r.rout.at[1], r.wyo.at[1])):
        copy.wait_recv()
        far2.append(fetch(src, dst))
    r.t_s[...] = r.n[...].T
    fetch(r.t_s, r.snT.at[:, pl.ds(0, GS)])
    push(r.t_s, r.snT.at[:, pl.ds(GS, GS)])
    for i in near2 + far2:
        ready(i)
    for half in range(2):
        at = slice(half * HALFW, (half + 1) * HALFW)
        for i, dst in enumerate((r.q2, r.k2, r.v2)):
            dst[:, at] = nn(r.n[...], r.wy[half, i]).astype(bf16)
    fetch(r.q2, r.yq)
    fetch(r.k2, r.yk)
    fetch(r.v2, r.yv)
    attention(r.q2, r.k2, r.v2, r.o2, r.oT2, r.yl, None, 0, 8)
    fetch(r.oT2.at[pl.ds(0, HALFW)], r.yoT.at[:, pl.ds(0, GS)])
    push(r.oT2.at[pl.ds(HALFW, HALFW)], r.yoT.at[:, pl.ds(GS, GS)])

    chunk_sem = len(kept)

    def chunk_copies(n, slot):
        c = lax.rem(n, 4)
        return (
            pltpu.make_async_copy(r.mi.at[:, lanes(c * HALFW, HALFW)], r.wmi.at[slot], local.at[chunk_sem + slot]),
            pltpu.make_async_copy(r.mo.at[rows_at(c * HALFW, HALFW)], r.wmo.at[slot], local.at[chunk_sem + 2 + slot]),
        )

    for copy in chunk_copies(jnp.int32(0), 0):
        copy.start()
    kept += [None] * 4
    r.s2[...] = r.s1[...] + out_project(r.o2, r.wyo)
    r.n[...] = normed(r.s2[...], r.gain_mlp[...], r.shift_mlp[...])
    met_rows = push(r.n, r.np)
    r.t_m[...] = r.n[...].T
    fetch(r.t_m, r.mnT.at[:, pl.ds(0, GS)])
    push(r.t_m, r.mnT.at[:, pl.ds(GS, GS)])
    r.acc[...] = jnp.zeros((2, GS, WIDE), f32)

    def feed(rows, who):
        def step(n, _):
            slot = lax.rem(n, 2)

            @pl.when(n + 1 < 8)
            def _():
                for copy in chunk_copies(n + 1, 1 - slot):
                    copy.start()

            for copy in chunk_copies(n, slot):
                copy.wait()
            hidden = nn(rows[...], r.wmi[slot]) + r.mib[:, lanes(lax.rem(n, 4) * HALFW, HALFW)]
            area = 0.5 + 0.5 * lax.erf(hidden * (0.5 ** 0.5))
            density = jnp.exp(-0.5 * hidden * hidden) * ((2 * math.pi) ** -0.5)
            act = (hidden * area).astype(bf16)
            r.dgs[n] = (area + hidden * density).astype(bf16)
            r.aT[n] = act.T.reshape(2, GS, GS)
            r.acc[who] += nn(act, r.wmo[slot])
            return 0

        lax.fori_loop(4 * who, 4 * who + 4, step, 0)

    feed(r.n, 0)
    met_rows.wait_recv()
    got.append(met_rows)
    feed(r.np, 1)
    r.part[0] = r.acc[1].astype(bf16)
    met_part = push(r.part.at[0], r.part.at[1])
    got.append(met_part)
    for c in range(4):
        for who in range(2):
            fetch(r.aT.at[4 * who + c], r.actT.at[pl.ds(2 * c, 2), :, pl.ds(who * GS, GS)])
    fetch(r.dgs, r.dg)
    met_part.wait_recv()
    r.result[...] = (r.s2[...] + (r.acc[0] + r.part[1].astype(f32) + r.mob[...])).astype(bf16)
    for i, entry in enumerate(kept):
        if entry is not None and not entry[1]:
            ready(i)
    seen = [id(c) for c in got]
    for copy in sent:
        copy.wait_send()
        if id(copy) not in seen:
            copy.wait_recv()


def forward(*args):
    return pl.pallas_call(
        forward_kernel,
        out_shape=[jax.ShapeDtypeStruct(shape, dtype) for _, shape, dtype, _ in FWD_OUT],
        in_specs=[spec for _, spec in FWD_IN],
        out_specs=[spec for _, _, _, spec in FWD_OUT],
        scratch_shapes=[pltpu.VMEM(shape, dtype) for _, shape, dtype in FWD_SCRATCH]
        + [pltpu.SemaphoreType.DMA((24,)), pltpu.SemaphoreType.DMA((24,)), pltpu.SemaphoreType.DMA((64,))],
        compiler_params=pltpu.CompilerParams(collective_id=1, has_side_effects=True, vmem_limit_bytes=60 << 20),
    )(*args)


BWD_IN = (
    ("latents", VM), ("inputs", ANY), ("counts", SM), ("cot", VM),
    ("gain_latent", VM), ("gain_input", VM), ("gain_self", VM), ("gain_mlp", VM),
    ("cq", ANY), ("ck", ANY), ("cv", ANY), ("co", ANY), ("sq", ANY), ("sk", ANY), ("sv", ANY), ("so", ANY),
    ("mi", ANY), ("mo", ANY),
) + tuple((name, VM if name in ("xl", "yl") else ANY) for name, _, _, _ in FWD_OUT[1:])
ROWS_OUT = 8192
BWD_OUT = (
    ("grads", (ROWS_OUT, WIDE), bf16, ANY), ("summed", (ROWS_OUT, WIDE), bf16, ANY), ("small", (SMALL, WIDE), f32, VM),
    ("grad_latents", (GS, WIDE), f32, VM), ("grad_inputs", (IN, WIDE), f32, ANY),
)
BWD_SCRATCH = (
    ("wy", (2, 3, WIDE, HALFW), bf16), ("wyo", (2, HALFW, WIDE), bf16), ("wxo", (2, HALFW, WIDE), bf16),
    ("wmi", (2, WIDE, HALFW), bf16), ("wmo", (2, HALFW, WIDE), bf16),
    ("mc", (2 * GS, WIDE), bf16), ("sc", (2 * GS, WIDE), bf16),
    ("dk", (8, GS, HALFW), bf16), ("dgs", (2, GS, HALFW), bf16),
    ("mT", (WIDE, 2 * GS), bf16), ("big", (4, HALFW, HALFW), bf16), ("bigr", (4, GS, HALFW), bf16),
    ("sT", (WIDE, 2 * GS), bf16), ("kv", (2, IN, WIDE), bf16),
    ("q", (GS, WIDE), bf16), ("oT", (HALFW, 2 * GS), bf16),
    ("qkv2", (3, GS, WIDE), bf16), ("oT2", (HALFW, 2 * GS), bf16),
    ("g", (GS, WIDE), bf16), ("up", (GS, WIDE), bf16),
    ("dq", (2 * GS, HALFW), bf16), ("dqr", (GS, HALFW), bf16), ("dvr", (2, HALFW, HALFW), bf16),
    ("dq2", (3, 2 * GS, HALFW), bf16), ("dqr2", (3, GS, HALFW), bf16),
    ("wide", (2, GS, WIDE), f32),
    ("stage", (2, HALFW, WIDE), bf16), ("bsum", (4, HALFW), f32), ("sacc", (SMALL, WIDE), f32), ("sbuf", (5, SMALL, WIDE), f32),
)
ROW_MO, ROW_MI, ROW_SO, ROW_SQ, ROW_CO, ROW_CQ = 0, 2048, 4096, 4608, 6144, 6656


def backward_kernel(reduce, *refs):
    r = named(refs, BWD_IN, BWD_OUT, BWD_SCRATCH, REDUCE_SCRATCH if reduce else ())
    send, recv, local, stage_sem, chunk_sem, x_sem, *reduce_sems = r.rest
    core = lax.axis_index("mp")
    partner = (lax.axis_index("dp"), 1 - core)
    if reduce:
        met, part, small_devs = reducer(r, *reduce_sems[:3])
    else:
        met = meet(partner)
    sent, kept, staged = [], [], []
    state = {"tick": 0, "settled": 0}

    def settle(upto=None):
        upto = len(staged) if upto is None else upto
        for copy in staged[state["settled"]:upto]:
            copy.wait()
        state["settled"] = max(state["settled"], upto)

    def may_take(first, last):
        for n in range(first, last):
            if n % 3 == 0:
                assert min(n // 3 + AHEAD + 1, PAIRS) <= state["settled"]

    def tick(count=1):
        for _ in range(count):
            n = state["tick"]
            state["tick"] = n + 1
            if reduce:
                may_take(n, n + 1)
                part(n // 3, n % 3)

    def loop_tick(n):
        if reduce:
            for k in range(3):
                pl.when(lax.rem(n, 3) == k)(functools.partial(part, n // 3, k))

    def loop_ticks(count):
        n = state["tick"]
        state["tick"] = n + count
        if reduce:
            may_take(n, n + count)
        return n

    def push(src, dst):
        i = len(sent)
        copy = pltpu.make_async_remote_copy(
            src_ref=src, dst_ref=dst, send_sem=send.at[i], recv_sem=recv.at[i], device_id=partner, device_id_type=MESH)
        copy.start()
        sent.append(copy)
        return copy

    def fetch(src, dst):
        copy = pltpu.make_async_copy(src, dst, local.at[len(kept)])
        copy.start()
        kept.append(copy)
        return copy

    def stage(write, row):
        i = len(staged)
        slot = i % 2
        if i >= 2 and state["settled"] <= i - 2:
            staged[i - 2].wait()
            state["settled"] = i - 1
        write(r.stage.at[slot])
        copy = pltpu.make_async_copy(r.stage.at[slot], r.grads.at[pl.ds(row, HALFW)], stage_sem.at[slot])
        copy.start()
        staged.append(copy)

    early = [fetch(r.actT, r.dk), fetch(r.cotp, r.mc.at[pl.ds(GS, GS)])]

    def chunk_copies(i, slot):
        c = lax.rem(i, 4)
        return (
            pltpu.make_async_copy(r.mi.at[:, lanes(c * HALFW, HALFW)], r.wmi.at[slot], chunk_sem.at[0, slot]),
            pltpu.make_async_copy(r.mo.at[rows_at(c * HALFW, HALFW)], r.wmo.at[slot], chunk_sem.at[1, slot]),
            pltpu.make_async_copy(r.dg.at[lax.rem(i + 4, 8)], r.dgs.at[slot], chunk_sem.at[2, slot]),
        )

    for copy in chunk_copies(jnp.int32(0), 0):
        copy.start()
    load_m = [fetch(r.mnT, r.mT)]
    load_y = [fetch(w, r.wy.at[0, i]) for i, w in enumerate((r.sq, r.sk, r.sv))]
    load_y += [fetch(r.rin.at[pl.ds(3, 3)], r.wy.at[1]), fetch(r.so, r.wyo.at[0]), fetch(r.rout.at[1], r.wyo.at[1])]
    load_y += [fetch(a, b) for a, b in ((r.yq, r.qkv2.at[0]), (r.yk, r.qkv2.at[1]), (r.yv, r.qkv2.at[2]), (r.yoT, r.oT2), (r.snT, r.sT))]
    r.mc[pl.ds(0, GS)] = r.cot[...]
    for copy in early:
        copy.wait()
    for m in range(4):
        def write(dst, m=m):
            dst[...] = nn(r.dk[2 * m:2 * m + 2].reshape(HALFW, 2 * GS), r.mc[...]).astype(bf16)

        stage(write, ROW_MO + m * HALFW)
        if m == 0:
            met()
        elif reduce and m <= AHEAD:
            settle(m)
            part(m - 1 - AHEAD, 0)
    settle()
    r.wide[...] = jnp.zeros((2, GS, WIDE), f32)

    def feed(i, who, ticks=None):
        slot = lax.rem(i, 2)

        @pl.when(i + 1 < 8)
        def _():
            for copy in chunk_copies(i + 1, 1 - slot):
                copy.start()

        for copy in chunk_copies(i, slot):
            copy.wait()
        grad = (nt(r.mc[who * GS:(who + 1) * GS], r.wmo[slot]) * r.dgs[slot].astype(f32)).astype(bf16)
        total = jnp.sum(grad.astype(f32), axis=0, keepdims=True)
        c = lax.rem(i, 4)
        if who:
            r.bsum[pl.ds(c, 1)] = total
        else:
            r.bsum[pl.ds(c, 1)] += total
        r.big[c, who * GS:(who + 1) * GS] = grad
        r.wide[who] += nt(grad, r.wmi[slot])
        if ticks is not None:
            loop_tick(i + ticks)
        return 0

    lax.fori_loop(0, 4, lambda i, _: feed(i, 1), 0)
    r.g[...] = r.wide[1].astype(bf16)
    push_u = push(r.g, r.up)
    load_m.append(fetch(r.s2, r.wide.at[1]))
    lax.fori_loop(4, 5, lambda i, _: feed(i, 0), 0)
    first_tick = loop_ticks(3)
    lax.fori_loop(5, 8, lambda i, _: feed(i, 0, first_tick - 5), 0)
    load_x = [fetch(r.co, r.wxo.at[0]), fetch(r.rout.at[0], r.wxo.at[1])]
    load_x += [fetch(a, b) for a, b in ((r.xq, r.q), (r.xk, r.kv.at[0]), (r.xv, r.kv.at[1]), (r.xoT, r.oT))]

    for copy in load_m:
        copy.wait()
    push_u.wait()
    grad, along, plain = norm_back(r.wide[1], r.gain_mlp[...], r.wide[0] + r.up[...].astype(f32))
    load_s = fetch(r.s1, r.wide.at[1])
    r.small[6:7] = along
    r.small[7:8] = plain
    r.wide[0] = r.cot[...].astype(f32) + grad
    r.sc[pl.ds(0, GS)] = r.wide[0].astype(bf16)
    push_c = push(r.sc.at[pl.ds(0, GS)], r.sc.at[pl.ds(GS, GS)])
    tick()
    for c in range(4):
        def write(dst, c=c):
            dst[...] = jnp.concatenate(
                [nn(r.mT[c % 2 * HALFW:(c % 2 + 1) * HALFW], r.big[c // 2 * 2 + e]).astype(bf16)
                 for e in range(2)], axis=1)

        stage(write, ROW_MI + c * HALFW)
        settle(3 + c)
        tick()
    settle()
    load_l = fetch(r.lnlT, r.mT)

    def attention_back(queries, keys, values, logs, limit, take, own, other, hand_over, every):
        first = loop_ticks(8 // every)

        def group(i, _):
            g = lax.rem(i + 4, 8)
            at = lanes(g * 128, 128)
            to = lanes(lax.rem(i, 4) * 128, 128)
            pl.when(i == 4)(hand_over)
            grad_q, grad_k, grad_v = attend_back(queries[:, at], keys[:, at], values[:, at], r.g[:, at], logs[g], limit)
            grad_q, grad_k, grad_v = grad_q.astype(bf16).T, grad_k.astype(bf16), grad_v.astype(bf16)
            pl.when(i < 4)(lambda: take(other, to, grad_q, grad_k, grad_v))
            pl.when(i >= 4)(lambda: take(own, to, grad_q, grad_k, grad_v))
            if every == 1:
                loop_tick(first + i)
            else:
                pl.when(lax.rem(i, every) == every - 1)(lambda: loop_tick(first + i // every))
            return 0

        lax.fori_loop(0, 8, group, 0)

    def out_back(cots, weight):
        cot = cots[pl.ds(0, GS)]
        for half in range(2):
            r.g[:, half * HALFW:(half + 1) * HALFW] = nt(cot, weight[half]).astype(bf16)

    def grad_fold(left, right, row):
        def write(dst):
            for e in range(2):
                dst[:, e * HALFW:(e + 1) * HALFW] = nn(left[e * HALFW:(e + 1) * HALFW], right[...]).astype(bf16)

        stage(write, row)

    def crossing(i, src, dst):
        return pltpu.make_async_remote_copy(
            src_ref=src, dst_ref=dst, send_sem=send.at[i], recv_sem=recv.at[i], device_id=partner, device_id_type=MESH)

    push_y = crossing(12, r.dqr2, r.dq2.at[:, pl.ds(GS, GS)])
    push_x = [
        crossing(13, r.dqr, r.dq.at[pl.ds(GS, GS)]), crossing(14, r.bigr, r.dk.at[pl.ds(4, 4)]),
        crossing(15, r.dvr, r.big.at[pl.ds(2, 2)])]

    def take_y(dst, to, grad_q, grad_k, grad_v):
        for i, grad in enumerate((grad_q, grad_k, grad_v)):
            dst[i, pl.ds(0, GS), to] = grad

    def take_x(dst, to, grad_q, grad_k, grad_v):
        dst_q, dst_k, dst_v = dst
        dst_q[pl.ds(0, GS), to] = grad_q
        dst_k[pl.ds(0, 4), :, to] = grad_k.reshape(4, GS, 128)
        dst_v[pl.ds(0, 2), :, to] = grad_v.reshape(2, HALFW, 128)

    for copy in load_y:
        copy.wait()
    out_back(r.sc, r.wyo)
    tick()
    attention_back(r.qkv2.at[0], r.qkv2.at[1], r.qkv2.at[2], r.yl, None, take_y, r.dq2, r.dqr2, push_y.start, 1)
    push_c.wait_recv()

    def write_so(dst):
        dst[...] = nn(r.oT2[...], r.sc[...]).astype(bf16)

    stage(write_so, ROW_SO)
    tick()
    settle()
    load_s.wait()
    upstream = None
    for i in range(3):
        term = nt(r.dq2[i, :GS], r.wy[0, i]) + nt(r.dqr2[i], r.wy[1, i])
        upstream = term if upstream is None else upstream + term
    grad, along, plain = norm_back(r.wide[1], r.gain_self[...], upstream)
    r.small[4:5] = along
    r.small[5:6] = plain
    r.wide[0] += grad
    load_w = [fetch(w, r.wy.at[0, i]) for i, w in enumerate((r.cq, r.ck, r.cv))] + [fetch(r.rin.at[pl.ds(0, 3)], r.wy.at[1])]
    r.mc[pl.ds(0, GS)] = r.wide[0].astype(bf16)
    push_c2 = push(r.mc.at[pl.ds(0, GS)], r.mc.at[pl.ds(GS, GS)])
    push_y.wait_recv()
    tick()
    for i in range(3):
        grad_fold(r.sT, r.dq2.at[i], ROW_SQ + i * HALFW)
        settle(9 + i)
        tick()

    for copy in load_x:
        copy.wait()
    out_back(r.mc, r.wxo)
    tick()
    count = r.counts[core]
    push_c2.wait_recv()

    def write_co(dst):
        dst[...] = nn(r.oT[...], r.mc[...]).astype(bf16)

    stage(write_co, ROW_CO)
    tick()
    settle()

    def hand_over_x():
        for copy in push_x:
            copy.start()

    attention_back(r.q, r.kv.at[0], r.kv.at[1], r.xl, count, take_x, (r.dq, r.dk, r.big), (r.dqr, r.bigr, r.dvr), hand_over_x, 1)
    load_i = [fetch(r.lniT.at[:, pl.ds(0, IN)], r.kv.at[0]), fetch(r.lniT.at[:, pl.ds(IN, IN)], r.kv.at[1])]
    for copy in push_x:
        copy.wait_recv()
    load_l.wait()
    grad_fold(r.mT, r.dq, ROW_CQ)
    settle()
    tick()
    for copy in load_i:
        copy.wait()

    def tall(blocks):
        return blocks.reshape(IN, HALFW)

    def grad_tall(right, row):
        def write(dst):
            for e in range(2):
                at = slice(e * HALFW, (e + 1) * HALFW)
                dst[:, at] = (nn(r.kv[0, at], tall(right[0])) + nn(r.kv[1, at], tall(right[1]))).astype(bf16)

        stage(write, row)

    grad_tall((r.dk[:4], r.dk[4:]), ROW_CQ + HALFW)
    tick()
    grad_tall((r.big[:2], r.big[2:]), ROW_CQ + 2 * HALFW)
    settle()
    tick()
    for copy in load_w:
        copy.wait()
    upstream = nt(r.dq[:GS], r.wy[0, 0]) + nt(r.dqr[...], r.wy[1, 0])
    grad, along, plain = norm_back(r.latents[...].astype(f32), r.gain_latent[...], upstream)
    r.small[0:1] = along
    r.small[1:2] = plain
    r.grad_latents[...] = r.wide[0] + grad
    r.small[2:4] = jnp.zeros((2, WIDE), f32)

    def x_in(b):
        slot = lax.rem(b, 2)
        return pltpu.make_async_copy(r.inputs.at[rows_at(b * GS, GS)], r.qkv2.at[slot], x_sem.at[0, slot])

    def x_out(b):
        slot = lax.rem(b, 2)
        return pltpu.make_async_copy(r.wide.at[slot], r.grad_inputs.at[rows_at(b * GS, GS)], x_sem.at[1, slot])

    x_in(jnp.int32(0)).start()

    def input_back(b, _):
        slot = lax.rem(b, 2)

        @pl.when(b + 1 < IN // GS)
        def _():
            x_in(b + 1).start()

        x_in(b).wait()

        @pl.when(b >= 2)
        def _():
            x_out(b - 2).wait()

        half, at = b // 2, rows_at(lax.rem(b, 2) * GS, GS)
        up = nt(r.dk[b], r.wy[0, 1]) + nt(r.bigr[b], r.wy[1, 1]) + nt(r.big[half, at], r.wy[0, 2]) + nt(r.dvr[half, at], r.wy[1, 2])
        grad, along, plain = norm_back(r.qkv2[slot].astype(f32), r.gain_input[...], up)
        r.small[2:3] += along
        r.small[3:4] += plain
        r.wide[slot] = grad
        x_out(b).start()
        loop_tick(ticks + b)
        return 0

    ticks = loop_ticks(IN // GS)

    lax.fori_loop(0, IN // GS, input_back, 0)
    r.small[8:9] = jnp.sum(r.cot[...].astype(f32), axis=0, keepdims=True)
    r.small[13:16] = jnp.zeros((3, WIDE), f32)
    for i in range(4):
        half, odd = i // 2, i % 2 * 2
        mine = jnp.concatenate([r.bsum[odd:odd + 1], r.bsum[odd + 1:odd + 2]], axis=1)
        r.small[9 + i:10 + i] = jnp.where(core == half, mine, 0.0)
    x_out(jnp.int32(IN // GS - 2)).wait()
    x_out(jnp.int32(IN // GS - 1)).wait()
    for copy in (push_c, push_y, push_c2, *push_x):
        copy.wait_send()
    if not reduce:
        return
    tick(-state["tick"] % 3)
    begin = state["tick"] // 3
    small_send, small_recv = reduce_sems[3:]

    def small_copy(i):
        return pltpu.make_async_remote_copy(
            src_ref=r.sacc, dst_ref=r.sbuf.at[i], send_sem=small_send.at[i], recv_sem=small_recv.at[i],
            device_id=small_devs[i], device_id_type=MESH)

    r.sacc[...] = r.small[...]
    small_copy(0).start()

    def iteration(t, _):
        for k in range(3):
            part(t, k)
        for i in range(5):
            @pl.when(t == begin + i)
            def _():
                small_copy(i).wait()
                r.sacc[...] += r.sbuf[i]
                if i < 4:
                    small_copy(i + 1).start()
        return 0

    lax.fori_loop(begin, PAIRS + BEHIND, iteration, 0)
    r.small[...] = r.sacc[...]


def backward(reduce, *args):
    scratch = [pltpu.VMEM(shape, dtype) for _, shape, dtype in BWD_SCRATCH]
    sems = [(16,), (16,), (48,), (2,), (3, 2), (2, 2)]
    if reduce:
        scratch += [pltpu.VMEM(shape, bf16) for _, shape in REDUCE_SCRATCH]
        sems += [(12, 2, NS), (12, 2, NS), (2, 2, NS), (5,), (5,)]
    return pl.pallas_call(
        functools.partial(backward_kernel, reduce),
        out_shape=[jax.ShapeDtypeStruct(shape, dtype) for _, shape, dtype, _ in BWD_OUT],
        in_specs=[spec for _, spec in BWD_IN],
        out_specs=[spec for _, _, _, spec in BWD_OUT],
        scratch_shapes=scratch + [pltpu.SemaphoreType.DMA(shape) for shape in sems],
        compiler_params=pltpu.CompilerParams(
            collective_id=0 if reduce else 2, has_side_effects=True, vmem_limit_bytes=63 << 20),
    )(*args)


FINISH_OUT = (
    ("cq", (WIDE, HALFW)), ("ck", (WIDE, HALFW)), ("cv", (WIDE, HALFW)), ("co", (HALFW, WIDE)),
    ("sq", (WIDE, HALFW)), ("sk", (WIDE, HALFW)), ("sv", (WIDE, HALFW)), ("so", (HALFW, WIDE)),
    ("mi", (WIDE, 2048)), ("mo", (2048, WIDE)), ("gi", (IN, WIDE)), ("gl", (GS, WIDE)), ("result", (GS, WIDE)),
)


def finish_kernel(packed, gi, gl, result, *refs):
    r = named(refs, FINISH_OUT)
    low, high, mid_gi, mid_gl, mid_result, sem_in, sem_out, sem_copy = r.rest
    through = [
        [pltpu.make_async_copy(src, mid, sem_copy.at[0, i]), pltpu.make_async_copy(mid, dst, sem_copy.at[1, i])]
        for i, (src, mid, dst) in enumerate(((gi, mid_gi, r.gi), (gl, mid_gl, r.gl), (result, mid_result, r.result)))]
    plan = []
    for c in range(4):
        plan.append((ROW_MO + c * HALFW, [(r.mo.at[pl.ds(c * HALFW, HALFW)], 0, WIDE)]))
    for c in range(4):
        plan.append((ROW_MI + c * HALFW, [(r.mi.at[pl.ds(c % 2 * HALFW, HALFW), pl.ds(c // 2 * WIDE, WIDE)], 0, WIDE)]))
    for start, out, tall in ((ROW_SO, r.so, (r.sq, r.sk, r.sv)), (ROW_CO, r.co, (r.cq, r.ck, r.cv))):
        plan.append((start, [(out, 0, WIDE)]))
        for i, dst in enumerate(tall):
            plan.append((start + (i + 1) * HALFW, [(dst.at[pl.ds(e * HALFW, HALFW)], e * HALFW, HALFW) for e in range(2)]))
    slots = low.shape[0]

    def load(n):
        return pltpu.make_async_copy(packed.at[pl.ds(plan[n][0], HALFW)], low.at[n % slots], sem_in.at[n % slots])

    def stores(n):
        return [
            pltpu.make_async_copy(high.at[n % slots, :, pl.ds(at, size)], dst, sem_out.at[n % slots, e])
            for e, (dst, at, size) in enumerate(plan[n][1])]

    for n in range(slots - 1):
        load(n).start()
    for pair in through:
        pair[0].start()
    for n in range(len(plan)):
        if n + slots - 1 < len(plan):
            load(n + slots - 1).start()
        load(n).wait()
        if n >= slots:
            for copy in stores(n - slots):
                copy.wait()
        high[n % slots] = low[n % slots].astype(f32)
        for copy in stores(n):
            copy.start()
        if 4 <= n < 7:
            through[n - 4][0].wait()
            through[n - 4][1].start()
    for n in range(len(plan) - slots, len(plan)):
        for copy in stores(n):
            copy.wait()
    for pair in through:
        pair[1].wait()


def finish(*args):
    slots = 4
    return pl.pallas_call(
        finish_kernel,
        out_shape=[jax.ShapeDtypeStruct(shape, bf16 if name == "result" else f32) for name, shape in FINISH_OUT],
        in_specs=[ANY] * 4,
        out_specs=[ANY] * len(FINISH_OUT),
        scratch_shapes=[pltpu.VMEM((slots, HALFW, WIDE), bf16), pltpu.VMEM((slots, HALFW, WIDE), f32),
                        pltpu.VMEM((IN, WIDE), f32), pltpu.VMEM((GS, WIDE), f32), pltpu.VMEM((GS, WIDE), bf16)]
        + [pltpu.SemaphoreType.DMA((slots,)), pltpu.SemaphoreType.DMA((slots, 2)), pltpu.SemaphoreType.DMA((2, 3))],
        compiler_params=pltpu.CompilerParams(vmem_limit_bytes=60 << 20),
    )(*args)


def local(
    latents, inputs, valid_counts, cotangent,
    gain_latent, shift_latent, gain_input, shift_input,
    cross_query, cross_key, cross_value, cross_out,
    gain_self, shift_self,
    self_query, self_key, self_value, self_out,
    gain_mlp, shift_mlp,
    mlp_in, mlp_in_bias, mlp_out, mlp_out_bias,
):
    core = lax.axis_index("mp")

    def row(vector):
        return vector.reshape(1, -1)

    weights = (cross_query, cross_key, cross_value, cross_out, self_query, self_key, self_value, self_out)
    result, *kept = forward(
        latents, inputs, valid_counts, cotangent,
        row(gain_latent), row(shift_latent), row(gain_input), row(shift_input),
        row(gain_self), row(shift_self), row(gain_mlp), row(shift_mlp),
        *weights, mlp_in, row(mlp_in_bias), mlp_out, row(mlp_out_bias))
    reduce = lax.axis_size("dp") == 16
    grads, packed, small, grad_latents, grad_inputs = backward(
        reduce, latents, inputs, valid_counts, cotangent,
        row(gain_latent), row(gain_input), row(gain_self), row(gain_mlp),
        *weights, mlp_in, mlp_out, *kept)
    if not reduce:
        packed, small = lax.psum(grads, "dp"), lax.psum(small, ("dp", "mp"))

    cq, ck, cv, co, sq, sk, sv, so, mi, mo, grad_inputs, grad_latents, result = finish(
        packed, grad_inputs, grad_latents, result)
    half = mlp_in_bias.shape[0]
    hidden_bias = lax.dynamic_slice_in_dim(small[9:13].reshape(-1), core * half, half)
    return (
        result, grad_latents, grad_inputs, *(small[i] for i in range(4)), cq, ck, cv, co,
        small[4], small[5], sq, sk, sv, so, small[6], small[7], mi, hidden_bias, mo, small[8],
    )


def solution(mesh):
    return jax.shard_map(
        local,
        mesh=mesh,
        in_specs=(
            P(("dp", "mp"), None),
            P(("dp", "mp"), None),
            P("dp"),
            P(("dp", "mp"), None),
            P(),
            P(),
            P(),
            P(),
            P(None, "mp"),
            P(None, "mp"),
            P(None, "mp"),
            P("mp", None),
            P(),
            P(),
            P(None, "mp"),
            P(None, "mp"),
            P(None, "mp"),
            P("mp", None),
            P(),
            P(),
            P(None, "mp"),
            P("mp"),
            P("mp", None),
            P(),
        ),
        out_specs=(
            P(("dp", "mp"), None),
            P(("dp", "mp"), None),
            P(("dp", "mp"), None),
            P(),
            P(),
            P(),
            P(),
            P(None, "mp"),
            P(None, "mp"),
            P(None, "mp"),
            P("mp", None),
            P(),
            P(),
            P(None, "mp"),
            P(None, "mp"),
            P(None, "mp"),
            P("mp", None),
            P(),
            P(),
            P(None, "mp"),
            P("mp"),
            P("mp", None),
            P(),
        ),
        check_vma=False,
    )
```

```python
import functools
import math

import jax
import jax.numpy as jnp
from jax import lax
from jax.experimental import pallas as pl
from jax.experimental.pallas import tpu as pltpu
from jax.sharding import PartitionSpec as P

MESH = pl.DeviceIdType.MESH
NS = 16
CH = 256
HALF = CH // 2
PIECE = HALF // 4
SUB = PIECE // 2
SMALL = 16
PARTS = (
    (("a", -2), ("b", 0), ("d", 2)),
    (("j", 6), ("i", 5), ("c", 1)),
    (("h", 4), ("f", 3), ("e", 2), ("k", 8)),
)
BEHIND = 8
AHEAD = 2
OWN = 3
HELD = 6
PAIRS = 16
REDUCE_SCRATCH = (
    ("own", (2 * OWN, HALF, 1024)), ("xr", (2 * HELD, HALF, 1024)), ("ur", (2 * HELD, HALF, 1024)), ("dr", (2 * HELD, HALF, 1024)),
    ("fb", (2 * HELD, PIECE, 1024)), ("yr", (2 * HELD, PIECE, 1024)),
)


def reducer(r, send, recv, loc):
    g_ref, out_ref, own, xr, ur, dr, fb, yr = r.grads, r.summed, r.own, r.xr, r.ur, r.dr, r.fb, r.yr
    dp = lax.axis_index("dp")
    core = lax.axis_index("mp")
    z = dp // 4
    px = lax.rem(dp, 2)
    py = lax.rem(dp // 2, 2)
    x_dev = (dp + 1 - 2 * px, core)
    y_dev = (dp + 2 - 4 * py, core)
    c_dev = (dp, 1 - core)
    up_dev = (dp + 4, core)
    down_dev = (dp - 4, core)
    z1_dev = (dp + 4 - 8 * lax.rem(z, 2), core)
    z2_dev = (dp + 8 - 16 * (z // 2), core)
    has_up = z < 3
    has_down = z > 0

    barrier = pltpu.get_barrier_semaphore()
    for dev in (x_dev, y_dev, c_dev, z2_dev):
        pl.semaphore_signal(barrier, inc=1, device_id=dev, device_id_type=MESH)

    @pl.when(has_up)
    def _():
        pl.semaphore_signal(barrier, inc=1, device_id=up_dev, device_id_type=MESH)

    @pl.when(has_down)
    def _():
        pl.semaphore_signal(barrier, inc=1, device_id=down_dev, device_id_type=MESH)

    def met():
        pl.semaphore_wait(barrier, 4 + has_up.astype(jnp.int32) + has_down.astype(jnp.int32))

    def remote(src, dst, kind, p, s, dev):
        slot = lax.rem(p, NS)
        return pltpu.make_async_remote_copy(
            src_ref=src, dst_ref=dst, send_sem=send.at[kind, s, slot], recv_sem=recv.at[kind, s, slot],
            device_id=dev, device_id_type=MESH)

    a_pos = (px, py)
    b_pos = (py, px)
    a_dev = (x_dev, y_dev)
    b_dev = (y_dev, x_dev)

    def base(p, s):
        return (2 * p + s) * CH

    def first(p, s):
        c = lax.rem(p, HELD) * 2 + s
        return remote(g_ref.at[pl.ds(base(p, s) + (1 - a_pos[s]) * HALF, HALF)], xr.at[c], 0, p, s, a_dev[s])

    def mine(p, s):
        c = lax.rem(p, OWN) * 2 + s
        return pltpu.make_async_copy(g_ref.at[pl.ds(base(p, s) + a_pos[s] * HALF, HALF)], own.at[c], loc.at[0, s, lax.rem(p, NS)])

    def up(p, s, lo):
        c = lax.rem(p, HELD) * 2 + s
        src = xr if lo == 1 else ur
        return remote(src.at[c, pl.ds(lo * PIECE, (4 - lo) * PIECE)], ur.at[c, pl.ds(lo * PIECE, (4 - lo) * PIECE)], 1, p, s, up_dev)

    def down(p, s, hi):
        c = lax.rem(p, HELD) * 2 + s
        src = xr if hi == 3 else dr
        return remote(src.at[c, pl.ds(0, hi * PIECE)], dr.at[c, pl.ds(0, hi * PIECE)], 2, p, s, down_dev)

    def last(p, s):
        c = lax.rem(p, HELD) * 2 + s
        return remote(fb.at[c], yr.at[c], 3, p, s, b_dev[s])

    def keep(p, s):
        c = lax.rem(p, HELD) * 2 + s
        return pltpu.make_async_copy(yr.at[c], piece_of(p, s, z), loc.at[1, s, lax.rem(p, NS)])

    def piece_of(p, s, k):
        return out_ref.at[pl.ds(base(p, s) + a_pos[s] * HALF + k * PIECE, PIECE)]

    def back(p, s, hop, k, kind, dev):
        src = yr.at[lax.rem(p, HELD) * 2 + s] if hop == 0 else piece_of(p, s, k)
        return remote(src, piece_of(p, s, k), kind, p, s, dev)

    def up_back(p, s, hop):
        return back(p, s, hop, jnp.maximum(z - hop, 0), 5 + hop, up_dev)

    def down_back(p, s, hop):
        return back(p, s, hop, jnp.minimum(z + hop, 3), 8 + hop, down_dev)

    def first_back(p, s):
        rows = out_ref.at[pl.ds(base(p, s) + a_pos[s] * HALF, HALF)]
        return remote(rows, rows, 11, p, s, a_dev[s])

    def add(*terms):
        total = terms[0].astype(jnp.float32)
        for term in terms[1:]:
            total = total + term.astype(jnp.float32)
        return total.astype(jnp.bfloat16)

    def step_a(p):
        for s in range(2):
            first(p, s).start()
            mine(p, s).start()

    def step_b(p):
        for s in range(2):
            c = lax.rem(p, HELD) * 2 + s
            first(p, s).wait_recv()
            mine(p, s).wait()
            xr[c] = add(own[lax.rem(p, OWN) * 2 + s], xr[c])

            @pl.when(z == 0)
            def _():
                up(p, s, 1).start()

            @pl.when(z == 3)
            def _():
                down(p, s, 3).start()

    def step_c(p):
        for s in range(2):
            c = lax.rem(p, HELD) * 2 + s

            @pl.when(z == 1)
            def _():
                up(p, s, 1).wait_recv()
                ur[c, 2 * PIECE:] = add(ur[c, 2 * PIECE:], xr[c, 2 * PIECE:])
                up(p, s, 2).start()

            @pl.when(z == 2)
            def _():
                down(p, s, 3).wait_recv()
                dr[c, : 2 * PIECE] = add(dr[c, : 2 * PIECE], xr[c, : 2 * PIECE])
                down(p, s, 2).start()

    def step_d(p):
        for s in range(2):
            c = lax.rem(p, HELD) * 2 + s

            @pl.when(z == 2)
            def _():
                up(p, s, 2).wait_recv()
                ur[c, 3 * PIECE:] = add(ur[c, 3 * PIECE:], xr[c, 3 * PIECE:])
                up(p, s, 3).start()

            @pl.when(z == 1)
            def _():
                down(p, s, 2).wait_recv()
                dr[c, :PIECE] = add(dr[c, :PIECE], xr[c, :PIECE])
                down(p, s, 1).start()

    def step_e(p):
        for s in range(2):
            c = lax.rem(p, HELD) * 2 + s

            @pl.when(z == 0)
            def _():
                down(p, s, 1).wait_recv()
                up(p, s, 1).wait_send()
                fb[c] = add(xr[c, :PIECE], dr[c, :PIECE])

            @pl.when(z == 1)
            def _():
                fb[c] = add(xr[c, PIECE: 2 * PIECE], ur[c, PIECE: 2 * PIECE], dr[c, PIECE: 2 * PIECE])

            @pl.when(z == 2)
            def _():
                fb[c] = add(xr[c, 2 * PIECE: 3 * PIECE], ur[c, 2 * PIECE: 3 * PIECE], dr[c, 2 * PIECE: 3 * PIECE])

            @pl.when(z == 3)
            def _():
                up(p, s, 3).wait_recv()
                down(p, s, 3).wait_send()
                fb[c] = add(xr[c, 3 * PIECE:], ur[c, 3 * PIECE:])

        for s in range(2):
            last(p, s).start()

    def step_f(p):
        for s in range(2):
            c = lax.rem(p, HELD) * 2 + s

            @pl.when(z == 1)
            def _():
                up(p, s, 2).wait_send()
                down(p, s, 1).wait_send()

            @pl.when(z == 2)
            def _():
                up(p, s, 3).wait_send()
                down(p, s, 2).wait_send()

            last(p, s).wait()
            yr[c] = add(fb[c], yr[c])
            keep(p, s).start()

            @pl.when(has_up)
            def _():
                up_back(p, s, 0).start()

            @pl.when(has_down)
            def _():
                down_back(p, s, 0).start()

    def step_h(p):
        for s in range(2):
            @pl.when(has_down)
            def _():
                up_back(p, s, 0).wait_recv()

            @pl.when(has_down & has_up)
            def _():
                up_back(p, s, 1).start()

            @pl.when(has_up)
            def _():
                down_back(p, s, 0).wait_recv()

            @pl.when(has_down & has_up)
            def _():
                down_back(p, s, 1).start()

    def step_i(p):
        for s in range(2):
            @pl.when(has_up)
            def _():
                up_back(p, s, 0).wait_send()

            @pl.when(has_down)
            def _():
                down_back(p, s, 0).wait_send()

            @pl.when(z >= 2)
            def _():
                up_back(p, s, 1).wait_recv()

            @pl.when(z == 2)
            def _():
                up_back(p, s, 2).start()

            @pl.when(z <= 1)
            def _():
                down_back(p, s, 1).wait_recv()

            @pl.when(z == 1)
            def _():
                down_back(p, s, 2).start()

    def step_j(p):
        for s in range(2):
            @pl.when(z == 3)
            def _():
                up_back(p, s, 2).wait_recv()

            @pl.when(z == 0)
            def _():
                down_back(p, s, 2).wait_recv()

            keep(p, s).wait()
            first_back(p, s).start()

    def step_k(p):
        for s in range(2):
            first_back(p, s).wait()
            first(p, s).wait_send()

            @pl.when(has_up & has_down)
            def _():
                up_back(p, s, 1).wait_send()
                down_back(p, s, 1).wait_send()

            @pl.when(z == 2)
            def _():
                up_back(p, s, 2).wait_send()

            @pl.when(z == 1)
            def _():
                down_back(p, s, 2).wait_send()

    steps = {"a": step_a, "b": step_b, "c": step_c, "d": step_d, "e": step_e, "f": step_f, "h": step_h,
             "i": step_i, "j": step_j, "k": step_k}

    def part(t, k):
        for name, behind in PARTS[k]:
            p = t - behind
            if isinstance(p, int):
                if 0 <= p < PAIRS:
                    steps[name](jnp.int32(p))
            else:
                pl.when((p >= 0) & (p < PAIRS))(functools.partial(steps[name], p))

    return met, part, (c_dev, x_dev, y_dev, z1_dev, z2_dev)


HD = 32
GS = 256
IN = 1024
WIDE = 1024
HALFW = 512
NEG = -1e30
EPS = 1e-05
LOG2E = math.log2(math.e)
SCALE = HD ** -0.5
bf16 = jnp.bfloat16
f32 = jnp.float32
ANY = pl.BlockSpec(memory_space=pl.ANY)
VM = pl.BlockSpec(memory_space=pltpu.VMEM)
SM = pl.BlockSpec(memory_space=pltpu.SMEM)


def nn(left, right):
    return jnp.dot(left, right, preferred_element_type=f32)


def nt(left, right):
    return lax.dot_general(left, right, (((1,), (1,)), ((), ())), preferred_element_type=f32)


def lanes(start, size):
    return pl.ds(pl.multiple_of(start, 128), size)


def rows_at(start, size):
    return pl.ds(pl.multiple_of(start, size), size)


def head_block(tile):
    lane = lax.broadcasted_iota(jnp.int32, tile.shape, 1) // HD
    zero = jnp.zeros_like(tile)
    return jnp.concatenate([jnp.where(lane == j, tile, zero) for j in range(4)], axis=0)


def scores_of(keys, query_block, count):
    scores = nt(keys, query_block)
    if count is None:
        return scores
    place = lax.broadcasted_iota(jnp.int32, scores.shape, 0)
    return jnp.where(place < count, scores, NEG)


def attend(queries, keys, values, count):
    values_t = values.T
    scores = scores_of(keys, head_block(queries), count)
    top = jnp.max(scores, axis=0, keepdims=True)
    weights = jnp.exp2((scores - top) * (LOG2E * SCALE))
    total = jnp.sum(weights, axis=0, keepdims=True)
    low = weights.astype(bf16)
    log_total = top * (LOG2E * SCALE) + jnp.log2(total)
    inverse = 1.0 / total
    mixed, logs = [], []
    for j in range(4):
        span = slice(j * GS, (j + 1) * GS)
        mixed.append(nn(values_t[j * HD:(j + 1) * HD], low[:, span]) * inverse[:, span])
        logs.append(log_total[:, span])
    return jnp.concatenate(mixed, axis=0), jnp.concatenate(logs, axis=0)


def attend_back(queries, keys, values, grads, logs, count):
    keys_t = keys.T
    query_block = head_block(queries)
    grad_block = head_block(grads)
    grad_keys = grad_values = None
    grad_queries = []
    for j in range(4):
        own_query = query_block[j * GS:(j + 1) * GS]
        own_grad = grad_block[j * GS:(j + 1) * GS]
        weights = jnp.exp2(scores_of(keys, own_query, count) * (LOG2E * SCALE) - logs[j:j + 1])
        weighted = weights * nt(values, own_grad)
        inner = jnp.sum(weighted, axis=0, keepdims=True)
        grad_scores = (weighted - weights * inner).astype(bf16)
        value_part = nn(weights.astype(bf16), own_grad)
        key_part = nn(grad_scores, own_query)
        grad_values = value_part if j == 0 else grad_values + value_part
        grad_keys = key_part if j == 0 else grad_keys + key_part
        grad_queries.append(nn(keys_t[j * HD:(j + 1) * HD], grad_scores))
    return jnp.concatenate(grad_queries, axis=0) * SCALE, grad_keys * SCALE, grad_values


def centre(stream):
    centered = stream - jnp.mean(stream, axis=1, keepdims=True)
    inverse = lax.rsqrt(jnp.mean(centered * centered, axis=1, keepdims=True) + EPS)
    return centered * inverse, inverse


def normed(stream, gain, shift):
    return (centre(stream)[0] * gain + shift).astype(bf16)


def norm_back(stream, gain, upstream):
    xhat, inverse = centre(stream)
    scaled = upstream * gain
    along = upstream * xhat
    mean_scaled = jnp.mean(scaled, axis=1, keepdims=True)
    mean_along = jnp.mean(scaled * xhat, axis=1, keepdims=True)
    grad = inverse * (scaled - mean_scaled - xhat * mean_along)
    return grad, jnp.sum(along, axis=0, keepdims=True), jnp.sum(upstream, axis=0, keepdims=True)


def meet(partner):
    barrier = pltpu.get_barrier_semaphore()
    pl.semaphore_signal(barrier, inc=1, device_id=partner, device_id_type=MESH)
    return lambda: pl.semaphore_wait(barrier, 1)


FWD_IN = (
    ("latents", VM), ("inputs", VM), ("counts", SM), ("cot", ANY),
    ("gain_latent", VM), ("shift_latent", VM), ("gain_input", VM), ("shift_input", VM),
    ("gain_self", VM), ("shift_self", VM), ("gain_mlp", VM), ("shift_mlp", VM),
    ("cq", ANY), ("ck", ANY), ("cv", ANY), ("co", ANY), ("sq", ANY), ("sk", ANY), ("sv", ANY), ("so", ANY),
    ("mi", ANY), ("mib", VM), ("mo", ANY), ("mob", VM),
)
FWD_OUT = (
    ("result", (GS, WIDE), bf16, VM),
    ("s1", (GS, WIDE), f32, VM), ("s2", (GS, WIDE), f32, VM),
    ("lnlT", (WIDE, 2 * GS), bf16, ANY), ("lniT", (WIDE, 2 * IN), bf16, ANY),
    ("snT", (WIDE, 2 * GS), bf16, ANY), ("mnT", (WIDE, 2 * GS), bf16, ANY),
    ("actT", (8, GS, 2 * GS), bf16, ANY), ("dg", (8, GS, HALFW), bf16, ANY),
    ("xq", (GS, WIDE), bf16, ANY), ("xk", (IN, WIDE), bf16, ANY), ("xv", (IN, WIDE), bf16, ANY),
    ("xoT", (HALFW, 2 * GS), bf16, ANY), ("xl", (8, 4, GS), f32, VM),
    ("yq", (GS, WIDE), bf16, ANY), ("yk", (GS, WIDE), bf16, ANY), ("yv", (GS, WIDE), bf16, ANY),
    ("yoT", (HALFW, 2 * GS), bf16, ANY), ("yl", (8, 4, GS), f32, VM),
    ("cotp", (GS, WIDE), bf16, ANY),
    ("rin", (6, WIDE, HALFW), bf16, ANY), ("rout", (2, HALFW, WIDE), bf16, ANY),
)
FWD_SCRATCH = (
    ("wx", (2, 3, WIDE, HALFW), bf16), ("wxo", (2, HALFW, WIDE), bf16),
    ("wy", (2, 3, WIDE, HALFW), bf16), ("wyo", (2, HALFW, WIDE), bf16),
    ("wmi", (2, WIDE, HALFW), bf16), ("wmo", (2, HALFW, WIDE), bf16),
    ("n", (GS, WIDE), bf16), ("ln", (IN, WIDE), bf16),
    ("t_l", (WIDE, GS), bf16), ("t_i", (WIDE, IN), bf16), ("t_s", (WIDE, GS), bf16), ("t_m", (WIDE, GS), bf16),
    ("q", (GS, WIDE), bf16), ("k", (IN, WIDE), bf16), ("v", (IN, WIDE), bf16), ("o", (GS, WIDE), bf16), ("oT", (WIDE, GS), bf16),
    ("q2", (GS, WIDE), bf16), ("k2", (GS, WIDE), bf16), ("v2", (GS, WIDE), bf16), ("o2", (GS, WIDE), bf16), ("oT2", (WIDE, GS), bf16),
    ("aT", (8, 2, GS, GS), bf16), ("dgs", (8, GS, HALFW), bf16), ("acc", (2, GS, WIDE), f32),
    ("np", (GS, WIDE), bf16), ("part", (2, GS, WIDE), bf16),
)


class Names:
    pass


def named(refs, *tables):
    out = Names()
    place = 0
    for table in tables:
        for entry in table:
            setattr(out, entry[0], refs[place])
            place += 1
    out.rest = refs[place:]
    return out


def forward_kernel(*refs):
    r = named(refs, FWD_IN, FWD_OUT, FWD_SCRATCH)
    send, recv, local = r.rest
    core = lax.axis_index("mp")
    partner = (lax.axis_index("dp"), 1 - core)
    met = meet(partner)
    sent, kept = [], []

    def push(src, dst):
        i = len(sent)
        copy = pltpu.make_async_remote_copy(
            src_ref=src, dst_ref=dst, send_sem=send.at[i], recv_sem=recv.at[i], device_id=partner, device_id_type=MESH)
        copy.start()
        sent.append(copy)
        return copy

    def fetch(src, dst):
        i = len(kept)
        copy = pltpu.make_async_copy(src, dst, local.at[i])
        copy.start()
        kept.append([copy, False])
        return i

    def ready(i):
        kept[i][0].wait()
        kept[i][1] = True

    near = [fetch(w, r.wx.at[0, i]) for i, w in ((1, r.ck), (2, r.cv), (0, r.cq))] + [fetch(r.co, r.wxo.at[0])]

    met()
    got = [push(r.ck, r.rin.at[1]), push(r.cv, r.rin.at[2]), push(r.cq, r.rin.at[0]), push(r.co, r.rout.at[0])]
    r.n[...] = normed(r.latents[...].astype(f32), r.gain_latent[...], r.shift_latent[...])
    r.t_l[...] = r.n[...].T
    fetch(r.t_l, r.lnlT.at[:, pl.ds(0, GS)])
    gain, shift = r.gain_input[...], r.shift_input[...]

    def input_norm(b, _):
        span = rows_at(b * GS, GS)
        block = normed(r.inputs[span].astype(f32), gain, shift)
        r.ln[span] = block
        r.t_i[:, lanes(b * GS, GS)] = block.T
        return 0

    lax.fori_loop(0, IN // GS, input_norm, 0, unroll=True)
    fetch(r.t_i, r.lniT.at[:, pl.ds(0, IN)])
    for i in near[:3]:
        ready(i)

    def project_inputs(half):
        def block(b, _):
            span = rows_at(b * GS, GS)
            rows = r.ln[span]
            r.k[span, half * HALFW:(half + 1) * HALFW] = nn(rows, r.wx[half, 1]).astype(bf16)
            r.v[span, half * HALFW:(half + 1) * HALFW] = nn(rows, r.wx[half, 2]).astype(bf16)
            return 0

        lax.fori_loop(0, IN // GS, block, 0)
        r.q[:, half * HALFW:(half + 1) * HALFW] = nn(r.n[...], r.wx[half, 0]).astype(bf16)

    project_inputs(0)
    got += [push(w, r.rin.at[i]) for i, w in ((3, r.sq), (4, r.sk), (5, r.sv))] + [push(r.so, r.rout.at[1])]
    near2 = [fetch(w, r.wy.at[0, i]) for i, w in enumerate((r.sq, r.sk, r.sv))] + [fetch(r.so, r.wyo.at[0])]
    count = r.counts[core]

    def attention(queries, keys, values, mixed, mixed_t, logs, limit, first, last):
        def group(g, _):
            at = lanes(g * 128, 128)
            out_t, log_total = attend(queries[:, at], keys[:, at], values[:, at], limit)
            out_t = out_t.astype(bf16)
            mixed_t[rows_at(g * 128, 128)] = out_t
            mixed[:, at] = out_t.T
            logs[g] = log_total
            return 0

        lax.fori_loop(first, last, group, 0, unroll=True)

    attention(r.q, r.k, r.v, r.o, r.oT, r.xl, count, 0, 3)
    far = []
    for copy, src, dst in (
        (got[0], r.rin.at[1], r.wx.at[1, 1]), (got[1], r.rin.at[2], r.wx.at[1, 2]),
        (got[2], r.rin.at[0], r.wx.at[1, 0]), (got[3], r.rout.at[0], r.wxo.at[1])):
        copy.wait_recv()
        far.append(fetch(src, dst))
    attention(r.q, r.k, r.v, r.o, r.oT, r.xl, count, 3, 4)
    for i in far[:3]:
        ready(i)
    project_inputs(1)
    fetch(r.q, r.xq)
    fetch(r.k, r.xk)
    fetch(r.v, r.xv)
    attention(r.q, r.k, r.v, r.o, r.oT, r.xl, count, 4, 8)
    fetch(r.oT.at[pl.ds(0, HALFW)], r.xoT.at[:, pl.ds(0, GS)])
    push(r.oT.at[pl.ds(HALFW, HALFW)], r.xoT.at[:, pl.ds(GS, GS)])
    push(r.t_l, r.lnlT.at[:, pl.ds(GS, GS)])
    push(r.t_i, r.lniT.at[:, pl.ds(IN, IN)])
    push(r.cot, r.cotp)
    ready(near[3])
    ready(far[3])

    def out_project(mixed, weight):
        return nn(mixed[:, :HALFW], weight[0]) + nn(mixed[:, HALFW:], weight[1])

    r.s1[...] = r.latents[...].astype(f32) + out_project(r.o, r.wxo)
    r.n[...] = normed(r.s1[...], r.gain_self[...], r.shift_self[...])
    far2 = []
    for copy, src, dst in (
        (got[4], r.rin.at[3], r.wy.at[1, 0]), (got[5], r.rin.at[4], r.wy.at[1, 1]),
        (got[6], r.rin.at[5], r.wy.at[1, 2]), (got[7], r.rout.at[1], r.wyo.at[1])):
        copy.wait_recv()
        far2.append(fetch(src, dst))
    r.t_s[...] = r.n[...].T
    fetch(r.t_s, r.snT.at[:, pl.ds(0, GS)])
    push(r.t_s, r.snT.at[:, pl.ds(GS, GS)])
    for i in near2 + far2:
        ready(i)
    for half in range(2):
        at = slice(half * HALFW, (half + 1) * HALFW)
        for i, dst in enumerate((r.q2, r.k2, r.v2)):
            dst[:, at] = nn(r.n[...], r.wy[half, i]).astype(bf16)
    fetch(r.q2, r.yq)
    fetch(r.k2, r.yk)
    fetch(r.v2, r.yv)
    attention(r.q2, r.k2, r.v2, r.o2, r.oT2, r.yl, None, 0, 8)
    fetch(r.oT2.at[pl.ds(0, HALFW)], r.yoT.at[:, pl.ds(0, GS)])
    push(r.oT2.at[pl.ds(HALFW, HALFW)], r.yoT.at[:, pl.ds(GS, GS)])

    chunk_sem = len(kept)

    def chunk_copies(n, slot):
        c = lax.rem(n, 4)
        return (
            pltpu.make_async_copy(r.mi.at[:, lanes(c * HALFW, HALFW)], r.wmi.at[slot], local.at[chunk_sem + slot]),
            pltpu.make_async_copy(r.mo.at[rows_at(c * HALFW, HALFW)], r.wmo.at[slot], local.at[chunk_sem + 2 + slot]),
        )

    for copy in chunk_copies(jnp.int32(0), 0):
        copy.start()
    kept += [None] * 4
    r.s2[...] = r.s1[...] + out_project(r.o2, r.wyo)
    r.n[...] = normed(r.s2[...], r.gain_mlp[...], r.shift_mlp[...])
    met_rows = push(r.n, r.np)
    r.t_m[...] = r.n[...].T
    fetch(r.t_m, r.mnT.at[:, pl.ds(0, GS)])
    push(r.t_m, r.mnT.at[:, pl.ds(GS, GS)])
    r.acc[...] = jnp.zeros((2, GS, WIDE), f32)

    def feed(rows, who):
        def step(n, _):
            slot = lax.rem(n, 2)

            @pl.when(n + 1 < 8)
            def _():
                for copy in chunk_copies(n + 1, 1 - slot):
                    copy.start()

            for copy in chunk_copies(n, slot):
                copy.wait()
            hidden = nn(rows[...], r.wmi[slot]) + r.mib[:, lanes(lax.rem(n, 4) * HALFW, HALFW)]
            area = 0.5 + 0.5 * lax.erf(hidden * (0.5 ** 0.5))
            density = jnp.exp(-0.5 * hidden * hidden) * ((2 * math.pi) ** -0.5)
            act = (hidden * area).astype(bf16)
            r.dgs[n] = (area + hidden * density).astype(bf16)
            r.aT[n] = act.T.reshape(2, GS, GS)
            r.acc[who] += nn(act, r.wmo[slot])
            return 0

        lax.fori_loop(4 * who, 4 * who + 4, step, 0, unroll=True)

    feed(r.n, 0)
    met_rows.wait_recv()
    got.append(met_rows)
    feed(r.np, 1)
    r.part[0] = r.acc[1].astype(bf16)
    met_part = push(r.part.at[0], r.part.at[1])
    got.append(met_part)
    for c in range(4):
        for who in range(2):
            fetch(r.aT.at[4 * who + c], r.actT.at[pl.ds(2 * c, 2), :, pl.ds(who * GS, GS)])
    fetch(r.dgs, r.dg)
    met_part.wait_recv()
    r.result[...] = (r.s2[...] + (r.acc[0] + r.part[1].astype(f32) + r.mob[...])).astype(bf16)
    for i, entry in enumerate(kept):
        if entry is not None and not entry[1]:
            ready(i)
    seen = [id(c) for c in got]
    for copy in sent:
        copy.wait_send()
        if id(copy) not in seen:
            copy.wait_recv()


def forward(*args):
    return pl.pallas_call(
        forward_kernel,
        out_shape=[jax.ShapeDtypeStruct(shape, dtype) for _, shape, dtype, _ in FWD_OUT],
        in_specs=[spec for _, spec in FWD_IN],
        out_specs=[spec for _, _, _, spec in FWD_OUT],
        scratch_shapes=[pltpu.VMEM(shape, dtype) for _, shape, dtype in FWD_SCRATCH]
        + [pltpu.SemaphoreType.DMA((24,)), pltpu.SemaphoreType.DMA((24,)), pltpu.SemaphoreType.DMA((64,))],
        compiler_params=pltpu.CompilerParams(collective_id=1, has_side_effects=True, vmem_limit_bytes=60 << 20),
    )(*args)


BWD_IN = (
    ("latents", VM), ("inputs", ANY), ("counts", SM), ("cot", VM),
    ("gain_latent", VM), ("gain_input", VM), ("gain_self", VM), ("gain_mlp", VM),
    ("cq", ANY), ("ck", ANY), ("cv", ANY), ("co", ANY), ("sq", ANY), ("sk", ANY), ("sv", ANY), ("so", ANY),
    ("mi", ANY), ("mo", ANY),
) + tuple((name, VM if name in ("xl", "yl") else ANY) for name, _, _, _ in FWD_OUT[1:])
ROWS_OUT = 8192
BWD_OUT = (
    ("grads", (ROWS_OUT, WIDE), bf16, ANY), ("summed", (ROWS_OUT, WIDE), bf16, ANY), ("small", (SMALL, WIDE), f32, VM),
    ("grad_latents", (GS, WIDE), f32, VM), ("grad_inputs", (IN, WIDE), f32, ANY),
)
BWD_SCRATCH = (
    ("wy", (2, 3, WIDE, HALFW), bf16), ("wyo", (2, HALFW, WIDE), bf16), ("wxo", (2, HALFW, WIDE), bf16),
    ("wmi", (2, WIDE, HALFW), bf16), ("wmo", (2, HALFW, WIDE), bf16),
    ("mc", (2 * GS, WIDE), bf16), ("sc", (2 * GS, WIDE), bf16),
    ("dk", (8, GS, HALFW), bf16), ("dgs", (2, GS, HALFW), bf16),
    ("mT", (WIDE, 2 * GS), bf16), ("big", (4, HALFW, HALFW), bf16), ("bigr", (4, GS, HALFW), bf16),
    ("sT", (WIDE, 2 * GS), bf16), ("kv", (2, IN, WIDE), bf16),
    ("q", (GS, WIDE), bf16), ("oT", (HALFW, 2 * GS), bf16),
    ("qkv2", (3, GS, WIDE), bf16), ("oT2", (HALFW, 2 * GS), bf16),
    ("g", (GS, WIDE), bf16), ("up", (GS, WIDE), bf16),
    ("dq", (2 * GS, HALFW), bf16), ("dqr", (GS, HALFW), bf16), ("dvr", (2, HALFW, HALFW), bf16),
    ("dq2", (3, 2 * GS, HALFW), bf16), ("dqr2", (3, GS, HALFW), bf16),
    ("wide", (2, GS, WIDE), f32),
    ("stage", (2, HALFW, WIDE), bf16), ("bsum", (4, HALFW), f32), ("sacc", (SMALL, WIDE), f32), ("sbuf", (5, SMALL, WIDE), f32),
)
ROW_MO, ROW_MI, ROW_SO, ROW_SQ, ROW_CO, ROW_CQ = 0, 2048, 4096, 4608, 6144, 6656


def backward_kernel(reduce, *refs):
    r = named(refs, BWD_IN, BWD_OUT, BWD_SCRATCH, REDUCE_SCRATCH if reduce else ())
    send, recv, local, stage_sem, chunk_sem, x_sem, *reduce_sems = r.rest
    core = lax.axis_index("mp")
    partner = (lax.axis_index("dp"), 1 - core)
    if reduce:
        met, part, small_devs = reducer(r, *reduce_sems[:3])
    else:
        met = meet(partner)
    sent, kept, staged = [], [], []
    state = {"tick": 0, "settled": 0}

    def settle(upto=None):
        upto = len(staged) if upto is None else upto
        for copy in staged[state["settled"]:upto]:
            copy.wait()
        state["settled"] = max(state["settled"], upto)

    def may_take(first, last):
        for n in range(first, last):
            if n % 3 == 0:
                assert min(n // 3 + AHEAD + 1, PAIRS) <= state["settled"]

    def tick(count=1):
        for _ in range(count):
            n = state["tick"]
            state["tick"] = n + 1
            if reduce:
                may_take(n, n + 1)
                part(n // 3, n % 3)

    def loop_tick(n):
        if reduce:
            for k in range(3):
                pl.when(lax.rem(n, 3) == k)(functools.partial(part, n // 3, k))

    def loop_ticks(count):
        n = state["tick"]
        state["tick"] = n + count
        if reduce:
            may_take(n, n + count)
        return n

    def push(src, dst):
        i = len(sent)
        copy = pltpu.make_async_remote_copy(
            src_ref=src, dst_ref=dst, send_sem=send.at[i], recv_sem=recv.at[i], device_id=partner, device_id_type=MESH)
        copy.start()
        sent.append(copy)
        return copy

    def fetch(src, dst):
        copy = pltpu.make_async_copy(src, dst, local.at[len(kept)])
        copy.start()
        kept.append(copy)
        return copy

    def stage(write, row):
        i = len(staged)
        slot = i % 2
        if i >= 2 and state["settled"] <= i - 2:
            staged[i - 2].wait()
            state["settled"] = i - 1
        write(r.stage.at[slot])
        copy = pltpu.make_async_copy(r.stage.at[slot], r.grads.at[pl.ds(row, HALFW)], stage_sem.at[slot])
        copy.start()
        staged.append(copy)

    early = [fetch(r.actT, r.dk), fetch(r.cotp, r.mc.at[pl.ds(GS, GS)])]

    def chunk_copies(i, slot):
        c = lax.rem(i, 4)
        return (
            pltpu.make_async_copy(r.mi.at[:, lanes(c * HALFW, HALFW)], r.wmi.at[slot], chunk_sem.at[0, slot]),
            pltpu.make_async_copy(r.mo.at[rows_at(c * HALFW, HALFW)], r.wmo.at[slot], chunk_sem.at[1, slot]),
            pltpu.make_async_copy(r.dg.at[lax.rem(i + 4, 8)], r.dgs.at[slot], chunk_sem.at[2, slot]),
        )

    for copy in chunk_copies(jnp.int32(0), 0):
        copy.start()
    load_m = [fetch(r.mnT, r.mT)]
    load_y = [fetch(w, r.wy.at[0, i]) for i, w in enumerate((r.sq, r.sk, r.sv))]
    load_y += [fetch(r.rin.at[pl.ds(3, 3)], r.wy.at[1]), fetch(r.so, r.wyo.at[0]), fetch(r.rout.at[1], r.wyo.at[1])]
    load_y += [fetch(a, b) for a, b in ((r.yq, r.qkv2.at[0]), (r.yk, r.qkv2.at[1]), (r.yv, r.qkv2.at[2]), (r.yoT, r.oT2), (r.snT, r.sT))]
    r.mc[pl.ds(0, GS)] = r.cot[...]
    for copy in early:
        copy.wait()
    for m in range(4):
        def write(dst, m=m):
            dst[...] = nn(r.dk[2 * m:2 * m + 2].reshape(HALFW, 2 * GS), r.mc[...]).astype(bf16)

        stage(write, ROW_MO + m * HALFW)
        if m == 0:
            met()
        elif reduce and m <= AHEAD:
            settle(m)
            part(m - 1 - AHEAD, 0)
    settle()
    r.wide[...] = jnp.zeros((2, GS, WIDE), f32)

    def feed(i, who, ticks=None):
        slot = lax.rem(i, 2)

        @pl.when(i + 1 < 8)
        def _():
            for copy in chunk_copies(i + 1, 1 - slot):
                copy.start()

        for copy in chunk_copies(i, slot):
            copy.wait()
        grad = (nt(r.mc[who * GS:(who + 1) * GS], r.wmo[slot]) * r.dgs[slot].astype(f32)).astype(bf16)
        total = jnp.sum(grad.astype(f32), axis=0, keepdims=True)
        c = lax.rem(i, 4)
        if who:
            r.bsum[pl.ds(c, 1)] = total
        else:
            r.bsum[pl.ds(c, 1)] += total
        r.big[c, who * GS:(who + 1) * GS] = grad
        r.wide[who] += nt(grad, r.wmi[slot])
        if ticks is not None:
            loop_tick(i + ticks)
        return 0

    lax.fori_loop(0, 4, lambda i, _: feed(i, 1), 0)
    r.g[...] = r.wide[1].astype(bf16)
    push_u = push(r.g, r.up)
    load_m.append(fetch(r.s2, r.wide.at[1]))
    lax.fori_loop(4, 5, lambda i, _: feed(i, 0), 0)
    first_tick = loop_ticks(3)
    lax.fori_loop(5, 8, lambda i, _: feed(i, 0, first_tick - 5), 0)
    load_x = [fetch(r.co, r.wxo.at[0]), fetch(r.rout.at[0], r.wxo.at[1])]
    load_x += [fetch(a, b) for a, b in ((r.xq, r.q), (r.xk, r.kv.at[0]), (r.xv, r.kv.at[1]), (r.xoT, r.oT))]

    for copy in load_m:
        copy.wait()
    push_u.wait()
    grad, along, plain = norm_back(r.wide[1], r.gain_mlp[...], r.wide[0] + r.up[...].astype(f32))
    load_s = fetch(r.s1, r.wide.at[1])
    r.small[6:7] = along
    r.small[7:8] = plain
    r.wide[0] = r.cot[...].astype(f32) + grad
    r.sc[pl.ds(0, GS)] = r.wide[0].astype(bf16)
    push_c = push(r.sc.at[pl.ds(0, GS)], r.sc.at[pl.ds(GS, GS)])
    tick()
    for c in range(4):
        def write(dst, c=c):
            dst[...] = jnp.concatenate(
                [nn(r.mT[c % 2 * HALFW:(c % 2 + 1) * HALFW], r.big[c // 2 * 2 + e]).astype(bf16)
                 for e in range(2)], axis=1)

        stage(write, ROW_MI + c * HALFW)
        settle(3 + c)
        tick()
    settle()
    load_l = fetch(r.lnlT, r.mT)

    def attention_back(queries, keys, values, logs, limit, take, own, other, hand_over, every):
        first = loop_ticks(8 // every)

        def group(i, _):
            g = lax.rem(i + 4, 8)
            at = lanes(g * 128, 128)
            to = lanes(lax.rem(i, 4) * 128, 128)
            pl.when(i == 4)(hand_over)
            grad_q, grad_k, grad_v = attend_back(queries[:, at], keys[:, at], values[:, at], r.g[:, at], logs[g], limit)
            grad_q, grad_k, grad_v = grad_q.astype(bf16).T, grad_k.astype(bf16), grad_v.astype(bf16)
            pl.when(i < 4)(lambda: take(other, to, grad_q, grad_k, grad_v))
            pl.when(i >= 4)(lambda: take(own, to, grad_q, grad_k, grad_v))
            if every == 1:
                loop_tick(first + i)
            else:
                pl.when(lax.rem(i, every) == every - 1)(lambda: loop_tick(first + i // every))
            return 0

        lax.fori_loop(0, 8, group, 0)

    def out_back(cots, weight):
        cot = cots[pl.ds(0, GS)]
        for half in range(2):
            r.g[:, half * HALFW:(half + 1) * HALFW] = nt(cot, weight[half]).astype(bf16)

    def grad_fold(left, right, row):
        def write(dst):
            for e in range(2):
                dst[:, e * HALFW:(e + 1) * HALFW] = nn(left[e * HALFW:(e + 1) * HALFW], right[...]).astype(bf16)

        stage(write, row)

    def crossing(i, src, dst):
        return pltpu.make_async_remote_copy(
            src_ref=src, dst_ref=dst, send_sem=send.at[i], recv_sem=recv.at[i], device_id=partner, device_id_type=MESH)

    push_y = crossing(12, r.dqr2, r.dq2.at[:, pl.ds(GS, GS)])
    push_x = [
        crossing(13, r.dqr, r.dq.at[pl.ds(GS, GS)]), crossing(14, r.bigr, r.dk.at[pl.ds(4, 4)]),
        crossing(15, r.dvr, r.big.at[pl.ds(2, 2)])]

    def take_y(dst, to, grad_q, grad_k, grad_v):
        for i, grad in enumerate((grad_q, grad_k, grad_v)):
            dst[i, pl.ds(0, GS), to] = grad

    def take_x(dst, to, grad_q, grad_k, grad_v):
        dst_q, dst_k, dst_v = dst
        dst_q[pl.ds(0, GS), to] = grad_q
        dst_k[pl.ds(0, 4), :, to] = grad_k.reshape(4, GS, 128)
        dst_v[pl.ds(0, 2), :, to] = grad_v.reshape(2, HALFW, 128)

    for copy in load_y:
        copy.wait()
    out_back(r.sc, r.wyo)
    tick()
    attention_back(r.qkv2.at[0], r.qkv2.at[1], r.qkv2.at[2], r.yl, None, take_y, r.dq2, r.dqr2, push_y.start, 1)
    push_c.wait_recv()

    def write_so(dst):
        dst[...] = nn(r.oT2[...], r.sc[...]).astype(bf16)

    stage(write_so, ROW_SO)
    tick()
    settle()
    load_s.wait()
    upstream = None
    for i in range(3):
        term = nt(r.dq2[i, :GS], r.wy[0, i]) + nt(r.dqr2[i], r.wy[1, i])
        upstream = term if upstream is None else upstream + term
    grad, along, plain = norm_back(r.wide[1], r.gain_self[...], upstream)
    r.small[4:5] = along
    r.small[5:6] = plain
    r.wide[0] += grad
    load_w = [fetch(w, r.wy.at[0, i]) for i, w in enumerate((r.cq, r.ck, r.cv))] + [fetch(r.rin.at[pl.ds(0, 3)], r.wy.at[1])]
    r.mc[pl.ds(0, GS)] = r.wide[0].astype(bf16)
    push_c2 = push(r.mc.at[pl.ds(0, GS)], r.mc.at[pl.ds(GS, GS)])
    push_y.wait_recv()
    tick()
    for i in range(3):
        grad_fold(r.sT, r.dq2.at[i], ROW_SQ + i * HALFW)
        settle(9 + i)
        tick()

    for copy in load_x:
        copy.wait()
    out_back(r.mc, r.wxo)
    tick()
    count = r.counts[core]
    push_c2.wait_recv()

    def write_co(dst):
        dst[...] = nn(r.oT[...], r.mc[...]).astype(bf16)

    stage(write_co, ROW_CO)
    tick()
    settle()

    def hand_over_x():
        for copy in push_x:
            copy.start()

    attention_back(r.q, r.kv.at[0], r.kv.at[1], r.xl, count, take_x, (r.dq, r.dk, r.big), (r.dqr, r.bigr, r.dvr), hand_over_x, 1)
    load_i = [fetch(r.lniT.at[:, pl.ds(0, IN)], r.kv.at[0]), fetch(r.lniT.at[:, pl.ds(IN, IN)], r.kv.at[1])]
    for copy in push_x:
        copy.wait_recv()
    load_l.wait()
    grad_fold(r.mT, r.dq, ROW_CQ)
    settle()
    tick()
    for copy in load_i:
        copy.wait()

    def tall(blocks):
        return blocks.reshape(IN, HALFW)

    def grad_tall(right, row):
        def write(dst):
            for e in range(2):
                at = slice(e * HALFW, (e + 1) * HALFW)
                dst[:, at] = (nn(r.kv[0, at], tall(right[0])) + nn(r.kv[1, at], tall(right[1]))).astype(bf16)

        stage(write, row)

    grad_tall((r.dk[:4], r.dk[4:]), ROW_CQ + HALFW)
    tick()
    grad_tall((r.big[:2], r.big[2:]), ROW_CQ + 2 * HALFW)
    settle()
    tick()
    for copy in load_w:
        copy.wait()
    upstream = nt(r.dq[:GS], r.wy[0, 0]) + nt(r.dqr[...], r.wy[1, 0])
    grad, along, plain = norm_back(r.latents[...].astype(f32), r.gain_latent[...], upstream)
    r.small[0:1] = along
    r.small[1:2] = plain
    r.grad_latents[...] = r.wide[0] + grad
    r.small[2:4] = jnp.zeros((2, WIDE), f32)

    def x_in(b):
        slot = lax.rem(b, 2)
        return pltpu.make_async_copy(r.inputs.at[rows_at(b * GS, GS)], r.qkv2.at[slot], x_sem.at[0, slot])

    def x_out(b):
        slot = lax.rem(b, 2)
        return pltpu.make_async_copy(r.wide.at[slot], r.grad_inputs.at[rows_at(b * GS, GS)], x_sem.at[1, slot])

    x_in(jnp.int32(0)).start()

    def input_back(b, _):
        slot = lax.rem(b, 2)

        @pl.when(b + 1 < IN // GS)
        def _():
            x_in(b + 1).start()

        x_in(b).wait()

        @pl.when(b >= 2)
        def _():
            x_out(b - 2).wait()

        half, at = b // 2, rows_at(lax.rem(b, 2) * GS, GS)
        up = nt(r.dk[b], r.wy[0, 1]) + nt(r.bigr[b], r.wy[1, 1]) + nt(r.big[half, at], r.wy[0, 2]) + nt(r.dvr[half, at], r.wy[1, 2])
        grad, along, plain = norm_back(r.qkv2[slot].astype(f32), r.gain_input[...], up)
        r.small[2:3] += along
        r.small[3:4] += plain
        r.wide[slot] = grad
        x_out(b).start()
        loop_tick(ticks + b)
        return 0

    ticks = loop_ticks(IN // GS)

    lax.fori_loop(0, IN // GS, input_back, 0)
    r.small[8:9] = jnp.sum(r.cot[...].astype(f32), axis=0, keepdims=True)
    r.small[13:16] = jnp.zeros((3, WIDE), f32)
    for i in range(4):
        half, odd = i // 2, i % 2 * 2
        mine = jnp.concatenate([r.bsum[odd:odd + 1], r.bsum[odd + 1:odd + 2]], axis=1)
        r.small[9 + i:10 + i] = jnp.where(core == half, mine, 0.0)
    x_out(jnp.int32(IN // GS - 2)).wait()
    x_out(jnp.int32(IN // GS - 1)).wait()
    for copy in (push_c, push_y, push_c2, *push_x):
        copy.wait_send()
    if not reduce:
        return
    tick(-state["tick"] % 3)
    begin = state["tick"] // 3
    small_send, small_recv = reduce_sems[3:]

    def small_copy(i):
        return pltpu.make_async_remote_copy(
            src_ref=r.sacc, dst_ref=r.sbuf.at[i], send_sem=small_send.at[i], recv_sem=small_recv.at[i],
            device_id=small_devs[i], device_id_type=MESH)

    r.sacc[...] = r.small[...]
    small_copy(0).start()

    def iteration(t, _):
        for k in range(3):
            part(t, k)
        for i in range(5):
            @pl.when(t == begin + i)
            def _():
                small_copy(i).wait()
                r.sacc[...] += r.sbuf[i]
                if i < 4:
                    small_copy(i + 1).start()
        return 0

    lax.fori_loop(begin, PAIRS + BEHIND, iteration, 0)
    r.small[...] = r.sacc[...]


def backward(reduce, *args):
    scratch = [pltpu.VMEM(shape, dtype) for _, shape, dtype in BWD_SCRATCH]
    sems = [(16,), (16,), (48,), (2,), (3, 2), (2, 2)]
    if reduce:
        scratch += [pltpu.VMEM(shape, bf16) for _, shape in REDUCE_SCRATCH]
        sems += [(12, 2, NS), (12, 2, NS), (2, 2, NS), (5,), (5,)]
    return pl.pallas_call(
        functools.partial(backward_kernel, reduce),
        out_shape=[jax.ShapeDtypeStruct(shape, dtype) for _, shape, dtype, _ in BWD_OUT],
        in_specs=[spec for _, spec in BWD_IN],
        out_specs=[spec for _, _, _, spec in BWD_OUT],
        scratch_shapes=scratch + [pltpu.SemaphoreType.DMA(shape) for shape in sems],
        compiler_params=pltpu.CompilerParams(
            collective_id=0 if reduce else 2, has_side_effects=True, vmem_limit_bytes=63 << 20),
    )(*args)


FINISH_OUT = (
    ("cq", (WIDE, HALFW)), ("ck", (WIDE, HALFW)), ("cv", (WIDE, HALFW)), ("co", (HALFW, WIDE)),
    ("sq", (WIDE, HALFW)), ("sk", (WIDE, HALFW)), ("sv", (WIDE, HALFW)), ("so", (HALFW, WIDE)),
    ("mi", (WIDE, 2048)), ("mo", (2048, WIDE)), ("gi", (IN, WIDE)), ("gl", (GS, WIDE)), ("result", (GS, WIDE)),
)


def finish_kernel(packed, gi, gl, result, *refs):
    r = named(refs, FINISH_OUT)
    low, high, mid_gi, mid_gl, mid_result, sem_in, sem_out, sem_copy = r.rest
    through = [
        [pltpu.make_async_copy(src, mid, sem_copy.at[0, i]), pltpu.make_async_copy(mid, dst, sem_copy.at[1, i])]
        for i, (src, mid, dst) in enumerate(((gi, mid_gi, r.gi), (gl, mid_gl, r.gl), (result, mid_result, r.result)))]
    plan = []
    for c in range(4):
        plan.append((ROW_MO + c * HALFW, [(r.mo.at[pl.ds(c * HALFW, HALFW)], 0, WIDE)]))
    for c in range(4):
        plan.append((ROW_MI + c * HALFW, [(r.mi.at[pl.ds(c % 2 * HALFW, HALFW), pl.ds(c // 2 * WIDE, WIDE)], 0, WIDE)]))
    for start, out, tall in ((ROW_SO, r.so, (r.sq, r.sk, r.sv)), (ROW_CO, r.co, (r.cq, r.ck, r.cv))):
        plan.append((start, [(out, 0, WIDE)]))
        for i, dst in enumerate(tall):
            plan.append((start + (i + 1) * HALFW, [(dst.at[pl.ds(e * HALFW, HALFW)], e * HALFW, HALFW) for e in range(2)]))
    slots = low.shape[0]

    def load(n):
        return pltpu.make_async_copy(packed.at[pl.ds(plan[n][0], HALFW)], low.at[n % slots], sem_in.at[n % slots])

    def stores(n):
        return [
            pltpu.make_async_copy(high.at[n % slots, :, pl.ds(at, size)], dst, sem_out.at[n % slots, e])
            for e, (dst, at, size) in enumerate(plan[n][1])]

    for n in range(slots - 1):
        load(n).start()
    for pair in through:
        pair[0].start()
    for n in range(len(plan)):
        if n + slots - 1 < len(plan):
            load(n + slots - 1).start()
        load(n).wait()
        if n >= slots:
            for copy in stores(n - slots):
                copy.wait()
        high[n % slots] = low[n % slots].astype(f32)
        for copy in stores(n):
            copy.start()
        if 4 <= n < 7:
            through[n - 4][0].wait()
            through[n - 4][1].start()
    for n in range(len(plan) - slots, len(plan)):
        for copy in stores(n):
            copy.wait()
    for pair in through:
        pair[1].wait()


def finish(*args):
    slots = 4
    return pl.pallas_call(
        finish_kernel,
        out_shape=[jax.ShapeDtypeStruct(shape, bf16 if name == "result" else f32) for name, shape in FINISH_OUT],
        in_specs=[ANY] * 4,
        out_specs=[ANY] * len(FINISH_OUT),
        scratch_shapes=[pltpu.VMEM((slots, HALFW, WIDE), bf16), pltpu.VMEM((slots, HALFW, WIDE), f32),
                        pltpu.VMEM((IN, WIDE), f32), pltpu.VMEM((GS, WIDE), f32), pltpu.VMEM((GS, WIDE), bf16)]
        + [pltpu.SemaphoreType.DMA((slots,)), pltpu.SemaphoreType.DMA((slots, 2)), pltpu.SemaphoreType.DMA((2, 3))],
        compiler_params=pltpu.CompilerParams(vmem_limit_bytes=60 << 20),
    )(*args)


def local(
    latents, inputs, valid_counts, cotangent,
    gain_latent, shift_latent, gain_input, shift_input,
    cross_query, cross_key, cross_value, cross_out,
    gain_self, shift_self,
    self_query, self_key, self_value, self_out,
    gain_mlp, shift_mlp,
    mlp_in, mlp_in_bias, mlp_out, mlp_out_bias,
):
    core = lax.axis_index("mp")

    def row(vector):
        return vector.reshape(1, -1)

    weights = (cross_query, cross_key, cross_value, cross_out, self_query, self_key, self_value, self_out)
    result, *kept = forward(
        latents, inputs, valid_counts, cotangent,
        row(gain_latent), row(shift_latent), row(gain_input), row(shift_input),
        row(gain_self), row(shift_self), row(gain_mlp), row(shift_mlp),
        *weights, mlp_in, row(mlp_in_bias), mlp_out, row(mlp_out_bias))
    reduce = lax.axis_size("dp") == 16
    grads, packed, small, grad_latents, grad_inputs = backward(
        reduce, latents, inputs, valid_counts, cotangent,
        row(gain_latent), row(gain_input), row(gain_self), row(gain_mlp),
        *weights, mlp_in, mlp_out, *kept)
    if not reduce:
        packed, small = lax.psum(grads, "dp"), lax.psum(small, ("dp", "mp"))

    cq, ck, cv, co, sq, sk, sv, so, mi, mo, grad_inputs, grad_latents, result = finish(
        packed, grad_inputs, grad_latents, result)
    half = mlp_in_bias.shape[0]
    hidden_bias = lax.dynamic_slice_in_dim(small[9:13].reshape(-1), core * half, half)
    return (
        result, grad_latents, grad_inputs, *(small[i] for i in range(4)), cq, ck, cv, co,
        small[4], small[5], sq, sk, sv, so, small[6], small[7], mi, hidden_bias, mo, small[8],
    )


def solution(mesh):
    return jax.shard_map(
        local,
        mesh=mesh,
        in_specs=(
            P(("dp", "mp"), None),
            P(("dp", "mp"), None),
            P("dp"),
            P(("dp", "mp"), None),
            P(),
            P(),
            P(),
            P(),
            P(None, "mp"),
            P(None, "mp"),
            P(None, "mp"),
            P("mp", None),
            P(),
            P(),
            P(None, "mp"),
            P(None, "mp"),
            P(None, "mp"),
            P("mp", None),
            P(),
            P(),
            P(None, "mp"),
            P("mp"),
            P("mp", None),
            P(),
        ),
        out_specs=(
            P(("dp", "mp"), None),
            P(("dp", "mp"), None),
            P(("dp", "mp"), None),
            P(),
            P(),
            P(),
            P(),
            P(None, "mp"),
            P(None, "mp"),
            P(None, "mp"),
            P("mp", None),
            P(),
            P(),
            P(None, "mp"),
            P(None, "mp"),
            P(None, "mp"),
            P("mp", None),
            P(),
            P(),
            P(None, "mp"),
            P("mp"),
            P("mp", None),
            P(),
        ),
        check_vma=False,
    )
```
